32 devices in a mesh: seq: 8 (over z, x), head: 4 (over y, core).
Axes of the slice: x: 2, y: 2, z: 4, core: 2. Of those that a mesh axis runs over, the one named last changes fastest.
Arguments:
- layer_input: bfloat16 [4096, 2048], P('seq', 'head'), may hold values from -6 to 6
- clip_lengths: int32 [3], replicated, may hold values from 1 to 4094, as said below
- key_padding: int32 [4096], replicated, may hold values 0 or 1
- norm1_gain: float32 [2048], replicated, may hold values from 0.1 to 1.9
- w_query: bfloat16 [2048, 2048], P(None, 'head'), may hold values from -0.125 to 0.125
- w_key: bfloat16 [2048, 2048], P(None, 'head'), may hold values from -0.125 to 0.125
- w_value: bfloat16 [2048, 2048], P(None, 'head'), may hold values from -0.125 to 0.125
- w_out: bfloat16 [2048, 2048], P(None, 'head'), may hold values from -1 to 1
- norm2_gain: float32 [2048], replicated, may hold values from 0.1 to 1.9
- w_up: bfloat16 [2048, 8192], P('seq', 'head'), may hold values from -0.125 to 0.125
- w_down: bfloat16 [2048, 8192], P('seq', 'head'), may hold values from -0.0625 to 0.0625
- out_grad: bfloat16 [4096, 2048], P('seq', 'head'), may hold values from -6 to 6
Outputs:
- layer_output: bfloat16 [4096, 2048], P('seq', 'head')
- input_grad: float32 [4096, 2048], P('seq', 'head')
- norm1_gain_grad: float32 [2048], replicated
- query_grad: float32 [2048, 2048], P(None, 'head')
- key_grad: float32 [2048, 2048], P(None, 'head')
- value_grad: float32 [2048, 2048], P(None, 'head')
- out_weight_grad: float32 [2048, 2048], P(None, 'head')
- norm2_gain_grad: float32 [2048], replicated
- up_grad: float32 [2048, 8192], P('seq', 'head')
- down_grad: float32 [2048, 8192], P('seq', 'head')
The draws below stay inside these ranges and needn't reach their ends.
Inputs may be any that keep to these rules, and one draw needn't show every extreme that they name: `clip_lengths`: the 3 lengths sum to 4096; the longest clip begins within the first 512 positions and ends within the last 512.
All inputs are finite; a program needn't handle non-finite values.
Results may differ from the reference program's by a relative error of at most 0.025.
Values may be sent and summed in bfloat16 or wider, within the bound.
A program may use at most 384 MiB of HBM per device.

```python
import math
import jax
import jax.numpy as jnp
from jax import lax

D = 2048
HD = 128
FF = 8192
TOK_DEV = 512
CLIPS = 3
TOKENS = 4096


def draw_clip_lengths(key, part):
    key = jax.random.fold_in(key, 17)
    short_key, place_key = jax.random.split(key)
    shorts = jax.random.randint(short_key, (CLIPS - 1,), 1, TOK_DEV // (CLIPS - 1))
    longest = TOKENS - jnp.sum(shorts)
    long_place = jax.random.randint(place_key, (), 0, CLIPS)
    clip_order = jnp.arange(CLIPS)
    short_index = jnp.clip(clip_order - (clip_order > long_place).astype(jnp.int32), 0, CLIPS - 2)
    return jnp.where(clip_order == long_place, longest, shorts[short_index]).astype(jnp.int32)


def plant(values, stream_key, low, largest):
    shape = values.shape
    spot = [jax.random.randint(jax.random.fold_in(stream_key, axis), (), 0, shape[axis]) for axis in range(len(shape))]
    values = values.at[tuple(spot)].set(low)
    longest = shape.index(max(shape))
    spot[longest] = (spot[longest] + 1) % shape[longest]
    return values.at[tuple(spot)].set(largest)


def levels(rng, shape, cuts, low, largest):
    def one(position, parts):
        heights = jax.random.uniform(jax.random.fold_in(jax.random.fold_in(rng, 6), position), (parts,), jnp.float32, low / len(cuts), largest / len(cuts))
        return jnp.repeat(jnp.exp(heights), shape[position] // parts).reshape((-1,) + (1,) * (len(shape) - position - 1))

    loudness = one(*cuts[0])
    for cut in cuts[1:]:
        loudness = loudness * one(*cut)
    return loudness


def gaussian(rng, extent, scale, bound, pieces=(), held_as=jnp.bfloat16):
    values = scale * jax.random.normal(rng, extent, jnp.float32)
    if pieces:
        values = values * levels(rng, extent, pieces, -0.22, 0.18)
    return jnp.clip(values, -bound, bound).astype(held_as)


def setup_inputs(seed: int = 0) -> dict:
    key_of = jax.random.split(jax.random.key(seed), 13)
    return {
        "layer_input": gaussian(key_of[0], (TOKENS, D), 1.0, 6.0, ((0, 8), (1, 4))),
        "clip_lengths": draw_clip_lengths(jax.random.fold_in(key_of[12], 71), 0),
        "key_padding": plant((jax.random.randint(key_of[2], (TOKENS,), 0, 4) < 3).astype(jnp.int32), jax.random.fold_in(key_of[2], 1), 0, 1),
        "norm1_gain": jnp.clip(1.0 + 0.18 * jax.random.normal(key_of[3], (D,), jnp.float32), 0.1, 1.9),
        "w_query": gaussian(key_of[4], (D, D), D ** -0.5, 0.125, ((1, 4),)),
        "w_key": gaussian(key_of[5], (D, D), D ** -0.5, 0.125, ((1, 4),)),
        "w_value": gaussian(key_of[6], (D, D), D ** -0.5, 0.125, ((1, 4),)),
        "w_out": gaussian(key_of[7], (D, D), (D // 64) ** -0.5, 1.0, ((1, 4),)),
        "norm2_gain": jnp.clip(1.0 + 0.18 * jax.random.normal(key_of[8], (D,), jnp.float32), 0.1, 1.9),
        "w_up": gaussian(key_of[9], (D, FF), D ** -0.5, 0.125, ((0, 8), (1, 4))),
        "w_down": gaussian(key_of[10], (D, FF), FF ** -0.5, 0.0625, ((0, 8), (1, 4))),
        "out_grad": gaussian(key_of[11], (TOKENS, D), 1.0, 6.0, ((0, 8), (1, 4))),
    }


norm_eps = 1e-05

@jax.custom_vjp
def low(v):
    return lax.optimization_barrier(v.astype(jnp.bfloat16)).astype(jnp.float32)

@jax.custom_vjp
def low_back(v):
    return v

def low_keep(v):
    return (low(v), None)

def low_pass(kept, grad):
    return (grad,)

def back_keep(v):
    return (v, None)

def back_low(kept, grad):
    return (low(grad),)
low.defvjp(low_keep, low_pass)
low_back.defvjp(back_keep, back_low)

def hdot(left, right):
    return jnp.dot(left, right, precision=lax.Precision.HIGHEST, preferred_element_type=jnp.float32)

def layer_norm(tok_rows, gain_vector):
    row_mean = lax.optimization_barrier(jnp.mean(tok_rows, axis=1, keepdims=True))
    centred = tok_rows - row_mean
    inverse = lax.rsqrt(lax.optimization_barrier(jnp.mean(centred * centred, axis=1, keepdims=True)) + norm_eps)
    return centred * inverse * gain_vector

def reference(layer_input, clip_lengths, key_padding, norm1_gain, w_query, w_key, w_value, w_out, norm2_gain, w_up, w_down, out_grad):
    head_count = D // HD
    positions = jnp.arange(TOKENS, dtype=jnp.int32)
    clip_ends = jnp.cumsum(clip_lengths).astype(jnp.int32)
    clip_ids = lax.optimization_barrier(jnp.sum((positions[:, None] >= clip_ends[None, :]).astype(jnp.int32), axis=1))
    key_keep = key_padding > 0
    block_rows = math.gcd(TOKENS, 512)
    block_count = TOKENS // block_rows
    score_scale = HD ** (-0.5)

    def forward(whole_input, gain_one, query_weight, key_weight, value_weight, out_weight, gain_two, up_weight, down_weight):
        attn_in = low(layer_norm(whole_input, gain_one))
        query_heads = low(low_back(hdot(attn_in, query_weight))).reshape(TOKENS, head_count, HD)
        key_heads = low(low_back(hdot(attn_in, key_weight))).reshape(TOKENS, head_count, HD)
        value_heads = low(low_back(hdot(attn_in, value_weight))).reshape(TOKENS, head_count, HD)

        def attend(block_args):
            query_block, pos_block, clip_block = block_args
            raw_scores = jnp.einsum('qhd,khd->hqk', query_block, key_heads, precision=lax.Precision.HIGHEST)
            scores = low_back(raw_scores) * score_scale
            allowed = (clip_block[:, None] == clip_ids[None, :]) & (positions[None, :] <= pos_block[:, None]) & (key_keep[None, :] | (positions[None, :] == pos_block[:, None]))
            scores = jnp.where(allowed[None], scores, -1e+30)
            row_high = lax.optimization_barrier(jnp.max(scores, axis=2, keepdims=True))
            exp_scores = jnp.where(allowed[None], jnp.exp(scores - row_high), 0.0)
            probabilities = exp_scores / lax.optimization_barrier(jnp.sum(exp_scores, axis=2, keepdims=True))
            return jnp.einsum('hqk,khd->qhd', low(probabilities), value_heads, precision=lax.Precision.HIGHEST)
        attended = lax.map(jax.checkpoint(attend), (query_heads.reshape(block_count, block_rows, head_count, HD), positions.reshape(block_count, block_rows), clip_ids.reshape(block_count, block_rows)))
        attended = low(low_back(attended.reshape(TOKENS, D)))
        resid = whole_input + low_back(hdot(attended, out_weight.T))
        mlp_in = low(layer_norm(resid, gain_two))
        up_proj = low_back(hdot(mlp_in, up_weight))
        activated = low(jax.nn.gelu(up_proj))
        return resid + low_back(hdot(activated, down_weight.T))
    layer_output, pullback = jax.vjp(forward, layer_input.astype(jnp.float32), norm1_gain, w_query.astype(jnp.float32), w_key.astype(jnp.float32), w_value.astype(jnp.float32), w_out.astype(jnp.float32), norm2_gain, w_up.astype(jnp.float32), w_down.astype(jnp.float32))
    all_grads = pullback(out_grad.astype(jnp.float32))
    return (layer_output.astype(jnp.bfloat16), all_grads[0], all_grads[1], all_grads[2], all_grads[3], all_grads[4], all_grads[5], all_grads[6], all_grads[7], all_grads[8])
```

```python
import jax
import jax.numpy as jnp
from jax import lax
from jax.sharding import Mesh, PartitionSpec as P

HD = 128
NORM_EPS = 1e-05
BF16 = jnp.bfloat16
F32 = jnp.float32
LAYER = ("x", "y", "core")


def shifted(block, axis, step, first, last):
    return lax.ppermute(block, axis, [(i, i + step) for i in range(first, last + 1)])


def swapped(block, axis):
    return lax.ppermute(block, axis, [(0, 1), (1, 0)])


def line_gather_up(block, count):
    found, moving = [], block
    for hop in range(1, count):
        moving = shifted(moving, "z", 1, hop - 1, count - 2)
        found.append(moving)
    return found


def line_gather_down(block, count):
    found, moving = [], block
    for hop in range(1, count):
        moving = shifted(moving, "z", -1, 1, count - hop)
        found.append(moving)
    return found


def line_whole(block, count, z):
    up = line_gather_up(block, count)
    down = line_gather_down(block, count)
    rows = block.shape[0]
    both = jnp.concatenate(up[::-1] + [block] + down, axis=0)
    return lax.dynamic_slice_in_dim(both, (count - 1 - z) * rows, count * rows, 0)


def line_reduce(partial, count, z):
    rows = partial.shape[0] // count

    def chunk(index):
        index = jnp.clip(index, 0, count - 1)
        return lax.dynamic_slice_in_dim(partial, index * rows, rows, 0)

    up = down = None
    for hop in range(1, count):
        own = chunk(count - hop + z)
        send = own if up is None else (own.astype(F32) + up.astype(F32)).astype(BF16)
        up = shifted(send, "z", 1, 0, min(hop - 1, count - 2))
        own = chunk(z - count + hop)
        send = own if down is None else (own.astype(F32) + down.astype(F32)).astype(BF16)
        down = shifted(send, "z", -1, max(count - hop, 1), count - 1)
    total = chunk(z).astype(F32)
    if up is not None:
        total = total + up.astype(F32) + down.astype(F32)
    return total


def layer_gather(share):
    wide = lax.all_gather(share, ("y", "core"), axis=1, tiled=True)
    return lax.all_gather(wide, "x", axis=0, tiled=True)


def layer_reduce(partial):
    tall = lax.psum_scatter(partial, "x", scatter_dimension=0, tiled=True)
    return lax.psum_scatter(tall, ("y", "core"), scatter_dimension=1, tiled=True)


def body(
    layer_input,
    clip_lengths,
    key_padding,
    norm1_gain,
    w_query,
    w_key,
    w_value,
    w_out,
    norm2_gain,
    w_up,
    w_down,
    out_grad,
):
    count = lax.axis_size("z")
    z, x = lax.axis_index("z"), lax.axis_index("x")
    column = lax.axis_index("y") * lax.axis_size("core") + lax.axis_index("core")
    share_rows, share_width = layer_input.shape
    rows = 2 * share_rows
    width = w_query.shape[0]
    local = w_query.shape[1] // 2
    heads = local // HD
    hidden = w_up.shape[1] // 2
    scale = HD ** (-0.5)
    gain1_share = lax.dynamic_slice_in_dim(norm1_gain, column * share_width, share_width)
    gain2_share = lax.dynamic_slice_in_dim(norm2_gain, column * share_width, share_width)

    def half(weight, which):
        size = weight.shape[1] // 2
        return lax.dynamic_slice_in_dim(weight, which * size, size, 1)

    def layer_rows(weight):
        other = swapped(half(weight, 1 - x), "x")
        own = half(weight, x)
        return jnp.where(
            x == 0, jnp.concatenate([own, other], 0), jnp.concatenate([other, own], 0)
        )

    down_full = line_whole(layer_rows(w_down), count, z)
    up_full = line_whole(layer_rows(w_up), count, z)

    whole_input = layer_gather(layer_input)
    grad_out = layer_gather(out_grad)

    wide = whole_input.astype(F32)
    mean1 = jnp.mean(wide, axis=1, keepdims=True)
    centred = wide - mean1
    inverse1 = lax.rsqrt(jnp.mean(centred * centred, axis=1, keepdims=True) + NORM_EPS)
    attn_in = (centred * inverse1 * norm1_gain).astype(BF16)

    query_w, key_w, value_w, out_w = (half(w, x) for w in (w_query, w_key, w_value, w_out))
    query = jnp.dot(attn_in, query_w, preferred_element_type=F32).astype(BF16)
    key = jnp.dot(attn_in, key_w, preferred_element_type=F32).astype(BF16)
    value = jnp.dot(attn_in, value_w, preferred_element_type=F32).astype(BF16)
    own_kv = jnp.concatenate([key, value], axis=1)
    below = line_gather_up(own_kv, count)

    clip_ends = jnp.cumsum(clip_lengths)

    def clip_of(positions):
        return jnp.sum((positions[:, None] >= clip_ends[None, :]).astype(jnp.int32), axis=1)

    query_pos = z * rows + jnp.arange(rows, dtype=jnp.int32)
    query_clip = clip_of(query_pos)

    def visible(first_key, key_rows):
        key_pos = first_key + jnp.arange(key_rows, dtype=jnp.int32)
        keep = key_padding[jnp.clip(key_pos, 0, key_padding.shape[0] - 1)] > 0
        same = (query_clip[:, None] == clip_of(key_pos)[None, :]) & (key_pos >= 0)[None, :]
        causal = key_pos[None, :] <= query_pos[:, None]
        return same & causal & (keep[None, :] | (key_pos[None, :] == query_pos[:, None]))

    def split(block):
        return block.reshape(block.shape[0], heads, HD)

    query_heads = split(query)
    all_kv = jnp.concatenate(below[::-1] + [own_kv], axis=0)
    allowed = visible((z - count + 1) * rows, count * rows)
    scores = (
        jnp.einsum("qhd,khd->hqk", query_heads, split(all_kv[:, :local]), preferred_element_type=F32)
        * scale
    )
    scores = jnp.where(allowed[None], scores, -1e30)
    high = jnp.max(scores, axis=2, keepdims=True)
    weights = jnp.where(allowed[None], jnp.exp(scores - high), 0.0)
    total = jnp.sum(weights, axis=2, keepdims=True)
    attn_heads = (
        jnp.einsum(
            "hqk,khd->hqd", weights.astype(BF16), split(all_kv[:, local:]), preferred_element_type=F32
        )
        / total
    )
    log_sum = high + jnp.log(total)
    attended = jnp.transpose(attn_heads, (1, 0, 2)).reshape(rows, local).astype(BF16)
    attn_part = jnp.einsum("tf,df->td", attended, out_w, preferred_element_type=F32).astype(BF16)
    resid = layer_input.astype(F32) + layer_reduce(attn_part).astype(F32)

    mean_own = jnp.mean(resid, axis=1, keepdims=True)
    spread_own = jnp.sum((resid - mean_own) ** 2, axis=1, keepdims=True)
    parts = lax.all_gather(
        jnp.concatenate([mean_own, spread_own], axis=1), ("y", "core"), axis=0, tiled=False
    )
    mean2 = jnp.mean(parts[:, :, 0], axis=0)[:, None]
    var2 = (
        jnp.sum(parts[:, :, 1], axis=0)[:, None]
        + share_width * jnp.sum((parts[:, :, 0] - mean2[:, 0]) ** 2, axis=0)[:, None]
    ) / width
    inverse2 = lax.rsqrt(var2 + NORM_EPS)
    normed2 = (resid - mean2) * inverse2
    mlp_in = layer_gather((normed2 * gain2_share).astype(BF16))

    grad_act = jnp.dot(grad_out, down_full, preferred_element_type=F32)
    up_f = jnp.dot(mlp_in, up_full, preferred_element_type=F32)
    gelu_value, gelu_back = jax.vjp(jax.nn.gelu, up_f)
    activated = gelu_value.astype(BF16)
    grad_up = gelu_back(grad_act)[0].astype(BF16)
    grad_mlp_part = jnp.einsum("tf,df->td", grad_up, up_full, preferred_element_type=F32)
    grad_mlp = layer_reduce(grad_mlp_part.astype(BF16)).astype(F32)
    down_part = jnp.einsum("tf,df->td", activated, down_full, preferred_element_type=F32)
    layer_output = (resid + layer_reduce(down_part.astype(BF16)).astype(F32)).astype(BF16)

    down_term = jnp.einsum("tc,tf->cf", grad_out, activated, preferred_element_type=F32)
    up_term = jnp.einsum("tc,tf->cf", mlp_in, grad_up, preferred_element_type=F32)

    def weight_home(term):
        mine = line_reduce(term.astype(BF16), count, z).astype(BF16)
        size = mine.shape[0] // 2
        other = swapped(lax.dynamic_slice_in_dim(mine, (1 - x) * size, size, 0), "x")
        own = lax.dynamic_slice_in_dim(mine, x * size, size, 0)
        return jnp.where(
            x == 0, jnp.concatenate([own, other], 1), jnp.concatenate([other, own], 1)
        ).astype(F32)

    down_grad = weight_home(down_term)
    up_grad = weight_home(up_term)

    def norm_back(grad, normed, inverse, gain_share):
        scaled = grad * gain_share
        sums = lax.psum(
            jnp.stack([jnp.sum(scaled, axis=1), jnp.sum(scaled * normed, axis=1)], axis=1),
            ("y", "core"),
        )
        centre, slope = sums[:, :1] / width, sums[:, 1:] / width
        return inverse * (scaled - centre - normed * slope), jnp.sum(grad * normed, axis=0)

    back2, gain2_part = norm_back(grad_mlp, normed2, inverse2, gain2_share)
    grad_resid = out_grad.astype(F32) + back2
    grad_branch = layer_gather(grad_resid.astype(BF16))
    out_weight_part = jnp.einsum("td,tf->df", grad_branch, attended, preferred_element_type=F32)
    grad_attended = jnp.dot(grad_branch, out_w, preferred_element_type=F32).astype(BF16)
    grad_heads = split(grad_attended)
    delta = jnp.einsum("thd,htd->ht", grad_heads.astype(F32), attn_heads)

    def stage(kv, distance):
        keys, values = split(kv[:, :local]), split(kv[:, local:])
        allowed = visible((z - distance) * rows, rows)
        scores = jnp.einsum("qhd,khd->hqk", query_heads, keys, preferred_element_type=F32) * scale
        probs = jnp.where(allowed[None], jnp.exp(scores - log_sum), 0.0)
        grad_probs = jnp.einsum("qhd,khd->hqk", grad_heads, values, preferred_element_type=F32)
        grad_scores = (probs * (grad_probs - delta[:, :, None]) * scale).astype(BF16)
        grad_query = jnp.einsum("hqk,khd->qhd", grad_scores, keys, preferred_element_type=F32)
        grad_key = jnp.einsum("hqk,qhd->khd", grad_scores, query_heads, preferred_element_type=F32)
        grad_value = jnp.einsum(
            "hqk,qhd->khd", probs.astype(BF16), grad_heads, preferred_element_type=F32
        )
        return grad_query.reshape(rows, local), jnp.concatenate(
            [grad_key.reshape(rows, local), grad_value.reshape(rows, local)], axis=1
        )

    grad_query, moving = jnp.zeros((rows, local), F32), None
    for hop in range(1, count):
        more, grad_kv = stage(below[count - hop - 1], count - hop)
        grad_query = grad_query + more
        if moving is not None:
            grad_kv = grad_kv + moving.astype(F32)
        moving = shifted(grad_kv.astype(BF16), "z", -1, max(count - hop, 1), count - 1)
    more, grad_kv = stage(own_kv, 0)
    grad_query = (grad_query + more).astype(BF16)
    if moving is not None:
        grad_kv = grad_kv + moving.astype(F32)
    grad_kv = grad_kv.astype(BF16)
    grads = jnp.concatenate([grad_query, grad_kv], axis=1)

    qkv_w = jnp.concatenate([query_w, key_w, value_w], axis=1)
    grad_attn_part = jnp.einsum("tf,df->td", grads, qkv_w, preferred_element_type=F32)
    grad_attn = layer_reduce(grad_attn_part.astype(BF16)).astype(F32)
    qkv_part = jnp.einsum("td,tf->df", attn_in, grads, preferred_element_type=F32)

    def weight_everywhere(partial):
        mine = line_reduce(partial.astype(BF16), count, z).astype(BF16)
        return line_whole(mine, count, z)

    def both_halves(block):
        other = swapped(block, "x")
        return jnp.where(
            x == 0, jnp.concatenate([block, other], 1), jnp.concatenate([other, block], 1)
        ).astype(F32)

    out_weight_grad = both_halves(weight_everywhere(out_weight_part))
    qkv_grad = weight_everywhere(qkv_part)
    query_grad = both_halves(qkv_grad[:, :local])
    key_grad = both_halves(qkv_grad[:, local : 2 * local])
    value_grad = both_halves(qkv_grad[:, 2 * local :])

    def share_of(stat):
        return lax.dynamic_slice_in_dim(stat, x * share_rows, share_rows, 0)

    mean1_share, inverse1_share = share_of(mean1), share_of(inverse1)
    normed1 = (layer_input.astype(F32) - mean1_share) * inverse1_share
    back1, gain1_part = norm_back(grad_attn, normed1, inverse1_share, gain1_share)
    input_grad = grad_resid + back1

    gains = lax.psum(jnp.stack([gain1_part, gain2_part]), ("z", "x"))
    gains = lax.all_gather(gains, ("y", "core"), axis=1, tiled=True)
    return (
        layer_output,
        input_grad,
        gains[0],
        query_grad,
        key_grad,
        value_grad,
        out_weight_grad,
        gains[1],
        up_grad,
        down_grad,
    )


def solution(mesh):
    seq, head = mesh.shape["seq"], mesh.shape["head"]
    fine = Mesh(mesh.devices.reshape(seq // 2, 2, head // 2, 2), ("z", "x", "y", "core"))
    seq_axes, head_axes = ("z", "x"), ("y", "core")
    both, columns = P(seq_axes, head_axes), P(None, head_axes)
    return jax.shard_map(
        body,
        mesh=fine,
        in_specs=(both, P(), P(), P(), columns, columns, columns, columns, P(), both, both, both),
        out_specs=(both, both, P(), columns, columns, columns, columns, P(), both, both),
        check_vma=False,
    )
```

```python
import functools

import jax
import jax.numpy as jnp
from jax import lax
from jax.experimental import pallas as pl
from jax.experimental.pallas import tpu as pltpu
from jax.sharding import Mesh, PartitionSpec as P

HD = 128
NORM_EPS = 1e-05
BF16 = jnp.bfloat16
F32 = jnp.float32
LAYER = ("x", "y", "core")


MESH = pl.DeviceIdType.MESH
LOG2E = 1.4426950408889634


def remote(src, dst, sends, recvs, slot, **device):
    return pltpu.make_async_remote_copy(
        src_ref=src,
        dst_ref=dst,
        send_sem=sends.at[slot],
        recv_sem=recvs.at[slot],
        device_id=device,
        device_id_type=MESH,
    )


def contract(left, right, dims):
    return lax.dot_general(left, right, (dims, ((), ())), preferred_element_type=F32)


class Place:
    def __init__(self, count):
        self.count = count
        self.z = lax.axis_index("z")
        self.x, self.y, self.c = lax.axis_index("x"), lax.axis_index("y"), lax.axis_index("core")
        self.ox, self.oy, self.oc = 1 - self.x, 1 - self.y, 1 - self.c

    def meet(self):
        barrier = pltpu.get_barrier_semaphore()
        for device in ({"x": self.ox}, {"y": self.oy}, {"core": self.oc}):
            pl.semaphore_signal(barrier, inc=1, device_id=device, device_id_type=MESH)
        above, below = self.z < self.count - 1, self.z > 0
        for there, step in ((above, 1), (below, -1)):

            @pl.when(there)
            def _():
                pl.semaphore_signal(
                    barrier, inc=1, device_id={"z": self.z + step}, device_id_type=MESH
                )

        pl.semaphore_wait(barrier, 3 + above.astype(jnp.int32) + below.astype(jnp.int32))


class Gather:
    def __init__(self, at, array, rows, width, sends, recvs, lead=()):
        self.at, self.array, self.sends, self.recvs, self.lead = at, array, sends, recvs, lead
        self.rows, self.width = rows, width

    def block(self, xi, yi, ci, first=0, size=None):
        size = self.rows if size is None else size
        return self.array.at[
            pl.ds(pl.multiple_of(xi * self.rows + first, size), size),
            pl.ds(pl.multiple_of((2 * yi + ci) * self.width, self.width), self.width),
        ]

    def copy(self, k, landing=False):
        at, half = self.at, self.rows // 2
        x, y, c, ox, oy, oc = at.x, at.y, at.c, at.ox, at.oy, at.oc
        place = {
            0: ((x, y, c), (ox, y, c), {"x": ox}),
            1: ((x, y, c), (x, oy, c), {"y": oy}),
            2: ((x, y, c), (x, y, oc), {"core": oc}),
            3: ((ox, y, c, 0, half), (ox, oy, c, 0, half), {"y": oy}),
            4: ((x, oy, c, half, half), (ox, oy, c, half, half), {"x": ox}),
            5: ((ox, y, c), (ox, y, oc), {"core": oc}),
            6: ((x, oy, c), (x, oy, oc), {"core": oc}),
            7: ((ox, oy, c, 0, half), (ox, oy, oc, 0, half), {"core": oc}),
            8: ((ox, oy, c, half, half), (ox, oy, oc, half, half), {"core": oc}),
        }
        source, lands, device = place[k]
        ref = self.block(*(lands if landing else source))
        return remote(ref, ref, self.sends, self.recvs, self.lead + (k,), **device)

    def start(self):
        for k in (0, 1, 2):
            self.copy(k).start()

    def middle(self):
        self.copy(0, True).wait_recv()
        self.copy(3).start()
        self.copy(5).start()
        self.copy(1, True).wait_recv()
        self.copy(4).start()
        self.copy(6).start()

    def corner(self):
        self.copy(3, True).wait_recv()
        self.copy(7).start()
        self.copy(4, True).wait_recv()
        self.copy(8).start()

    def end(self):
        for k in (2, 5, 6, 7, 8):
            self.copy(k, True).wait_recv()

    def drain(self):
        for k in range(9):
            self.copy(k).wait_send()


class Reduce:
    def __init__(self, at, array, rows, width, buffers, sends, recvs):
        self.at, self.array, self.sends, self.recvs = at, array, sends, recvs
        self.rows, self.width = rows, width
        self.twin, self.corner_x, self.corner_y, self.from_x, self.from_y = buffers

    def block(self, xi, yi, ci, first=0, size=None):
        return Gather.block(self, xi, yi, ci, first, size)

    def copy(self, k):
        at, half = self.at, self.rows // 2
        x, y, c, ox, oy, oc = at.x, at.y, at.c, at.ox, at.oy, at.oc
        low, high = pl.ds(0, half), pl.ds(half, half)
        place = {
            0: ((ox, oy, oc), self.twin.at[0], {"core": oc}),
            1: ((ox, y, oc), self.twin.at[1], {"core": oc}),
            2: ((x, oy, oc), self.twin.at[2], {"core": oc}),
            3: ((x, y, oc), self.twin.at[3], {"core": oc}),
            4: ((ox, oy, c, 0, half), self.corner_y, {"y": oy}),
            5: ((ox, oy, c, half, half), self.corner_x, {"x": ox}),
            6: ((ox, y, c, half, half), self.from_x.at[high], {"x": ox}),
            7: ((x, oy, c, 0, half), self.from_y.at[low], {"y": oy}),
            8: ((ox, y, c, 0, half), self.from_x.at[low], {"x": ox}),
            9: ((x, oy, c, half, half), self.from_y.at[high], {"y": oy}),
        }
        source, lands, device = place[k]
        return remote(self.block(*source), lands, self.sends, self.recvs, (k,), **device)

    def add(self, target, other):
        rows = target.shape[0]
        tile = min(rows, 128)

        @pl.loop(0, rows // tile)
        def _(i):
            part = pl.ds(pl.multiple_of(i * tile, tile), tile)
            target[part, :] = (target[part, :].astype(F32) + other[part, :].astype(F32)).astype(
                target.dtype
            )

    def start(self):
        for k in (0, 1, 2, 3):
            self.copy(k).start()

    def twins(self):
        at, half = self.at, self.rows // 2
        x, y, c, ox, oy = at.x, at.y, at.c, at.ox, at.oy
        self.copy(0).wait_recv()
        self.add(self.block(ox, oy, c), self.twin.at[0])
        self.copy(4).start()
        self.copy(5).start()
        self.copy(1).wait_recv()
        self.add(self.block(ox, y, c), self.twin.at[1])
        self.copy(6).start()
        self.copy(2).wait_recv()
        self.add(self.block(x, oy, c), self.twin.at[2])
        self.copy(7).start()
        self.copy(3).wait_recv()

    def corners(self):
        at, half = self.at, self.rows // 2
        self.copy(4).wait_recv()
        self.add(self.block(at.ox, at.y, at.c, 0, half), self.corner_y)
        self.copy(8).start()
        self.copy(5).wait_recv()
        self.add(self.block(at.x, at.oy, at.c, half, half), self.corner_x)
        self.copy(9).start()

    def end(self, store):
        for k in (6, 7, 8, 9):
            self.copy(k).wait_recv()
        own = self.block(self.at.x, self.at.y, self.at.c)
        tile = min(self.rows, 128)

        @pl.loop(0, self.rows // tile)
        def _(i):
            part = pl.ds(pl.multiple_of(i * tile, tile), tile)
            store(
                part,
                own[part, :].astype(F32)
                + self.twin[3, part, :].astype(F32)
                + self.from_x[part, :].astype(F32)
                + self.from_y[part, :].astype(F32),
            )

    def drain(self):
        for k in range(10):
            self.copy(k).wait_send()


def reduce_scratch(rows, width):
    return [
        pltpu.VMEM((4, rows, width), BF16),
        pltpu.VMEM((rows // 2, width), BF16),
        pltpu.VMEM((rows // 2, width), BF16),
        pltpu.VMEM((rows, width), BF16),
        pltpu.VMEM((rows, width), BF16),
    ]


def normed_rows(rows):
    mean = jnp.mean(rows, axis=1, keepdims=True)
    centred = rows - mean
    inverse = lax.rsqrt(jnp.mean(centred * centred, axis=1, keepdims=True) + NORM_EPS)
    return centred * inverse, inverse


class Weights:
    def __init__(self, at, which, weight, whole, sems):
        self.at, self.which, self.weight, self.whole = at, which, weight, whole
        self.local, self.xs, self.xr, self.us, self.ds, self.rs = sems
        self.half = weight.shape[1] // 2

    def columns(self, which):
        return self.weight.at[:, pl.ds(pl.multiple_of(which * self.half, self.half), self.half)]

    def own(self):
        at = self.at
        return pltpu.make_async_copy(
            self.columns(at.x), self.whole.at[at.z, at.x], self.local.at[self.which]
        )

    def swap(self, landing=False):
        at = self.at
        dst = self.whole.at[at.z, at.ox] if landing else self.whole.at[at.z, at.x]
        return remote(self.columns(at.ox), dst, self.xs, self.xr, (self.which,), x=at.ox)

    def move(self, layer, part, step):
        ref = self.whole.at[layer, part]
        sends = self.us if step > 0 else self.ds
        return pltpu.make_async_remote_copy(
            src_ref=ref,
            dst_ref=ref,
            send_sem=sends.at[self.which, layer, part],
            recv_sem=self.rs.at[self.which, layer, part],
            device_id={"z": self.at.z + step},
            device_id_type=MESH,
        )

    def first(self, mine):
        at = self.at
        part = at.x if mine else at.ox
        if mine:
            self.own().wait()
        else:
            self.swap(True).wait_recv()

        @pl.when(at.z < at.count - 1)
        def _():
            self.move(at.z, part, 1).start()

        @pl.when(at.z > 0)
        def _():
            self.move(at.z, part, -1).start()

    def hop(self, distance, mine):
        at = self.at
        part = at.x if mine else at.ox

        @pl.when(at.z >= distance)
        def _():
            self.move(at.z - distance, part, 1).wait_recv()

            @pl.when(at.z < at.count - 1)
            def _():
                self.move(at.z - distance, part, 1).start()

        @pl.when(at.z + distance < at.count)
        def _():
            self.move(at.z + distance, part, -1).wait_recv()

            @pl.when(at.z > 0)
            def _():
                self.move(at.z + distance, part, -1).start()

    def drain(self):
        at = self.at
        self.swap().wait_send()
        for part in (0, 1):

            @pl.loop(0, at.count)
            def _(layer):
                @pl.when((layer <= at.z) & (at.z < at.count - 1))
                def _():
                    self.move(layer, part, 1).wait_send()

                @pl.when((layer >= at.z) & (at.z > 0))
                def _():
                    self.move(layer, part, -1).wait_send()


def front_kernel(
    count,
    xs,
    og,
    w_query,
    w_key,
    w_value,
    w_out,
    w_up,
    w_down,
    gain1,
    gain2,
    start_of,
    key_place,
    x_all,
    in_all,
    kv_all,
    query_out,
    attended_out,
    log_out,
    branch_out,
    mlp_out,
    og_all,
    down_all,
    up_all,
    qkv_w,
    out_w,
    query,
    kv,
    high,
    total,
    sums,
    attended,
    partial,
    branch,
    twin,
    corner_x,
    corner_y,
    from_x,
    from_y,
    load_sem,
    gather_send,
    gather_recv,
    line_send,
    line_recv,
    w_local,
    w_xs,
    w_xr,
    w_us,
    w_ds,
    w_rs,
    reduce_send,
    reduce_recv,
):
    at = Place(count)
    z, x, y, c = at.z, at.x, at.y, at.c
    rows, width = xs.shape
    group = 2 * rows
    local = w_query.shape[1] // 2
    heads = local // HD
    features = gain1.shape[1]
    tile = 256 if group % 256 == 0 else group
    tiles = group // tile

    def columns_of(weight):
        return weight.at[:, pl.ds(pl.multiple_of(x * local, local), local)]

    loads = [
        pltpu.make_async_copy(
            columns_of(w), qkv_w.at[:, pl.ds(i * local, local)], load_sem.at[i]
        )
        for i, w in enumerate((w_key, w_value, w_query))
    ]
    loads.append(pltpu.make_async_copy(columns_of(w_out), out_w, load_sem.at[3]))

    def gather_of(d):
        return Gather(at, x_all.at[d], rows, width, gather_send, gather_recv, (d,))

    og_gather = Gather(at, og_all, rows, width, gather_send, gather_recv, (count,))
    branch_gather = Gather(at, branch, rows, width, gather_send, gather_recv, (count + 1,))

    def own_block(d):
        return gather_of(d).block(x, y, c)

    def line_copy(d):
        return remote(own_block(d), own_block(d + 1), line_send, line_recv, (d,), z=z + 1)

    weight_sems = (w_local, w_xs, w_xr, w_us, w_ds, w_rs)
    down = Weights(at, 0, w_down, down_all, weight_sems)
    up = Weights(at, 1, w_up, up_all, weight_sems)

    own_x = pltpu.make_async_copy(xs, own_block(0), load_sem.at[4])
    own_og = pltpu.make_async_copy(og, og_gather.block(x, y, c), load_sem.at[5])
    own_x.start()
    down.own().start()
    up.own().start()
    own_og.start()
    for load in loads:
        load.start()
    at.meet()
    own_x.wait()

    @pl.when(z < count - 1)
    def _():
        line_copy(0).start()

    gather_of(0).start()
    down.first(True)
    gather_of(0).middle()
    down.swap().start()
    for load in loads:
        load.wait()

    def project(d, with_query):
        size = qkv_w.shape[1] if with_query else 2 * local

        def step(x_ref, in_ref, kv_ref, *maybe_query):
            normed, _ = normed_rows(x_ref[...].astype(F32))
            rounded = (normed * gain1[...]).astype(BF16)
            in_ref[...] = rounded
            product = jnp.dot(rounded, qkv_w[:, :size], preferred_element_type=F32)
            kv_ref[...] = product[:, : 2 * local].astype(BF16)
            if with_query:
                maybe_query[0][...] = product[:, 2 * local :].astype(BF16)

        def rows_of(size):
            return pl.BlockSpec((tile, size), lambda i: (i, 0))

        outs = [rows_of(features), rows_of(2 * local)] + ([rows_of(local)] if with_query else [])
        refs = [in_all.at[d], kv_all.at[d]] + ([query_out] if with_query else [])
        pltpu.emit_pipeline(step, grid=(tiles,), in_specs=[rows_of(features)], out_specs=outs)(
            x_all.at[d], *refs
        )

    def attend(d, diagonal):
        keys = key_place[z - d]

        @pl.loop(0, tiles)
        def _(i):
            part = pl.ds(pl.multiple_of(i * tile, tile), tile)
            allowed = keys >= start_of[part, :]
            if diagonal:
                query_at = lax.broadcasted_iota(jnp.int32, (tile, group), 0) + i * tile
                key_at = lax.broadcasted_iota(jnp.int32, (tile, group), 1)
                allowed = (allowed & (key_at <= query_at)) | (key_at == query_at)
            for h in range(heads):
                span = slice(h * HD, (h + 1) * HD)
                scores = contract(query[part, span], kv[:, span], ((1,), (1,)))
                scores = jnp.where(allowed, scores * (HD**-0.5 * LOG2E), -1e30)
                top = jnp.max(scores, axis=1, keepdims=True)
                if not diagonal:
                    old = high[h, part, :1]
                    top = jnp.maximum(old, top)
                    fade = jnp.exp2(old - top)
                weights = jnp.exp2(scores - top)
                mass = jnp.sum(weights, axis=1, keepdims=True)
                value = jnp.dot(
                    weights.astype(BF16),
                    kv[:, local + h * HD : local + (h + 1) * HD],
                    preferred_element_type=F32,
                )
                if not diagonal:
                    mass = mass + total[h, part, :1] * fade
                    value = value + sums[part, span] * fade
                high[h, part, :] = jnp.broadcast_to(top, (tile, HD))
                total[h, part, :] = jnp.broadcast_to(mass, (tile, HD))
                sums[part, span] = value

    def piece(d, diagonal):
        project(d, diagonal)
        pltpu.sync_copy(kv_all.at[d], kv)
        if diagonal:
            pltpu.sync_copy(query_out, query)
        attend(d, diagonal)

    halves = [(up, True), (down, False), (up, False)]

    def send_half(step):
        weight, mine = halves[step]
        weight.first(mine)
        if step == 0:
            up.swap().start()

    def bring(d):
        @pl.when(z >= d)
        def _():
            remote(own_block(d - 1), own_block(d), line_send, line_recv, (d - 1,), z=z).wait_recv()

            @pl.when((d < count - 1) & (z < count - 1))
            def _():
                line_copy(d).start()

            gather_of(d).start()

    def within(d, *names):
        @pl.when(z >= d)
        def _():
            for name in names:
                getattr(gather_of(d), name)()

    hops = [
        (weight, distance, mine)
        for distance in range(1, count)
        for weight, mine in ((down, True), (up, True), (down, False), (up, False))
    ]

    def hop(many=1):
        for _ in range(min(many, len(hops))):
            weight, distance, mine = hops.pop(0)
            weight.hop(distance, mine)

    gather_of(0).corner()
    gather_of(0).end()
    bring(1)
    send_half(0)
    piece(0, True)
    within(1, "middle")

    @pl.loop(2, count)
    def _(d):
        within(d - 1, "corner", "end")
        bring(d)
        for step in (1, 2):

            @pl.when(d == step + 1)
            def _():
                send_half(step)

        @pl.when(z >= d - 1)
        def _():
            piece(d - 1, False)

        within(d, "middle")

    for step in range(max(count - 1, 1), 3):
        send_half(step)
    hop(2)
    within(count - 1, "corner", "end")
    own_og.wait()
    og_gather.start()

    @pl.when(z >= count - 1)
    def _():
        piece(count - 1, False)

    hop()
    og_gather.middle()

    @pl.loop(0, tiles)
    def _(i):
        part = pl.ds(pl.multiple_of(i * tile, tile), tile)
        for h in range(heads):
            span = slice(h * HD, (h + 1) * HD)
            mass = total[h, part, :]
            attended[part, span] = (sums[part, span] / mass).astype(BF16)
            high[h, part, :] = high[h, part, :] + jnp.log2(mass)
        partial[part, :] = contract(attended[part, :], out_w[...], ((1,), (1,))).astype(BF16)

    outs = [
        pltpu.make_async_copy(attended, attended_out, load_sem.at[6]),
        pltpu.make_async_copy(high, log_out, load_sem.at[7]),
    ]
    for out in outs:
        out.start()
    hop()
    og_gather.corner()
    reduce = Reduce(
        at, partial, rows, width, (twin, corner_x, corner_y, from_x, from_y), reduce_send, reduce_recv
    )
    reduce.start()
    og_gather.end()
    reduce.twins()
    hop()
    reduce.corners()
    hop()
    own_branch = branch_gather.block(x, y, c)

    def store(part, value):
        own_branch[part, :] = value.astype(BF16)

    reduce.end(store)
    branch_gather.start()
    hop()
    branch_gather.middle()
    hop()
    branch_gather.corner()
    hop()
    branch_gather.end()
    pltpu.sync_copy(branch, branch_out)

    def second_norm(x_ref, branch_ref, mlp_ref):
        normed, _ = normed_rows(x_ref[...].astype(F32) + branch_ref[...].astype(F32))
        mlp_ref[...] = (normed * gain2[...]).astype(BF16)

    spec = pl.BlockSpec((tile, features), lambda i: (i, 0))
    pltpu.emit_pipeline(second_norm, grid=(tiles,), in_specs=[spec, spec], out_specs=[spec])(
        x_all.at[0], branch_out, mlp_out
    )
    hop(len(hops))

    for out in outs:
        out.wait()
    down.drain()
    up.drain()
    reduce.drain()
    branch_gather.drain()
    og_gather.drain()

    @pl.loop(0, count)
    def _(d):
        within(d, "drain")

        @pl.when((z >= d) & (d < count - 1) & (z < count - 1))
        def _():
            line_copy(d).wait_send()


def front(count, xs, og, w_query, w_key, w_value, w_out, w_up, w_down, gain1, gain2, start_of, key_place):
    rows, width = xs.shape
    group, features = 2 * rows, gain1.shape[1]
    local = w_query.shape[1] // 2
    heads = local // HD
    hidden = w_up.shape[1] // 2
    w_rows = w_up.shape[0]
    hbm, vmem = pl.BlockSpec(memory_space=pl.ANY), pl.BlockSpec(memory_space=pltpu.VMEM)

    def out(*shape, dtype=BF16):
        return jax.ShapeDtypeStruct(shape, dtype)

    dma = pltpu.SemaphoreType.DMA
    return pl.pallas_call(
        functools.partial(front_kernel, count),
        name="front",
        out_shape=(
            out(count, group, features),
            out(count, group, features),
            out(count, group, 2 * local),
            out(group, local),
            out(group, local),
            out(heads, group, HD, dtype=F32),
            out(group, features),
            out(group, features),
            out(group, features),
            out(count, 2, w_rows, hidden),
            out(count, 2, w_rows, hidden),
        ),
        in_specs=[hbm] * 8 + [vmem] * 4,
        out_specs=[hbm] * 11,
        scratch_shapes=[
            pltpu.VMEM((features, 3 * local), BF16),
            pltpu.VMEM((features, local), BF16),
            pltpu.VMEM((group, local), BF16),
            pltpu.VMEM((group, 2 * local), BF16),
            pltpu.VMEM((heads, group, HD), F32),
            pltpu.VMEM((heads, group, HD), F32),
            pltpu.VMEM((group, local), F32),
            pltpu.VMEM((group, local), BF16),
            pltpu.VMEM((group, features), BF16),
            pltpu.VMEM((group, features), BF16),
            *reduce_scratch(rows, width),
            dma((8,)),
            dma((count + 2, 9)),
            dma((count + 2, 9)),
            dma((count,)),
            dma((count,)),
            dma((2,)),
            dma((2,)),
            dma((2,)),
            dma((2, count, 2)),
            dma((2, count, 2)),
            dma((2, count, 2)),
            dma((10,)),
            dma((10,)),
        ],
        compiler_params=pltpu.CompilerParams(
            collective_id=0, has_side_effects=True, vmem_limit_bytes=56 * 1024 * 1024
        ),
    )(xs, og, w_query, w_key, w_value, w_out, w_up, w_down, gain1, gain2, start_of, key_place)


def shifted(block, axis, step, first, last):
    return lax.ppermute(block, axis, [(i, i + step) for i in range(first, last + 1)])


def swapped(block, axis):
    return lax.ppermute(block, axis, [(0, 1), (1, 0)])


def line_gather_up(block, count):
    found, moving = [], block
    for hop in range(1, count):
        moving = shifted(moving, "z", 1, hop - 1, count - 2)
        found.append(moving)
    return found


def line_gather_down(block, count):
    found, moving = [], block
    for hop in range(1, count):
        moving = shifted(moving, "z", -1, 1, count - hop)
        found.append(moving)
    return found


def line_whole(block, count, z):
    up = line_gather_up(block, count)
    down = line_gather_down(block, count)
    rows = block.shape[0]
    both = jnp.concatenate(up[::-1] + [block] + down, axis=0)
    return lax.dynamic_slice_in_dim(both, (count - 1 - z) * rows, count * rows, 0)


def line_reduce(partial, count, z):
    rows = partial.shape[0] // count

    def chunk(index):
        index = jnp.clip(index, 0, count - 1)
        return lax.dynamic_slice_in_dim(partial, index * rows, rows, 0)

    up = down = None
    for hop in range(1, count):
        own = chunk(count - hop + z)
        send = own if up is None else (own.astype(F32) + up.astype(F32)).astype(BF16)
        up = shifted(send, "z", 1, 0, min(hop - 1, count - 2))
        own = chunk(z - count + hop)
        send = own if down is None else (own.astype(F32) + down.astype(F32)).astype(BF16)
        down = shifted(send, "z", -1, max(count - hop, 1), count - 1)
    total = chunk(z).astype(F32)
    if up is not None:
        total = total + up.astype(F32) + down.astype(F32)
    return total


def layer_gather(share):
    wide = lax.all_gather(share, ("y", "core"), axis=1, tiled=True)
    return lax.all_gather(wide, "x", axis=0, tiled=True)


def layer_reduce(partial):
    tall = lax.psum_scatter(partial, "x", scatter_dimension=0, tiled=True)
    return lax.psum_scatter(tall, ("y", "core"), scatter_dimension=1, tiled=True)


def body(
    layer_input,
    clip_lengths,
    key_padding,
    norm1_gain,
    w_query,
    w_key,
    w_value,
    w_out,
    norm2_gain,
    w_up,
    w_down,
    out_grad,
):
    count = lax.axis_size("z")
    z, x = lax.axis_index("z"), lax.axis_index("x")
    column = lax.axis_index("y") * lax.axis_size("core") + lax.axis_index("core")
    share_rows, share_width = layer_input.shape
    rows = 2 * share_rows
    width = w_query.shape[0]
    local = w_query.shape[1] // 2
    heads = local // HD
    hidden = w_up.shape[1] // 2
    scale = HD ** (-0.5)
    gain1_share = lax.dynamic_slice_in_dim(norm1_gain, column * share_width, share_width)
    gain2_share = lax.dynamic_slice_in_dim(norm2_gain, column * share_width, share_width)

    def half(weight, which):
        size = weight.shape[1] // 2
        return lax.dynamic_slice_in_dim(weight, which * size, size, 1)

    clip_ends = jnp.cumsum(clip_lengths)
    position = jnp.arange(key_padding.shape[0], dtype=jnp.int32)
    starts = jnp.max(jnp.where(position[:, None] >= clip_ends, clip_ends, 0), axis=1)
    key_place = jnp.where(key_padding > 0, position, -1).reshape(count, 1, rows)
    start_of = lax.dynamic_slice_in_dim(starts, z * rows, rows)[:, None]
    (x_all, in_all, kv_all, query, attended, log_sum, branch, mlp_in, grad_out, down_full, up_full) = front(
        count, layer_input, out_grad, w_query, w_key, w_value, w_out, w_up, w_down,
        norm1_gain[None], norm2_gain[None], start_of, key_place,
    )
    down_full = down_full.reshape(width, hidden)
    up_full = up_full.reshape(width, hidden)
    attn_in = in_all[0]
    below = [kv_all[d] for d in range(1, count)]
    own_kv = kv_all[0]
    log_sum = log_sum[:, :, :1]
    query_w, key_w, value_w, out_w = (half(w, x) for w in (w_query, w_key, w_value, w_out))
    wide = x_all[0].astype(F32)
    normed1_all, inverse1 = normed_rows(wide)
    mean1 = jnp.mean(wide, axis=1, keepdims=True)
    normed2_all, inverse2_all = normed_rows(wide + branch.astype(F32))

    def split(block):
        return block.reshape(block.shape[0], heads, HD)

    query_heads = split(query)

    def share_of(array):
        return lax.dynamic_slice_in_dim(array, x * share_rows, share_rows, 0)

    def block_of(array):
        return lax.dynamic_slice_in_dim(share_of(array), column * share_width, share_width, 1)

    resid = layer_input.astype(F32) + block_of(branch).astype(F32)
    normed2, inverse2 = block_of(normed2_all), share_of(inverse2_all)

    grad_act = jnp.dot(grad_out, down_full, preferred_element_type=F32)
    up_f = jnp.dot(mlp_in, up_full, preferred_element_type=F32)
    gelu_value, gelu_back = jax.vjp(jax.nn.gelu, up_f)
    activated = gelu_value.astype(BF16)
    grad_up = gelu_back(grad_act)[0].astype(BF16)
    grad_mlp_part = jnp.einsum("tf,df->td", grad_up, up_full, preferred_element_type=F32)
    grad_mlp = layer_reduce(grad_mlp_part.astype(BF16)).astype(F32)
    down_part = jnp.einsum("tf,df->td", activated, down_full, preferred_element_type=F32)
    layer_output = (resid + layer_reduce(down_part.astype(BF16)).astype(F32)).astype(BF16)

    down_term = jnp.einsum("tc,tf->cf", grad_out, activated, preferred_element_type=F32)
    up_term = jnp.einsum("tc,tf->cf", mlp_in, grad_up, preferred_element_type=F32)

    def weight_home(term):
        mine = line_reduce(term.astype(BF16), count, z).astype(BF16)
        size = mine.shape[0] // 2
        other = swapped(lax.dynamic_slice_in_dim(mine, (1 - x) * size, size, 0), "x")
        own = lax.dynamic_slice_in_dim(mine, x * size, size, 0)
        return jnp.where(
            x == 0, jnp.concatenate([own, other], 1), jnp.concatenate([other, own], 1)
        ).astype(F32)

    down_grad = weight_home(down_term)
    up_grad = weight_home(up_term)

    def norm_back(grad, normed, inverse, gain_share):
        scaled = grad * gain_share
        sums = lax.psum(
            jnp.stack([jnp.sum(scaled, axis=1), jnp.sum(scaled * normed, axis=1)], axis=1),
            ("y", "core"),
        )
        centre, slope = sums[:, :1] / width, sums[:, 1:] / width
        return inverse * (scaled - centre - normed * slope), jnp.sum(grad * normed, axis=0)

    back2, gain2_part = norm_back(grad_mlp, normed2, inverse2, gain2_share)
    grad_resid = out_grad.astype(F32) + back2
    grad_branch = layer_gather(grad_resid.astype(BF16))
    out_weight_part = jnp.einsum("td,tf->df", grad_branch, attended, preferred_element_type=F32)
    grad_attended = jnp.dot(grad_branch, out_w, preferred_element_type=F32).astype(BF16)
    grad_heads = split(grad_attended)
    delta = jnp.einsum("thd,thd->ht", grad_heads.astype(F32), split(attended).astype(F32))

    def stage(kv, distance):
        keys, values = split(kv[:, :local]), split(kv[:, local:])
        places = key_place[jnp.maximum(z - distance, 0)]
        allowed = (places >= start_of) & (z >= distance)
        if distance == 0:
            at = jnp.arange(rows)
            allowed = (allowed & (at[None, :] <= at[:, None])) | (at[None, :] == at[:, None])
        scores = jnp.einsum("qhd,khd->hqk", query_heads, keys, preferred_element_type=F32) * (scale * LOG2E)
        probs = jnp.where(allowed[None], jnp.exp2(scores - log_sum), 0.0)
        grad_probs = jnp.einsum("qhd,khd->hqk", grad_heads, values, preferred_element_type=F32)
        grad_scores = (probs * (grad_probs - delta[:, :, None]) * scale).astype(BF16)
        grad_query = jnp.einsum("hqk,khd->qhd", grad_scores, keys, preferred_element_type=F32)
        grad_key = jnp.einsum("hqk,qhd->khd", grad_scores, query_heads, preferred_element_type=F32)
        grad_value = jnp.einsum(
            "hqk,qhd->khd", probs.astype(BF16), grad_heads, preferred_element_type=F32
        )
        return grad_query.reshape(rows, local), jnp.concatenate(
            [grad_key.reshape(rows, local), grad_value.reshape(rows, local)], axis=1
        )

    grad_query, moving = jnp.zeros((rows, local), F32), None
    for hop in range(1, count):
        more, grad_kv = stage(below[count - hop - 1], count - hop)
        grad_query = grad_query + more
        if moving is not None:
            grad_kv = grad_kv + moving.astype(F32)
        moving = shifted(grad_kv.astype(BF16), "z", -1, max(count - hop, 1), count - 1)
    more, grad_kv = stage(own_kv, 0)
    grad_query = (grad_query + more).astype(BF16)
    if moving is not None:
        grad_kv = grad_kv + moving.astype(F32)
    grad_kv = grad_kv.astype(BF16)
    grads = jnp.concatenate([grad_query, grad_kv], axis=1)

    qkv_w = jnp.concatenate([query_w, key_w, value_w], axis=1)
    grad_attn_part = jnp.einsum("tf,df->td", grads, qkv_w, preferred_element_type=F32)
    grad_attn = layer_reduce(grad_attn_part.astype(BF16)).astype(F32)
    qkv_part = jnp.einsum("td,tf->df", attn_in, grads, preferred_element_type=F32)

    def weight_everywhere(partial):
        mine = line_reduce(partial.astype(BF16), count, z).astype(BF16)
        return line_whole(mine, count, z)

    def both_halves(block):
        other = swapped(block, "x")
        return jnp.where(
            x == 0, jnp.concatenate([block, other], 1), jnp.concatenate([other, block], 1)
        ).astype(F32)

    out_weight_grad = both_halves(weight_everywhere(out_weight_part))
    qkv_grad = weight_everywhere(qkv_part)
    query_grad = both_halves(qkv_grad[:, :local])
    key_grad = both_halves(qkv_grad[:, local : 2 * local])
    value_grad = both_halves(qkv_grad[:, 2 * local :])

    mean1_share, inverse1_share = share_of(mean1), share_of(inverse1)
    normed1 = (layer_input.astype(F32) - mean1_share) * inverse1_share
    back1, gain1_part = norm_back(grad_attn, normed1, inverse1_share, gain1_share)
    input_grad = grad_resid + back1

    gains = lax.psum(jnp.stack([gain1_part, gain2_part]), ("z", "x"))
    gains = lax.all_gather(gains, ("y", "core"), axis=1, tiled=True)
    return (
        layer_output,
        input_grad,
        gains[0],
        query_grad,
        key_grad,
        value_grad,
        out_weight_grad,
        gains[1],
        up_grad,
        down_grad,
    )


def solution(mesh):
    seq, head = mesh.shape["seq"], mesh.shape["head"]
    fine = Mesh(mesh.devices.reshape(seq // 2, 2, head // 2, 2), ("z", "x", "y", "core"))
    seq_axes, head_axes = ("z", "x"), ("y", "core")
    both, columns = P(seq_axes, head_axes), P(None, head_axes)
    return jax.shard_map(
        body,
        mesh=fine,
        in_specs=(both, P(), P(), P(), columns, columns, columns, columns, P(), both, both, both),
        out_specs=(both, both, P(), columns, columns, columns, columns, P(), both, both),
        check_vma=False,
    )
```

```python
import functools

import jax
import jax.numpy as jnp
from jax import lax
from jax.experimental import pallas as pl
from jax.experimental.pallas import tpu as pltpu
from jax.sharding import Mesh, PartitionSpec as P

HD = 128
NORM_EPS = 1e-05
BF16 = jnp.bfloat16
F32 = jnp.float32
LAYER = ("x", "y", "core")


MESH = pl.DeviceIdType.MESH
LOG2E = 1.4426950408889634


def remote(src, dst, sends, recvs, slot, **device):
    return pltpu.make_async_remote_copy(
        src_ref=src,
        dst_ref=dst,
        send_sem=sends.at[slot],
        recv_sem=recvs.at[slot],
        device_id=device,
        device_id_type=MESH,
    )


def contract(left, right, dims):
    return lax.dot_general(left, right, (dims, ((), ())), preferred_element_type=F32)


class Place:
    def __init__(self, count):
        self.count = count
        self.z = lax.axis_index("z")
        self.x, self.y, self.c = lax.axis_index("x"), lax.axis_index("y"), lax.axis_index("core")
        self.ox, self.oy, self.oc = 1 - self.x, 1 - self.y, 1 - self.c

    def meet(self, whole_line=False):
        barrier = pltpu.get_barrier_semaphore()
        for device in ({"x": self.ox}, {"y": self.oy}, {"core": self.oc}):
            pl.semaphore_signal(barrier, inc=1, device_id=device, device_id_type=MESH)
        if whole_line:
            for step in range(1, self.count):
                pl.semaphore_signal(
                    barrier,
                    inc=1,
                    device_id={"z": lax.rem(self.z + step, self.count)},
                    device_id_type=MESH,
                )
            pl.semaphore_wait(barrier, 3 + self.count - 1)
            return
        above, below = self.z < self.count - 1, self.z > 0
        for there, step in ((above, 1), (below, -1)):

            @pl.when(there)
            def _():
                pl.semaphore_signal(
                    barrier, inc=1, device_id={"z": self.z + step}, device_id_type=MESH
                )

        pl.semaphore_wait(barrier, 3 + above.astype(jnp.int32) + below.astype(jnp.int32))


class Gather:
    def __init__(self, at, array, rows, width, sends, recvs, lead=()):
        self.at, self.array, self.sends, self.recvs, self.lead = at, array, sends, recvs, lead
        self.rows, self.width = rows, width

    def block(self, xi, yi, ci, first=0, size=None):
        size = self.rows if size is None else size
        return self.array.at[
            pl.ds(pl.multiple_of(xi * self.rows + first, size), size),
            pl.ds(pl.multiple_of((2 * yi + ci) * self.width, self.width), self.width),
        ]

    def copy(self, k, landing=False):
        at, half = self.at, self.rows // 2
        x, y, c, ox, oy, oc = at.x, at.y, at.c, at.ox, at.oy, at.oc
        place = {
            0: ((x, y, c), (ox, y, c), {"x": ox}),
            1: ((x, y, c), (x, oy, c), {"y": oy}),
            2: ((x, y, c), (x, y, oc), {"core": oc}),
            3: ((ox, y, c, 0, half), (ox, oy, c, 0, half), {"y": oy}),
            4: ((x, oy, c, half, half), (ox, oy, c, half, half), {"x": ox}),
            5: ((ox, y, c), (ox, y, oc), {"core": oc}),
            6: ((x, oy, c), (x, oy, oc), {"core": oc}),
            7: ((ox, oy, c, 0, half), (ox, oy, oc, 0, half), {"core": oc}),
            8: ((ox, oy, c, half, half), (ox, oy, oc, half, half), {"core": oc}),
        }
        source, lands, device = place[k]
        ref = self.block(*(lands if landing else source))
        return remote(ref, ref, self.sends, self.recvs, self.lead + (k,), **device)

    def start(self):
        for k in (0, 1, 2):
            self.copy(k).start()

    def middle(self):
        self.copy(0, True).wait_recv()
        self.copy(3).start()
        self.copy(5).start()
        self.copy(1, True).wait_recv()
        self.copy(4).start()
        self.copy(6).start()

    def corner(self):
        self.copy(3, True).wait_recv()
        self.copy(7).start()
        self.copy(4, True).wait_recv()
        self.copy(8).start()

    def end(self):
        for k in (2, 5, 6, 7, 8):
            self.copy(k, True).wait_recv()

    def drain(self):
        for k in range(9):
            self.copy(k).wait_send()


class Reduce:
    def __init__(self, at, array, rows, width, buffers, sends, recvs):
        self.at, self.array, self.sends, self.recvs = at, array, sends, recvs
        self.rows, self.width = rows, width
        self.twin, self.corner_x, self.corner_y, self.from_x, self.from_y = buffers

    def block(self, xi, yi, ci, first=0, size=None):
        return Gather.block(self, xi, yi, ci, first, size)

    def copy(self, k):
        at, half = self.at, self.rows // 2
        x, y, c, ox, oy, oc = at.x, at.y, at.c, at.ox, at.oy, at.oc
        low, high = pl.ds(0, half), pl.ds(half, half)
        place = {
            0: ((ox, oy, oc), self.twin.at[0], {"core": oc}),
            1: ((ox, y, oc), self.twin.at[1], {"core": oc}),
            2: ((x, oy, oc), self.twin.at[2], {"core": oc}),
            3: ((x, y, oc), self.twin.at[3], {"core": oc}),
            4: ((ox, oy, c, 0, half), self.corner_y, {"y": oy}),
            5: ((ox, oy, c, half, half), self.corner_x, {"x": ox}),
            6: ((ox, y, c, half, half), self.from_x.at[high], {"x": ox}),
            7: ((x, oy, c, 0, half), self.from_y.at[low], {"y": oy}),
            8: ((ox, y, c, 0, half), self.from_x.at[low], {"x": ox}),
            9: ((x, oy, c, half, half), self.from_y.at[high], {"y": oy}),
        }
        source, lands, device = place[k]
        return remote(self.block(*source), lands, self.sends, self.recvs, (k,), **device)

    def add(self, target, other):
        rows = target.shape[0]
        tile = min(rows, 128)

        @pl.loop(0, rows // tile)
        def _(i):
            part = pl.ds(pl.multiple_of(i * tile, tile), tile)
            target[part, :] = (target[part, :].astype(F32) + other[part, :].astype(F32)).astype(
                target.dtype
            )

    def start(self):
        for k in (0, 1, 2, 3):
            self.copy(k).start()

    def twins(self):
        at, half = self.at, self.rows // 2
        x, y, c, ox, oy = at.x, at.y, at.c, at.ox, at.oy
        self.copy(0).wait_recv()
        self.add(self.block(ox, oy, c), self.twin.at[0])
        self.copy(4).start()
        self.copy(5).start()
        self.copy(1).wait_recv()
        self.add(self.block(ox, y, c), self.twin.at[1])
        self.copy(6).start()
        self.copy(2).wait_recv()
        self.add(self.block(x, oy, c), self.twin.at[2])
        self.copy(7).start()
        self.copy(3).wait_recv()

    def corners(self):
        at, half = self.at, self.rows // 2
        self.copy(4).wait_recv()
        self.add(self.block(at.ox, at.y, at.c, 0, half), self.corner_y)
        self.copy(8).start()
        self.copy(5).wait_recv()
        self.add(self.block(at.x, at.oy, at.c, half, half), self.corner_x)
        self.copy(9).start()

    def end(self, store):
        for k in (6, 7, 8, 9):
            self.copy(k).wait_recv()
        own = self.block(self.at.x, self.at.y, self.at.c)
        tile = min(self.rows, 128)

        @pl.loop(0, self.rows // tile)
        def _(i):
            part = pl.ds(pl.multiple_of(i * tile, tile), tile)
            store(
                part,
                own[part, :].astype(F32)
                + self.twin[3, part, :].astype(F32)
                + self.from_x[part, :].astype(F32)
                + self.from_y[part, :].astype(F32),
            )

    def drain(self):
        for k in range(10):
            self.copy(k).wait_send()


def reduce_scratch(rows, width):
    return [
        pltpu.VMEM((4, rows, width), BF16),
        pltpu.VMEM((rows // 2, width), BF16),
        pltpu.VMEM((rows // 2, width), BF16),
        pltpu.VMEM((rows, width), BF16),
        pltpu.VMEM((rows, width), BF16),
    ]


def normed_rows(rows):
    mean = jnp.mean(rows, axis=1, keepdims=True)
    centred = rows - mean
    inverse = lax.rsqrt(jnp.mean(centred * centred, axis=1, keepdims=True) + NORM_EPS)
    return centred * inverse, inverse


class Weights:
    def __init__(self, at, which, weight, whole, sems):
        self.at, self.which, self.weight, self.whole = at, which, weight, whole
        self.local, self.xs, self.xr, self.us, self.ds, self.rs = sems
        self.half = weight.shape[1] // 2

    def columns(self, which):
        return self.weight.at[:, pl.ds(pl.multiple_of(which * self.half, self.half), self.half)]

    def own(self):
        at = self.at
        return pltpu.make_async_copy(
            self.columns(at.x), self.whole.at[at.z, at.x], self.local.at[self.which]
        )

    def swap(self, landing=False):
        at = self.at
        dst = self.whole.at[at.z, at.ox] if landing else self.whole.at[at.z, at.x]
        return remote(self.columns(at.ox), dst, self.xs, self.xr, (self.which,), x=at.ox)

    def move(self, layer, part, step):
        ref = self.whole.at[layer, part]
        sends = self.us if step > 0 else self.ds
        return pltpu.make_async_remote_copy(
            src_ref=ref,
            dst_ref=ref,
            send_sem=sends.at[self.which, layer, part],
            recv_sem=self.rs.at[self.which, layer, part],
            device_id={"z": self.at.z + step},
            device_id_type=MESH,
        )

    def first(self, mine):
        at = self.at
        part = at.x if mine else at.ox
        if mine:
            self.own().wait()
        else:
            self.swap(True).wait_recv()

        @pl.when(at.z < at.count - 1)
        def _():
            self.move(at.z, part, 1).start()

        @pl.when(at.z > 0)
        def _():
            self.move(at.z, part, -1).start()

    def hop(self, distance, mine):
        at = self.at
        part = at.x if mine else at.ox

        @pl.when(at.z >= distance)
        def _():
            self.move(at.z - distance, part, 1).wait_recv()

            @pl.when(at.z < at.count - 1)
            def _():
                self.move(at.z - distance, part, 1).start()

        @pl.when(at.z + distance < at.count)
        def _():
            self.move(at.z + distance, part, -1).wait_recv()

            @pl.when(at.z > 0)
            def _():
                self.move(at.z + distance, part, -1).start()

    def drain(self):
        at = self.at
        self.swap().wait_send()
        for part in (0, 1):

            @pl.loop(0, at.count)
            def _(layer):
                @pl.when((layer <= at.z) & (at.z < at.count - 1))
                def _():
                    self.move(layer, part, 1).wait_send()

                @pl.when((layer >= at.z) & (at.z > 0))
                def _():
                    self.move(layer, part, -1).wait_send()


def front_kernel(
    count,
    xs,
    og,
    w_query,
    w_key,
    w_value,
    w_out,
    w_up,
    w_down,
    gain1,
    gain2,
    start_of,
    key_place,
    x_all,
    in_all,
    kv_all,
    query_out,
    attended_out,
    log_out,
    branch_out,
    mlp_out,
    og_all,
    down_all,
    up_all,
    qkv_w,
    out_w,
    query,
    kv,
    high,
    total,
    sums,
    attended,
    partial,
    branch,
    twin,
    corner_x,
    corner_y,
    from_x,
    from_y,
    load_sem,
    gather_send,
    gather_recv,
    line_send,
    line_recv,
    w_local,
    w_xs,
    w_xr,
    w_us,
    w_ds,
    w_rs,
    reduce_send,
    reduce_recv,
):
    at = Place(count)
    z, x, y, c = at.z, at.x, at.y, at.c
    rows, width = xs.shape
    group = 2 * rows
    local = w_query.shape[1] // 2
    heads = local // HD
    features = gain1.shape[1]
    tile = 256 if group % 256 == 0 else group
    tiles = group // tile

    def columns_of(weight):
        return weight.at[:, pl.ds(pl.multiple_of(x * local, local), local)]

    loads = [
        pltpu.make_async_copy(
            columns_of(w), qkv_w.at[:, pl.ds(i * local, local)], load_sem.at[i]
        )
        for i, w in enumerate((w_key, w_value, w_query))
    ]
    loads.append(pltpu.make_async_copy(columns_of(w_out), out_w, load_sem.at[3]))

    def gather_of(d):
        return Gather(at, x_all.at[d], rows, width, gather_send, gather_recv, (d,))

    og_gather = Gather(at, og_all, rows, width, gather_send, gather_recv, (count,))
    branch_gather = Gather(at, branch, rows, width, gather_send, gather_recv, (count + 1,))

    def own_block(d):
        return gather_of(d).block(x, y, c)

    def line_copy(d):
        return remote(own_block(d), own_block(d + 1), line_send, line_recv, (d,), z=z + 1)

    weight_sems = (w_local, w_xs, w_xr, w_us, w_ds, w_rs)
    down = Weights(at, 0, w_down, down_all, weight_sems)
    up = Weights(at, 1, w_up, up_all, weight_sems)

    own_x = pltpu.make_async_copy(xs, own_block(0), load_sem.at[4])
    own_og = pltpu.make_async_copy(og, og_gather.block(x, y, c), load_sem.at[5])
    own_x.start()
    down.own().start()
    up.own().start()
    own_og.start()
    for load in loads:
        load.start()
    at.meet()
    own_x.wait()

    @pl.when(z < count - 1)
    def _():
        line_copy(0).start()

    gather_of(0).start()
    down.first(True)
    gather_of(0).middle()
    down.swap().start()
    for load in loads:
        load.wait()

    def project(d, with_query):
        size = qkv_w.shape[1] if with_query else 2 * local

        def step(x_ref, in_ref, kv_ref, *maybe_query):
            normed, _ = normed_rows(x_ref[...].astype(F32))
            rounded = (normed * gain1[...]).astype(BF16)
            in_ref[...] = rounded
            product = jnp.dot(rounded, qkv_w[:, :size], preferred_element_type=F32)
            kv_ref[...] = product[:, : 2 * local].astype(BF16)
            if with_query:
                maybe_query[0][...] = product[:, 2 * local :].astype(BF16)

        def rows_of(size):
            return pl.BlockSpec((tile, size), lambda i: (i, 0))

        outs = [rows_of(features), rows_of(2 * local)] + ([rows_of(local)] if with_query else [])
        refs = [in_all.at[d], kv_all.at[d]] + ([query_out] if with_query else [])
        pltpu.emit_pipeline(step, grid=(tiles,), in_specs=[rows_of(features)], out_specs=outs)(
            x_all.at[d], *refs
        )

    def attend(d, diagonal):
        keys = key_place[z - d]

        @pl.loop(0, tiles)
        def _(i):
            part = pl.ds(pl.multiple_of(i * tile, tile), tile)
            allowed = keys >= start_of[part, :]
            if diagonal:
                query_at = lax.broadcasted_iota(jnp.int32, (tile, group), 0) + i * tile
                key_at = lax.broadcasted_iota(jnp.int32, (tile, group), 1)
                allowed = (allowed & (key_at <= query_at)) | (key_at == query_at)
            for h in range(heads):
                span = slice(h * HD, (h + 1) * HD)
                scores = contract(query[part, span], kv[:, span], ((1,), (1,)))
                scores = jnp.where(allowed, scores * (HD**-0.5 * LOG2E), -1e30)
                top = jnp.max(scores, axis=1, keepdims=True)
                if not diagonal:
                    old = high[h, part, :1]
                    top = jnp.maximum(old, top)
                    fade = jnp.exp2(old - top)
                weights = jnp.exp2(scores - top)
                mass = jnp.sum(weights, axis=1, keepdims=True)
                value = jnp.dot(
                    weights.astype(BF16),
                    kv[:, local + h * HD : local + (h + 1) * HD],
                    preferred_element_type=F32,
                )
                if not diagonal:
                    mass = mass + total[h, part, :1] * fade
                    value = value + sums[part, span] * fade
                high[h, part, :] = jnp.broadcast_to(top, (tile, HD))
                total[h, part, :] = jnp.broadcast_to(mass, (tile, HD))
                sums[part, span] = value

    def piece(d, diagonal):
        project(d, diagonal)
        pltpu.sync_copy(kv_all.at[d], kv)
        if diagonal:
            pltpu.sync_copy(query_out, query)
        attend(d, diagonal)

    halves = [(up, True), (down, False), (up, False)]

    def send_half(step):
        weight, mine = halves[step]
        weight.first(mine)
        if step == 0:
            up.swap().start()

    def bring(d):
        @pl.when(z >= d)
        def _():
            remote(own_block(d - 1), own_block(d), line_send, line_recv, (d - 1,), z=z).wait_recv()

            @pl.when((d < count - 1) & (z < count - 1))
            def _():
                line_copy(d).start()

            gather_of(d).start()

    def within(d, *names):
        @pl.when(z >= d)
        def _():
            for name in names:
                getattr(gather_of(d), name)()

    hops = [
        (weight, distance, mine)
        for distance in range(1, count)
        for weight, mine in ((down, True), (up, True), (down, False), (up, False))
    ]

    def hop(many=1):
        for _ in range(min(many, len(hops))):
            weight, distance, mine = hops.pop(0)
            weight.hop(distance, mine)

    gather_of(0).corner()
    gather_of(0).end()
    bring(1)
    send_half(0)
    piece(0, True)
    within(1, "middle")

    @pl.loop(2, count)
    def _(d):
        within(d - 1, "corner", "end")
        bring(d)
        for step in (1, 2):

            @pl.when(d == step + 1)
            def _():
                send_half(step)

        @pl.when(z >= d - 1)
        def _():
            piece(d - 1, False)

        within(d, "middle")

    for step in range(max(count - 1, 1), 3):
        send_half(step)
    hop(2)
    within(count - 1, "corner", "end")
    own_og.wait()
    og_gather.start()

    @pl.when(z >= count - 1)
    def _():
        piece(count - 1, False)

    hop()
    og_gather.middle()

    @pl.loop(0, tiles)
    def _(i):
        part = pl.ds(pl.multiple_of(i * tile, tile), tile)
        for h in range(heads):
            span = slice(h * HD, (h + 1) * HD)
            mass = total[h, part, :]
            attended[part, span] = (sums[part, span] / mass).astype(BF16)
            high[h, part, :] = high[h, part, :] + jnp.log2(mass)
        partial[part, :] = contract(attended[part, :], out_w[...], ((1,), (1,))).astype(BF16)

    outs = [
        pltpu.make_async_copy(attended, attended_out, load_sem.at[6]),
        pltpu.make_async_copy(high, log_out, load_sem.at[7]),
    ]
    for out in outs:
        out.start()
    hop()
    og_gather.corner()
    reduce = Reduce(
        at, partial, rows, width, (twin, corner_x, corner_y, from_x, from_y), reduce_send, reduce_recv
    )
    reduce.start()
    og_gather.end()
    reduce.twins()
    hop()
    reduce.corners()
    hop()
    own_branch = branch_gather.block(x, y, c)

    def store(part, value):
        own_branch[part, :] = value.astype(BF16)

    reduce.end(store)
    branch_gather.start()
    hop()
    branch_gather.middle()
    hop()
    branch_gather.corner()
    hop()
    branch_gather.end()
    pltpu.sync_copy(branch, branch_out)

    def second_norm(x_ref, branch_ref, mlp_ref):
        normed, _ = normed_rows(x_ref[...].astype(F32) + branch_ref[...].astype(F32))
        mlp_ref[...] = (normed * gain2[...]).astype(BF16)

    spec = pl.BlockSpec((tile, features), lambda i: (i, 0))
    pltpu.emit_pipeline(second_norm, grid=(tiles,), in_specs=[spec, spec], out_specs=[spec])(
        x_all.at[0], branch_out, mlp_out
    )
    hop(len(hops))

    for out in outs:
        out.wait()
    down.drain()
    up.drain()
    reduce.drain()
    branch_gather.drain()
    og_gather.drain()

    @pl.loop(0, count)
    def _(d):
        within(d, "drain")

        @pl.when((z >= d) & (d < count - 1) & (z < count - 1))
        def _():
            line_copy(d).wait_send()


def front(count, xs, og, w_query, w_key, w_value, w_out, w_up, w_down, gain1, gain2, start_of, key_place):
    rows, width = xs.shape
    group, features = 2 * rows, gain1.shape[1]
    local = w_query.shape[1] // 2
    heads = local // HD
    hidden = w_up.shape[1] // 2
    w_rows = w_up.shape[0]
    hbm, vmem = pl.BlockSpec(memory_space=pl.ANY), pl.BlockSpec(memory_space=pltpu.VMEM)

    def out(*shape, dtype=BF16):
        return jax.ShapeDtypeStruct(shape, dtype)

    dma = pltpu.SemaphoreType.DMA
    return pl.pallas_call(
        functools.partial(front_kernel, count),
        name="front",
        out_shape=(
            out(count, group, features),
            out(count, group, features),
            out(count, group, 2 * local),
            out(group, local),
            out(group, local),
            out(heads, group, HD, dtype=F32),
            out(group, features),
            out(group, features),
            out(group, features),
            out(count, 2, w_rows, hidden),
            out(count, 2, w_rows, hidden),
        ),
        in_specs=[hbm] * 8 + [vmem] * 4,
        out_specs=[hbm] * 11,
        scratch_shapes=[
            pltpu.VMEM((features, 3 * local), BF16),
            pltpu.VMEM((features, local), BF16),
            pltpu.VMEM((group, local), BF16),
            pltpu.VMEM((group, 2 * local), BF16),
            pltpu.VMEM((heads, group, HD), F32),
            pltpu.VMEM((heads, group, HD), F32),
            pltpu.VMEM((group, local), F32),
            pltpu.VMEM((group, local), BF16),
            pltpu.VMEM((group, features), BF16),
            pltpu.VMEM((group, features), BF16),
            *reduce_scratch(rows, width),
            dma((8,)),
            dma((count + 2, 9)),
            dma((count + 2, 9)),
            dma((count,)),
            dma((count,)),
            dma((2,)),
            dma((2,)),
            dma((2,)),
            dma((2, count, 2)),
            dma((2, count, 2)),
            dma((2, count, 2)),
            dma((10,)),
            dma((10,)),
        ],
        compiler_params=pltpu.CompilerParams(
            collective_id=0, has_side_effects=True, vmem_limit_bytes=56 * 1024 * 1024
        ),
    )(xs, og, w_query, w_key, w_value, w_out, w_up, w_down, gain1, gain2, start_of, key_place)


class LineSum:
    def __init__(self, at, which, terms, landing, sums, sends, recvs):
        self.at, self.which = at, which
        self.terms, self.landing, self.sums = terms, landing, sums
        self.sends, self.recvs = sends, recvs
        self.rows = sums.shape[2]

    def chunk(self, c):
        return self.terms.at[self.which, pl.ds(pl.multiple_of(c * self.rows, self.rows), self.rows)]

    def move(self, source, c, slot, step):
        return pltpu.make_async_remote_copy(
            src_ref=source,
            dst_ref=self.landing.at[self.which, slot],
            send_sem=self.sends.at[self.which, c],
            recv_sem=self.recvs.at[self.which, slot],
            device_id={"z": self.at.z + step},
            device_id_type=MESH,
        )

    def landed(self, slot):
        ref = self.landing.at[self.which, slot]
        self.move(ref, 0, slot, 0).wait_recv()

    def total(self, refs, out):
        tile = min(256, self.rows)

        def step(*tiles):
            value = tiles[0][...].astype(F32)
            for other in tiles[1:-1]:
                value = value + other[...].astype(F32)
            tiles[-1][...] = value.astype(BF16)

        spec = pl.BlockSpec((tile, self.sums.shape[3]), lambda i: (i, 0))
        pltpu.emit_pipeline(
            step, grid=(self.rows // tile,), in_specs=[spec] * len(refs), out_specs=[spec]
        )(*refs, out)

    def hop(self, h):
        at, n, z = self.at, self.at.count, self.at.z
        for step, c, there, slot in (
            (1, n - h + z, (z <= h - 1) & (z < n - 1), n - h + z),
            (-1, z - n + h, (z >= n - h) & (z > 0), None),
        ):
            if slot is None:
                slot = jnp.where(c == z - 1, n, c)
            first = z == (0 if step > 0 else n - 1)

            @pl.when(there & first)
            def _():
                self.move(self.chunk(c), c, slot, step).start()

            @pl.when(there & jnp.logical_not(first))
            def _():
                self.landed(c)
                self.total([self.chunk(c), self.landing.at[self.which, c]], self.sums.at[self.which, c])
                self.move(self.sums.at[self.which, c], c, slot, step).start()

    def final(self, out):
        n, z = self.at.count, self.at.z
        below, above = self.landing.at[self.which, z], self.landing.at[self.which, n]

        @pl.when(z > 0)
        def _():
            self.landed(z)

        @pl.when(z < n - 1)
        def _():
            self.landed(n)

        @pl.when(z == 0)
        def _():
            self.total([self.chunk(z), above], out)

        @pl.when(z == n - 1)
        def _():
            self.total([self.chunk(z), below], out)

        @pl.when((z > 0) & (z < n - 1))
        def _():
            self.total([self.chunk(z), below, above], out)

    def drain(self):
        z = self.at.z

        @pl.loop(0, self.at.count)
        def _(c):
            @pl.when(c != z)
            def _():
                self.move(self.chunk(c), c, 0, 0).wait_send()


class Spread:
    def __init__(self, at, whole, ups, downs, lines, sides, sidesr):
        self.at, self.whole = at, whole
        self.ups, self.downs, self.lines, self.sides, self.sidesr = ups, downs, lines, sides, sidesr

    def move(self, layer, step):
        ref = self.whole.at[layer, self.at.x]
        sends = self.ups if step > 0 else self.downs
        return remote(ref, ref, sends, self.lines, (layer,), z=self.at.z + step)

    def side(self, layer, part):
        ref = self.whole.at[layer, part]
        return remote(ref, ref, self.sides, self.sidesr, (layer,), x=self.at.ox)

    def first(self):
        at = self.at

        @pl.when(at.z < at.count - 1)
        def _():
            self.move(at.z, 1).start()

        @pl.when(at.z > 0)
        def _():
            self.move(at.z, -1).start()

        self.side(at.z, at.x).start()

    def hop(self, distance):
        at = self.at

        @pl.when(at.z >= distance)
        def _():
            self.move(at.z - distance, 1).wait_recv()

            @pl.when(at.z < at.count - 1)
            def _():
                self.move(at.z - distance, 1).start()

            self.side(at.z - distance, at.x).start()

        @pl.when(at.z + distance < at.count)
        def _():
            self.move(at.z + distance, -1).wait_recv()

            @pl.when(at.z > 0)
            def _():
                self.move(at.z + distance, -1).start()

            self.side(at.z + distance, at.x).start()

    def end(self):
        at = self.at

        @pl.loop(0, at.count)
        def _(layer):
            self.side(layer, at.ox).wait_recv()
            self.side(layer, at.x).wait_send()

            @pl.when((layer <= at.z) & (at.z < at.count - 1))
            def _():
                self.move(layer, 1).wait_send()

            @pl.when((layer >= at.z) & (at.z > 0))
            def _():
                self.move(layer, -1).wait_send()


def back_kernel(
    count,
    x_all,
    in_all,
    kv_all,
    query_in,
    attended_in,
    log_in,
    branch_in,
    mlp_in,
    og_all,
    down_all,
    up_all,
    w_query,
    w_key,
    w_value,
    w_out,
    gain1,
    gain2,
    start_row,
    key_place,
    output,
    input_grad,
    gains_out,
    mlp_grads,
    attn_grads,
    terms,
    landing,
    sums,
    mine,
    grad_branch,
    grad_resid,
    kv_own,
    kv_landing,
    kv_sums,
    partial,
    partial2,
    full1,
    full3,
    twin_a,
    corner_xa,
    corner_ya,
    from_xa,
    from_ya,
    twin_b,
    corner_xb,
    corner_yb,
    from_xb,
    from_yb,
    twin_c,
    corner_xc,
    corner_yc,
    from_xc,
    from_yc,
    gains,
    gains_landing,
    load_sem,
    reduce_send,
    reduce_recv,
    gather_send,
    gather_recv,
    sum_send,
    sum_recv,
    home_send,
    home_recv,
    spread_up,
    spread_down,
    spread_line,
    spread_side,
    spread_side_recv,
    kv_send,
    kv_recv,
    gain_send,
    gain_recv,
):
    at = Place(count)
    z, x, y, c = at.z, at.x, at.y, at.c
    group, features = mlp_in.shape
    rows = group // 2
    width = output.shape[1]
    local = w_query.shape[1] // 2
    heads = local // HD
    hidden = down_all.shape[1]
    tile = min(256, group)
    tiles = group // tile
    thin = min(128, group)
    block = min(512, features)
    blocks = features // block
    own_column = pl.ds(pl.multiple_of((2 * y + c) * width, width), width)

    def columns_of(weight):
        return weight.at[:, pl.ds(pl.multiple_of(x * local, local), local)]

    def rows_spec(size, many=None):
        return pl.BlockSpec((many or tile, size), lambda i: (i, 0))

    def column_spec(tall):
        return pl.BlockSpec((tall, block), lambda i: (0, i))

    def whole_spec(*shape):
        return pl.BlockSpec(shape, lambda i: (0,) * len(shape))

    def reduce_of(array, buffers, k):
        return Reduce(at, array, rows, width, buffers, reduce_send.at[k], reduce_recv.at[k])

    def gather_of(array, k):
        return Gather(at, array, rows, width, gather_send, gather_recv, (k,))

    first_sum = reduce_of(partial, (twin_a, corner_xa, corner_ya, from_xa, from_ya), 0)
    out_sum = reduce_of(partial2, (twin_b, corner_xb, corner_yb, from_xb, from_yb), 1)
    last_sum = reduce_of(partial, (twin_c, corner_xc, corner_yc, from_xc, from_yc), 2)
    first_gather, last_gather = gather_of(full1, 0), gather_of(full3, 1)
    down_line, up_line, attn_line = (
        LineSum(at, k, terms, landing, sums, sum_send, sum_recv) for k in range(3)
    )
    spread = Spread(
        at, attn_grads, spread_up, spread_down, spread_line, spread_side, spread_side_recv
    )

    def weight_terms(which, left, right, size, column):
        def step(left_ref, right_ref, out_ref):
            out_ref[...] = contract(left_ref[...], right_ref[...], ((0,), (0,))).astype(BF16)

        pltpu.emit_pipeline(
            step,
            grid=(blocks,),
            in_specs=[column_spec(group), whole_spec(group, size)],
            out_specs=[pl.BlockSpec((block, size), lambda i: (i, column))],
        )(left, right, terms.at[which])

    def home(which):
        line = (down_line, up_line)[which]
        line.final(mine.at[which])
        half = mine.shape[1] // 2
        own = pltpu.make_async_copy(
            mine.at[which, pl.ds(pl.multiple_of(x * half, half), half)],
            mlp_grads.at[which, x],
            load_sem.at[which],
        )
        own.start()
        home_copy(which).start()
        own.wait()

    def home_copy(which, landing_part=False):
        half = mine.shape[1] // 2
        return remote(
            mine.at[which, pl.ds(pl.multiple_of(at.ox * half, half), half)],
            mlp_grads.at[which, at.ox if landing_part else x],
            home_send,
            home_recv,
            (which,),
            x=at.ox,
        )

    def store_into(gather):
        def store(part, value):
            gather.block(x, y, c)[part, :] = value.astype(BF16)

        return store

    at.meet(whole_line=True)

    def feed_forward(active, grad_up, w_down, w_up):
        loads = [
            pltpu.make_async_copy(up_all, w_up, load_sem.at[0]),
            pltpu.make_async_copy(down_all, w_down, load_sem.at[1]),
        ]
        for load in loads:
            load.start()
        for load in loads:
            load.wait()

        def step(mlp_ref, og_ref, active_ref, grad_ref):
            up = jnp.dot(mlp_ref[...], w_up[...], preferred_element_type=F32)
            grad = jnp.dot(og_ref[...], w_down[...], preferred_element_type=F32)
            square = up * up
            root = 0.7978845608028654
            bend = jnp.tanh(up * (root + (root * 0.044715) * square))
            half = 0.5 * (1.0 + bend)
            slope = half + 0.5 * up * (1.0 - bend * bend) * (root + (3.0 * root * 0.044715) * square)
            active_ref[...] = (up * half).astype(BF16)
            grad_ref[...] = (grad * slope).astype(BF16)

        pltpu.emit_pipeline(
            step,
            grid=(tiles,),
            in_specs=[rows_spec(features)] * 2,
            out_specs=[rows_spec(hidden)] * 2,
        )(mlp_in, og_all, active, grad_up)
        weight_terms(0, og_all, active, hidden, 0)
        down_line.hop(1)
        weight_terms(1, mlp_in, grad_up, hidden, 0)
        up_line.hop(1)

        @pl.loop(0, tiles)
        def _(i):
            part = pl.ds(pl.multiple_of(i * tile, tile), tile)
            partial[part, :] = contract(grad_up[part, :], w_up[...], ((1,), (1,))).astype(BF16)

        first_sum.start()

        @pl.loop(0, tiles)
        def _(i):
            part = pl.ds(pl.multiple_of(i * tile, tile), tile)
            partial2[part, :] = contract(active[part, :], w_down[...], ((1,), (1,))).astype(BF16)

    pl.run_scoped(
        feed_forward,
        pltpu.VMEM((group, hidden), BF16),
        pltpu.VMEM((group, hidden), BF16),
        pltpu.VMEM((features, hidden), BF16),
        pltpu.VMEM((features, hidden), BF16),
    )
    first_sum.twins()
    first_sum.corners()
    first_sum.end(store_into(first_gather))
    first_gather.start()
    down_line.hop(2)
    first_gather.middle()
    first_gather.corner()
    first_gather.end()
    out_sum.start()

    def attention(
        qkv_w, out_w, query, attended, kv, grad_att, grad_query, grad_kv, grad_kv_low, kv_weight,
        logs, log_row, delta_row, wide, resid_x, resid_branch,
    ):
        loads = [
            pltpu.make_async_copy(
                columns_of(w), qkv_w.at[:, pl.ds(i * local, local)], load_sem.at[i]
            )
            for i, w in enumerate((w_key, w_value, w_query))
        ]
        loads += [
            pltpu.make_async_copy(columns_of(w_out), out_w, load_sem.at[3]),
            pltpu.make_async_copy(query_in, query, load_sem.at[4]),
            pltpu.make_async_copy(attended_in, attended, load_sem.at[5]),
            pltpu.make_async_copy(log_in, logs, load_sem.at[6]),
        ]
        for load in loads:
            load.start()
        for load in loads:
            load.wait()
        gains[...] = jnp.zeros_like(gains)

        def second_back(x_ref, branch_ref, og_ref, grad_ref, low_ref, resid_ref, att_ref):
            normed, inverse = normed_rows(x_ref[...].astype(F32) + branch_ref[...].astype(F32))
            grad = grad_ref[...].astype(F32)
            scaled = grad * gain2[...]
            centre = jnp.mean(scaled, axis=1, keepdims=True)
            slope = jnp.mean(scaled * normed, axis=1, keepdims=True)
            gains[1:2, :] += jnp.sum(grad * normed, axis=0, keepdims=True)
            total = og_ref[...].astype(F32) + inverse * (scaled - centre - normed * slope)
            wide[...] = total
            low = total.astype(BF16)
            low_ref[...] = low
            resid_ref[...] = wide[:, own_column]
            att_ref[...] = jnp.dot(low, out_w[...], preferred_element_type=F32).astype(BF16)

        thin_spec = rows_spec(features, thin)
        pltpu.emit_pipeline(
            second_back,
            grid=(group // thin,),
            in_specs=[thin_spec] * 4,
            out_specs=[thin_spec, rows_spec(width, thin), rows_spec(local, thin)],
        )(x_all.at[0], branch_in, og_all, full1, grad_branch, grad_resid, grad_att)
        up_line.hop(2)
        out_sum.twins()
        weight_terms(2, grad_branch, attended, local, 3)
        for h in range(heads):
            span = slice(h * HD, (h + 1) * HD)
            log_row[h] = jnp.transpose(logs[h])[:1]
            product = grad_att[:, span].astype(F32) * attended[:, span].astype(F32)
            delta_row[h] = jnp.sum(jnp.transpose(product), axis=0, keepdims=True)
        grad_query[...] = jnp.zeros_like(grad_query)
        kv_weight[...] = jnp.zeros_like(kv_weight)

        def stage(layer, diagonal):
            pltpu.sync_copy(kv_all.at[z - layer], kv)
            grad_kv[...] = jnp.zeros_like(grad_kv)
            keys = jnp.transpose(jnp.broadcast_to(key_place[layer], (HD, group)))[:, :1]

            @pl.loop(0, tiles)
            def _(i):
                part = pl.ds(pl.multiple_of(i * tile, tile), tile)
                allowed = keys >= start_row[:, part]
                if diagonal:
                    query_at = lax.broadcasted_iota(jnp.int32, (group, tile), 1) + i * tile
                    key_at = lax.broadcasted_iota(jnp.int32, (group, tile), 0)
                    allowed = (allowed & (key_at <= query_at)) | (key_at == query_at)
                for h in range(heads):
                    span = slice(h * HD, (h + 1) * HD)
                    value_span = slice(local + h * HD, local + (h + 1) * HD)
                    key, value = kv[:, span], kv[:, value_span]
                    asked, grad = query[part, span], grad_att[part, span]
                    scores = contract(key, asked, ((1,), (1,))) * (HD**-0.5 * LOG2E)
                    probs = jnp.exp2(jnp.where(allowed, scores, -1e30) - log_row[h, :, part])
                    grad_probs = contract(value, grad, ((1,), (1,)))
                    grad_scores = (
                        probs * (grad_probs - delta_row[h, :, part]) * HD**-0.5
                    ).astype(BF16)
                    grad_kv[:, value_span] += jnp.dot(
                        probs.astype(BF16), grad, preferred_element_type=F32
                    )
                    grad_kv[:, span] += jnp.dot(grad_scores, asked, preferred_element_type=F32)
                    grad_query[part, span] += contract(grad_scores, key, ((0,), (0,)))

            grad_kv_low[...] = grad_kv[...].astype(BF16)

            def add(in_ref, grad_ref, out_ref):
                out_ref[...] += contract(in_ref[...], grad_ref[...], ((0,), (0,)))

            pltpu.emit_pipeline(
                add,
                grid=(blocks,),
                in_specs=[column_spec(group), whole_spec(group, 2 * local)],
                out_specs=[pl.BlockSpec((block, 2 * local), lambda i: (i, 0))],
            )(in_all.at[z - layer], grad_kv_low, kv_weight)

        def kv_move(layer, source):
            return remote(
                source.at[layer], kv_landing.at[layer], kv_send, kv_recv, (layer,), z=z - 1
            )

        def finish_output():
            own = pl.ds(pl.multiple_of(x * rows, rows), rows)
            pltpu.sync_copy(x_all.at[0, own, own_column], resid_x)
            pltpu.sync_copy(branch_in.at[own, own_column], resid_branch)

            def store(part, value):
                resid = resid_x[part, :].astype(F32) + resid_branch[part, :].astype(F32)
                resid_x[part, :] = (resid + value).astype(BF16)

            out_sum.end(store)
            pltpu.sync_copy(resid_x, output)

        events = [out_sum.corners, finish_output]
        for h in range(3, count):
            events += [functools.partial(down_line.hop, h), functools.partial(up_line.hop, h)]
        share = -(-len(events) // count)

        @pl.loop(0, count)
        def _(layer):
            @pl.when(layer < z)
            def _():
                stage(layer, False)
                pltpu.sync_copy(grad_kv_low, kv_own.at[layer])

                @pl.when(z == count - 1)
                def _():
                    kv_move(layer, kv_own).start()

            @pl.when(layer == z)
            def _():
                stage(layer, True)

            for k in range(count):
                batch = events[k * share : (k + 1) * share]
                if batch:

                    @pl.when(layer == k)
                    def _():
                        for event in batch:
                            event()

        grad_kv_low[:, :local] = grad_query[...].astype(BF16)

        def query_terms(in_ref, grad_ref, kv_ref, kv_out, query_out):
            kv_out[...] = kv_ref[...].astype(BF16)
            query_out[...] = contract(in_ref[...], grad_ref[:, :local], ((0,), (0,))).astype(BF16)

        pltpu.emit_pipeline(
            query_terms,
            grid=(blocks,),
            in_specs=[
                column_spec(group),
                whole_spec(group, 2 * local),
                pl.BlockSpec((block, 2 * local), lambda i: (i, 0)),
            ],
            out_specs=[
                pl.BlockSpec((block, 2 * local), lambda i: (i, 0)),
                pl.BlockSpec((block, local), lambda i: (i, 2)),
            ],
        )(in_all.at[0], grad_kv_low, kv_weight, terms.at[2], terms.at[2])
        attn_line.hop(1)

        def kv_line(layer):
            @pl.when((layer < z) & (z < count - 1))
            def _():
                kv_move(layer, kv_own).wait_recv()
                add_rows(kv_own.at[layer], kv_landing.at[layer], kv_sums.at[layer])
                kv_move(layer, kv_sums).start()

        def add_rows(left, right, out):
            def step(left_ref, right_ref, out_ref):
                out_ref[...] = (left_ref[...].astype(F32) + right_ref[...].astype(F32)).astype(BF16)

            pltpu.emit_pipeline(
                step,
                grid=(tiles,),
                in_specs=[rows_spec(2 * local)] * 2,
                out_specs=[rows_spec(2 * local)],
            )(left, right, out)

        home(0)
        for h in range(2, count):
            kv_line(h - 2)
            attn_line.hop(h)
            if h == 2:
                home(1)
        kv_line(count - 2)
        first_sum.drain()

        @pl.when(z < count - 1)
        def _():
            kv_move(z, kv_own).wait_recv()
            pltpu.sync_copy(kv_landing.at[z], kv)

        @pl.loop(0, tiles)
        def _(i):
            part = pl.ds(pl.multiple_of(i * tile, tile), tile)

            @pl.when(z < count - 1)
            def _():
                grad_kv[part, :] += kv[part, :].astype(F32)

            partial[part, :] = (
                contract(grad_kv[part, :].astype(BF16), qkv_w[:, : 2 * local], ((1,), (1,)))
                + contract(grad_query[part, :].astype(BF16), qkv_w[:, 2 * local :], ((1,), (1,)))
            ).astype(BF16)

        last_sum.start()
        last_sum.twins()
        attn_line.final(attn_grads.at[z, x])
        spread.first()
        last_sum.corners()
        last_sum.end(store_into(last_gather))
        last_gather.start()
        last_gather.middle()
        spread.hop(1)
        last_gather.corner()
        last_gather.end()

        def first_back(x_ref, grad_ref, resid_ref, out_ref):
            normed, inverse = normed_rows(x_ref[...].astype(F32))
            grad = grad_ref[...].astype(F32)
            scaled = grad * gain1[...]
            centre = jnp.mean(scaled, axis=1, keepdims=True)
            slope = jnp.mean(scaled * normed, axis=1, keepdims=True)
            gains[0:1, :] += jnp.sum(grad * normed, axis=0, keepdims=True)
            wide[...] = inverse * (scaled - centre - normed * slope)
            out_ref[...] = resid_ref[...] + wide[:, own_column]

        pltpu.emit_pipeline(
            first_back,
            grid=(group // thin,),
            in_specs=[thin_spec, thin_spec, rows_spec(width, thin)],
            out_specs=[rows_spec(width, thin)],
        )(x_all.at[0], full3, grad_resid, input_grad)

        def gain_copy(step):
            to = lax.rem(z + step, count)
            return pltpu.make_async_remote_copy(
                src_ref=gains,
                dst_ref=gains_landing.at[z],
                send_sem=gain_send.at[step],
                recv_sem=gain_recv.at[z],
                device_id={"z": to},
                device_id_type=MESH,
            )

        for step in range(1, count):
            gain_copy(step).start()
        for h in range(2, count):
            spread.hop(h)
        gains_landing[z] = gains[...]
        for step in range(1, count):
            source = lax.rem(z + step, count)
            pltpu.make_async_remote_copy(
                src_ref=gains,
                dst_ref=gains_landing.at[source],
                send_sem=gain_send.at[step],
                recv_sem=gain_recv.at[source],
                device_id={"z": source},
                device_id_type=MESH,
            ).wait_recv()
        for step in range(1, count):
            gain_copy(step).wait_send()
        gains[...] = jnp.sum(gains_landing[...], axis=0)
        pltpu.sync_copy(gains, gains_out)
        spread.end()

        @pl.loop(0, count)
        def _(layer):
            @pl.when(layer < z)
            def _():
                kv_move(layer, kv_own).wait_send()

    pl.run_scoped(
        attention,
        pltpu.VMEM((features, 3 * local), BF16),
        pltpu.VMEM((features, local), BF16),
        pltpu.VMEM((group, local), BF16),
        pltpu.VMEM((group, local), BF16),
        pltpu.VMEM((group, 2 * local), BF16),
        pltpu.VMEM((group, local), BF16),
        pltpu.VMEM((group, local), F32),
        pltpu.VMEM((group, 2 * local), F32),
        pltpu.VMEM((group, 2 * local), BF16),
        pltpu.VMEM((features, 2 * local), F32),
        pltpu.VMEM((heads, group, HD), F32),
        pltpu.VMEM((heads, 1, group), F32),
        pltpu.VMEM((heads, 1, group), F32),
        pltpu.VMEM((thin, features), F32),
        pltpu.VMEM((rows, width), BF16),
        pltpu.VMEM((rows, width), BF16),
    )
    for which in (0, 1):
        home_copy(which, True).wait_recv()
        home_copy(which).wait_send()
    for line in (down_line, up_line, attn_line):
        line.drain()
    out_sum.drain()
    last_sum.drain()
    first_gather.drain()
    last_gather.drain()


def back(count, *args):
    (x_all, in_all, kv_all, query, *_, w_out, gain1, gain2, start_row, key_place) = args
    down_all, w_query = args[9], args[11]
    _, group, features = x_all.shape
    rows = group // 2
    local = query.shape[1]
    heads = local // HD
    hidden = down_all.shape[1]
    width = features // 4
    chunk = features // count
    hbm, vmem = pl.BlockSpec(memory_space=pl.ANY), pl.BlockSpec(memory_space=pltpu.VMEM)

    def out(*shape, dtype=BF16):
        return jax.ShapeDtypeStruct(shape, dtype)

    dma = pltpu.SemaphoreType.DMA
    return pl.pallas_call(
        functools.partial(back_kernel, count),
        name="back",
        out_shape=(
            out(rows, width),
            out(group, width, dtype=F32),
            out(8, features, dtype=F32),
            out(2, 2, chunk // 2, hidden),
            out(count, 2, chunk, 4 * local),
            out(3, features, hidden),
            out(3, count + 1, chunk, hidden),
            out(3, count, chunk, hidden),
            out(2, chunk, hidden),
            out(group, features),
            out(group, width, dtype=F32),
            out(count, group, 2 * local),
            out(count, group, 2 * local),
            out(count, group, 2 * local),
        ),
        in_specs=[hbm] * 15 + [vmem] * 4,
        out_specs=[hbm] * 14,
        scratch_shapes=[
            pltpu.VMEM((group, features), BF16),
            pltpu.VMEM((group, features), BF16),
            pltpu.VMEM((group, features), BF16),
            pltpu.VMEM((group, features), BF16),
            *reduce_scratch(rows, width),
            *reduce_scratch(rows, width),
            *reduce_scratch(rows, width),
            pltpu.VMEM((8, features), F32),
            pltpu.VMEM((count, 8, features), F32),
            dma((8,)),
            dma((3, 10)),
            dma((3, 10)),
            dma((2, 9)),
            dma((2, 9)),
            dma((3, count)),
            dma((3, count + 1)),
            dma((2,)),
            dma((2,)),
            *[dma((count,))] * 9,
        ],
        compiler_params=pltpu.CompilerParams(
            collective_id=1, has_side_effects=True, vmem_limit_bytes=60 * 1024 * 1024
        ),
    )(*args)


def body(
    layer_input,
    clip_lengths,
    key_padding,
    norm1_gain,
    w_query,
    w_key,
    w_value,
    w_out,
    norm2_gain,
    w_up,
    w_down,
    out_grad,
):
    count = lax.axis_size("z")
    z, x = lax.axis_index("z"), lax.axis_index("x")
    rows = layer_input.shape[0]
    width = w_query.shape[0]
    local = w_query.shape[1] // 2
    hidden = w_up.shape[1] // 2
    clip_ends = jnp.cumsum(clip_lengths)
    position = jnp.arange(key_padding.shape[0], dtype=jnp.int32)
    starts = jnp.max(jnp.where(position[:, None] >= clip_ends, clip_ends, 0), axis=1)
    key_place = jnp.where(key_padding > 0, position, -1).reshape(count, 1, 2 * rows)
    own_starts = lax.dynamic_slice_in_dim(starts, z * 2 * rows, 2 * rows)
    gain1, gain2 = norm1_gain[None], norm2_gain[None]
    *kept, down_full, up_full = front(
        count, layer_input, out_grad, w_query, w_key, w_value, w_out, w_up, w_down,
        gain1, gain2, own_starts[:, None], key_place,
    )
    output, input_grad, gains, mlp_grads, attn_grads, *_ = back(
        count, *kept, down_full.reshape(width, hidden), up_full.reshape(width, hidden),
        w_query, w_key, w_value, w_out, gain1, gain2, own_starts[None], key_place,
    )

    def both_halves(first, size):
        part = attn_grads[..., first : first + size].astype(F32)
        return jnp.concatenate(
            [part[:, 0].reshape(width, size), part[:, 1].reshape(width, size)], axis=1
        )

    key_grad, value_grad, query_grad, out_grad_w = (
        both_halves(i * local, local) for i in range(4)
    )
    down_grad, up_grad = (
        jnp.concatenate([mlp_grads[i, 0], mlp_grads[i, 1]], axis=1).astype(F32) for i in range(2)
    )
    return (
        output,
        lax.dynamic_slice_in_dim(input_grad, x * rows, rows, 0),
        gains[0],
        query_grad,
        key_grad,
        value_grad,
        out_grad_w,
        gains[1],
        up_grad,
        down_grad,
    )


def solution(mesh):
    seq, head = mesh.shape["seq"], mesh.shape["head"]
    fine = Mesh(mesh.devices.reshape(seq // 2, 2, head // 2, 2), ("z", "x", "y", "core"))
    seq_axes, head_axes = ("z", "x"), ("y", "core")
    both, columns = P(seq_axes, head_axes), P(None, head_axes)
    return jax.shard_map(
        body,
        mesh=fine,
        in_specs=(both, P(), P(), P(), columns, columns, columns, columns, P(), both, both, both),
        out_specs=(both, both, P(), columns, columns, columns, columns, P(), both, both),
        check_vma=False,
    )
```

```python
import copy
import functools

import jax
import jax.numpy as jnp
from jax import lax
from jax.experimental import pallas as pl
from jax.experimental.pallas import tpu as pltpu
from jax.sharding import Mesh, PartitionSpec as P

HD = 128
NORM_EPS = 1e-05
BF16 = jnp.bfloat16
F32 = jnp.float32
LAYER = ("x", "y", "core")


MESH = pl.DeviceIdType.MESH
LOG2E = 1.4426950408889634


def remote(src, dst, sends, recvs, slot, **device):
    return pltpu.make_async_remote_copy(
        src_ref=src,
        dst_ref=dst,
        send_sem=sends.at[slot],
        recv_sem=recvs.at[slot],
        device_id=device,
        device_id_type=MESH,
    )


def pick(which, left, right):
    if isinstance(which, bool):
        return left if which else right
    return jnp.where(which, left, right)


def contract(left, right, dims):
    return lax.dot_general(left, right, (dims, ((), ())), preferred_element_type=F32)


class Place:
    def __init__(self, count):
        self.count = count
        self.z = lax.axis_index("z")
        self.x, self.y, self.c = lax.axis_index("x"), lax.axis_index("y"), lax.axis_index("core")
        self.ox, self.oy, self.oc = 1 - self.x, 1 - self.y, 1 - self.c

    def fixed(self, z):
        other = copy.copy(self)
        other.z = z
        return other

    def meet(self, whole_line=False):
        barrier = pltpu.get_barrier_semaphore()
        for device in ({"x": self.ox}, {"y": self.oy}, {"core": self.oc}):
            pl.semaphore_signal(barrier, inc=1, device_id=device, device_id_type=MESH)
        if whole_line:
            for step in range(1, self.count):
                pl.semaphore_signal(
                    barrier,
                    inc=1,
                    device_id={"z": lax.rem(self.z + step, self.count)},
                    device_id_type=MESH,
                )
            pl.semaphore_wait(barrier, 3 + self.count - 1)
            return
        above, below = self.z < self.count - 1, self.z > 0
        for there, step in ((above, 1), (below, -1)):

            @pl.when(there)
            def _():
                pl.semaphore_signal(
                    barrier, inc=1, device_id={"z": self.z + step}, device_id_type=MESH
                )

        pl.semaphore_wait(barrier, 3 + above.astype(jnp.int32) + below.astype(jnp.int32))


class Gather:
    def __init__(self, at, array, rows, width, sends, recvs, lead=()):
        self.at, self.array, self.sends, self.recvs, self.lead = at, array, sends, recvs, lead
        self.rows, self.width = rows, width

    def block(self, xi, yi, ci, first=0, size=None):
        size = self.rows if size is None else size
        return self.array.at[
            pl.ds(pl.multiple_of(xi * self.rows + first, size), size),
            pl.ds(pl.multiple_of((2 * yi + ci) * self.width, self.width), self.width),
        ]

    def copy(self, k, landing=False):
        at, half = self.at, self.rows // 2
        x, y, c, ox, oy, oc = at.x, at.y, at.c, at.ox, at.oy, at.oc
        place = {
            0: ((x, y, c), (ox, y, c), {"x": ox}),
            1: ((x, y, c), (x, oy, c), {"y": oy}),
            2: ((x, y, c), (x, y, oc), {"core": oc}),
            3: ((ox, y, c, 0, half), (ox, oy, c, 0, half), {"y": oy}),
            4: ((x, oy, c, half, half), (ox, oy, c, half, half), {"x": ox}),
            5: ((ox, y, c), (ox, y, oc), {"core": oc}),
            6: ((x, oy, c), (x, oy, oc), {"core": oc}),
            7: ((ox, oy, c, 0, half), (ox, oy, oc, 0, half), {"core": oc}),
            8: ((ox, oy, c, half, half), (ox, oy, oc, half, half), {"core": oc}),
        }
        source, lands, device = place[k]
        ref = self.block(*(lands if landing else source))
        return remote(ref, ref, self.sends, self.recvs, self.lead + (k,), **device)

    def start(self):
        for k in (0, 1, 2):
            self.copy(k).start()

    def middle(self):
        self.copy(0, True).wait_recv()
        self.copy(3).start()
        self.copy(5).start()
        self.copy(1, True).wait_recv()
        self.copy(4).start()
        self.copy(6).start()

    def corner(self):
        self.copy(3, True).wait_recv()
        self.copy(7).start()
        self.copy(4, True).wait_recv()
        self.copy(8).start()

    def end(self):
        for k in (2, 5, 6, 7, 8):
            self.copy(k, True).wait_recv()

    def drain(self):
        for k in range(9):
            self.copy(k).wait_send()


class Reduce:
    def __init__(self, at, array, rows, width, buffers, sends, recvs):
        self.at, self.array, self.sends, self.recvs = at, array, sends, recvs
        self.rows, self.width = rows, width
        self.twin, self.corner_x, self.corner_y, self.from_x, self.from_y = buffers

    def block(self, xi, yi, ci, first=0, size=None):
        return Gather.block(self, xi, yi, ci, first, size)

    def copy(self, k):
        at, half = self.at, self.rows // 2
        x, y, c, ox, oy, oc = at.x, at.y, at.c, at.ox, at.oy, at.oc
        low, high = pl.ds(0, half), pl.ds(half, half)
        place = {
            0: ((ox, oy, oc), self.twin.at[0], {"core": oc}),
            1: ((ox, y, oc), self.twin.at[1], {"core": oc}),
            2: ((x, oy, oc), self.twin.at[2], {"core": oc}),
            3: ((x, y, oc), self.twin.at[3], {"core": oc}),
            4: ((ox, oy, c, 0, half), self.corner_y, {"y": oy}),
            5: ((ox, oy, c, half, half), self.corner_x, {"x": ox}),
            6: ((ox, y, c, half, half), self.from_x.at[high], {"x": ox}),
            7: ((x, oy, c, 0, half), self.from_y.at[low], {"y": oy}),
            8: ((ox, y, c, 0, half), self.from_x.at[low], {"x": ox}),
            9: ((x, oy, c, half, half), self.from_y.at[high], {"y": oy}),
        }
        source, lands, device = place[k]
        return remote(self.block(*source), lands, self.sends, self.recvs, (k,), **device)

    def add(self, target, other):
        rows = target.shape[0]
        tile = min(rows, 128)

        @pl.loop(0, rows // tile)
        def _(i):
            part = pl.ds(pl.multiple_of(i * tile, tile), tile)
            target[part, :] = (target[part, :].astype(F32) + other[part, :].astype(F32)).astype(
                target.dtype
            )

    def start(self):
        for k in (0, 1, 2, 3):
            self.copy(k).start()

    def twins(self):
        at, half = self.at, self.rows // 2
        x, y, c, ox, oy = at.x, at.y, at.c, at.ox, at.oy
        self.copy(0).wait_recv()
        self.add(self.block(ox, oy, c), self.twin.at[0])
        self.copy(4).start()
        self.copy(5).start()
        self.copy(1).wait_recv()
        self.add(self.block(ox, y, c), self.twin.at[1])
        self.copy(6).start()
        self.copy(2).wait_recv()
        self.add(self.block(x, oy, c), self.twin.at[2])
        self.copy(7).start()
        self.copy(3).wait_recv()

    def corners(self):
        at, half = self.at, self.rows // 2
        self.copy(4).wait_recv()
        self.add(self.block(at.ox, at.y, at.c, 0, half), self.corner_y)
        self.copy(8).start()
        self.copy(5).wait_recv()
        self.add(self.block(at.x, at.oy, at.c, half, half), self.corner_x)
        self.copy(9).start()

    def end(self, store):
        for k in (6, 7, 8, 9):
            self.copy(k).wait_recv()
        own = self.block(self.at.x, self.at.y, self.at.c)
        tile = min(self.rows, 128)

        @pl.loop(0, self.rows // tile)
        def _(i):
            part = pl.ds(pl.multiple_of(i * tile, tile), tile)
            store(
                part,
                own[part, :].astype(F32)
                + self.twin[3, part, :].astype(F32)
                + self.from_x[part, :].astype(F32)
                + self.from_y[part, :].astype(F32),
            )

    def drain(self):
        for k in range(10):
            self.copy(k).wait_send()


def reduce_scratch(rows, width):
    return [
        pltpu.VMEM((4, rows, width), BF16),
        pltpu.VMEM((rows // 2, width), BF16),
        pltpu.VMEM((rows // 2, width), BF16),
        pltpu.VMEM((rows, width), BF16),
        pltpu.VMEM((rows, width), BF16),
    ]


def normed_rows(rows):
    mean = jnp.mean(rows, axis=1, keepdims=True)
    centred = rows - mean
    inverse = lax.rsqrt(jnp.mean(centred * centred, axis=1, keepdims=True) + NORM_EPS)
    return centred * inverse, inverse


class Weights:
    def __init__(self, at, which, weight, whole, sems):
        self.at, self.which, self.weight, self.whole = at, which, weight, whole
        self.local, self.xs, self.xr, self.us, self.ds, self.rs = sems
        self.half = weight.shape[1] // 2

    def columns(self, which):
        return self.weight.at[:, pl.ds(pl.multiple_of(which * self.half, self.half), self.half)]

    def own(self, stage, out):
        at = self.at
        source, target = (stage, self.whole.at[at.z, at.x]) if out else (self.columns(at.x), stage)
        return pltpu.make_async_copy(source, target, self.local.at[self.which])

    def swap(self, landing=False):
        at = self.at
        dst = self.whole.at[at.z, at.ox] if landing else self.whole.at[at.z, at.x]
        return remote(self.columns(at.ox), dst, self.xs, self.xr, (self.which,), x=at.ox)

    def move(self, layer, part, step):
        ref = self.whole.at[layer, part]
        sends = self.us if step > 0 else self.ds
        return pltpu.make_async_remote_copy(
            src_ref=ref,
            dst_ref=ref,
            send_sem=sends.at[self.which, layer, part],
            recv_sem=self.rs.at[self.which, layer, part],
            device_id={"z": self.at.z + step},
            device_id_type=MESH,
        )

    def first(self, mine, steps=(1, -1)):
        at = self.at
        part = at.x if mine else at.ox
        for step, there in ((1, at.z < at.count - 1), (-1, at.z > 0)):
            if step in steps:

                @pl.when(there)
                def _():
                    self.move(at.z, part, step).start()

    def hop(self, distance, mine):
        at = self.at
        part = at.x if mine else at.ox

        @pl.when(at.z >= distance)
        def _():
            self.move(at.z - distance, part, 1).wait_recv()

            @pl.when(at.z < at.count - 1)
            def _():
                self.move(at.z - distance, part, 1).start()

        @pl.when(at.z + distance < at.count)
        def _():
            self.move(at.z + distance, part, -1).wait_recv()

            @pl.when(at.z > 0)
            def _():
                self.move(at.z + distance, part, -1).start()

    def drain(self):
        at = self.at
        self.swap().wait_send()
        for part in (0, 1):

            @pl.loop(0, at.count)
            def _(layer):
                @pl.when((layer <= at.z) & (at.z < at.count - 1))
                def _():
                    self.move(layer, part, 1).wait_send()

                @pl.when((layer >= at.z) & (at.z > 0))
                def _():
                    self.move(layer, part, -1).wait_send()


def front_kernel(
    count,
    xs,
    og,
    w_query,
    w_key,
    w_value,
    w_out,
    w_up,
    w_down,
    gain1,
    gain2,
    start_of,
    key_place,
    x_all,
    in_all,
    kv_all,
    query_out,
    attended_out,
    log_out,
    branch_out,
    mlp_out,
    og_all,
    down_all,
    up_all,
    qkv_w,
    out_w,
    query,
    kv,
    high,
    total,
    sums,
    attended,
    partial,
    branch,
    twin,
    corner_x,
    corner_y,
    from_x,
    from_y,
    load_sem,
    gather_send,
    gather_recv,
    line_send,
    line_recv,
    w_local,
    w_xs,
    w_xr,
    w_us,
    w_ds,
    w_rs,
    reduce_send,
    reduce_recv,
):
    at = Place(count)
    z, x, y, c = at.z, at.x, at.y, at.c
    rows, width = xs.shape
    group = 2 * rows
    local = w_query.shape[1] // 2
    heads = local // HD
    features = gain1.shape[1]
    tile = 256 if group % 256 == 0 else group
    tiles = group // tile

    def columns_of(weight):
        return weight.at[:, pl.ds(pl.multiple_of(x * local, local), local)]

    loads = [
        pltpu.make_async_copy(
            columns_of(w), qkv_w.at[:, pl.ds(i * local, local)], load_sem.at[i]
        )
        for i, w in enumerate((w_key, w_value, w_query))
    ]
    loads.append(pltpu.make_async_copy(columns_of(w_out), out_w, load_sem.at[3]))

    def gather_of(d):
        return Gather(at, x_all.at[d], rows, width, gather_send, gather_recv, (d,))

    og_gather = Gather(at, og_all, rows, width, gather_send, gather_recv, (count,))
    branch_gather = Gather(at, branch, rows, width, gather_send, gather_recv, (count + 1,))

    def own_block(d):
        return gather_of(d).block(x, y, c)

    def line_copy(d):
        return remote(own_block(d), own_block(d + 1), line_send, line_recv, (d,), z=z + 1)

    weight_sems = (w_local, w_xs, w_xr, w_us, w_ds, w_rs)
    down = Weights(at, 0, w_down, down_all, weight_sems)
    up = Weights(at, 1, w_up, up_all, weight_sems)

    w_rows, hidden = w_up.shape[0], w_up.shape[1] // 2
    places = [
        partial.at[pl.ds(0, rows), pl.ds(i * width, width)] for i in range(2)
    ] + [partial.at[pl.ds(rows, w_rows), pl.ds(i * hidden, hidden)] for i in range(2)]
    into = [
        pltpu.make_async_copy(xs, places[0], load_sem.at[4]),
        down.own(places[2], False),
        up.own(places[3], False),
        pltpu.make_async_copy(og, places[1], load_sem.at[5]),
    ]
    onto = [
        pltpu.make_async_copy(places[0], own_block(0), load_sem.at[4]),
        down.own(places[2], True),
        up.own(places[3], True),
        pltpu.make_async_copy(places[1], og_gather.block(x, y, c), load_sem.at[5]),
    ]
    for copy in into + loads:
        copy.start()
    for first, second in zip(into, onto):
        first.wait()
        second.start()
    at.meet()
    onto[0].wait()

    @pl.when(z < count - 1)
    def _():
        line_copy(0).start()

    gather_of(0).start()
    onto[1].wait()
    down.first(True)
    onto[2].wait()
    up.first(True, (-1,))
    onto[3].wait()
    gather_of(0).middle()
    for load in loads:
        load.wait()

    def project(d, with_query):
        size = qkv_w.shape[1] if with_query else 2 * local

        def step(x_ref, in_ref, kv_ref, *maybe_query):
            normed, _ = normed_rows(x_ref[...].astype(F32))
            rounded = (normed * gain1[...]).astype(BF16)
            in_ref[...] = rounded
            product = jnp.dot(rounded, qkv_w[:, :size], preferred_element_type=F32)
            kv_ref[...] = product[:, : 2 * local].astype(BF16)
            if with_query:
                maybe_query[0][...] = product[:, 2 * local :].astype(BF16)

        def rows_of(size):
            return pl.BlockSpec((tile, size), lambda i: (i, 0))

        outs = [rows_of(features), rows_of(2 * local)] + ([rows_of(local)] if with_query else [])
        refs = [in_all.at[d], kv_all.at[d]] + ([query_out] if with_query else [])
        pltpu.emit_pipeline(step, grid=(tiles,), in_specs=[rows_of(features)], out_specs=outs)(
            x_all.at[d], *refs
        )

    def attend(d, diagonal):
        keys = key_place[z - d]

        @pl.loop(0, tiles)
        def _(i):
            part = pl.ds(pl.multiple_of(i * tile, tile), tile)
            allowed = keys >= start_of[part, :]
            if diagonal:
                query_at = lax.broadcasted_iota(jnp.int32, (tile, group), 0) + i * tile
                key_at = lax.broadcasted_iota(jnp.int32, (tile, group), 1)
                allowed = (allowed & (key_at <= query_at)) | (key_at == query_at)
            for h in range(heads):
                span = slice(h * HD, (h + 1) * HD)
                scores = contract(query[part, span], kv[:, span], ((1,), (1,)))
                scores = jnp.where(allowed, scores * (HD**-0.5 * LOG2E), -1e30)
                top = jnp.max(scores, axis=1, keepdims=True)
                if not diagonal:
                    old = high[h, part, :1]
                    top = jnp.maximum(old, top)
                    fade = jnp.exp2(old - top)
                weights = jnp.exp2(scores - top)
                mass = jnp.sum(weights, axis=1, keepdims=True)
                value = jnp.dot(
                    weights.astype(BF16),
                    kv[:, local + h * HD : local + (h + 1) * HD],
                    preferred_element_type=F32,
                )
                if not diagonal:
                    mass = mass + total[h, part, :1] * fade
                    value = value + sums[part, span] * fade
                high[h, part, :] = jnp.broadcast_to(top, (tile, HD))
                total[h, part, :] = jnp.broadcast_to(mass, (tile, HD))
                sums[part, span] = value

    def fetch(d, diagonal):
        pltpu.sync_copy(kv_all.at[d], kv)
        if diagonal:
            pltpu.sync_copy(query_out, query)

    def bring(d):
        @pl.when(z >= d)
        def _():
            remote(own_block(d - 1), own_block(d), line_send, line_recv, (d - 1,), z=z).wait_recv()

            @pl.when((d < count - 1) & (z < count - 1))
            def _():
                line_copy(d).start()

            gather_of(d).start()

    def within(d, *names):
        @pl.when(z >= d)
        def _():
            for name in names:
                getattr(gather_of(d), name)()

    def other_rows(weight):
        weight.swap(True).wait_recv()
        weight.first(False)

    def hop_of(weight, distance, mine):
        return functools.partial(weight.hop, distance, mine)

    events = [
        hop_of(down, 1, True),
        hop_of(up, 1, True),
        functools.partial(other_rows, down),
        hop_of(down, 1, False),
        functools.partial(other_rows, up),
        hop_of(up, 1, False),
    ]
    for distance in range(2, count):
        for mine in (True, False):
            events += [hop_of(down, distance, mine), hop_of(up, distance, mine)]

    def advance(many=1):
        for _ in range(min(many, len(events))):
            events.pop(0)()

    bring(1)
    up.first(True, (1,))
    gather_of(0).corner()
    gather_of(0).end()
    project(0, True)
    within(1, "middle")
    down.swap().start()
    fetch(0, True)
    attend(0, True)

    @pl.loop(2, count)
    def _(d):
        bring(d)

        for k in (2, 3):

            @pl.when(d == k)
            def _():
                events[2 * k - 4]()

        within(d - 1, "corner", "end")

        @pl.when(z >= d - 1)
        def _():
            project(d - 1, False)

        within(d, "middle")

        for k in (2, 3):

            @pl.when(d == k)
            def _():
                if k == 2:
                    up.swap().start()
                events[2 * k - 3]()

        @pl.when(z >= d - 1)
        def _():
            fetch(d - 1, False)
            attend(d - 1, False)

    if count < 3:
        up.swap().start()
    del events[: 2 * min(count - 2, 2)]
    advance()
    og_gather.start()
    within(count - 1, "corner", "end")

    @pl.when(z >= count - 1)
    def _():
        project(count - 1, False)

    advance()
    og_gather.middle()

    @pl.when(z >= count - 1)
    def _():
        fetch(count - 1, False)
        attend(count - 1, False)

    advance(2)
    og_gather.corner()

    @pl.loop(0, tiles)
    def _(i):
        part = pl.ds(pl.multiple_of(i * tile, tile), tile)
        for h in range(heads):
            span = slice(h * HD, (h + 1) * HD)
            mass = total[h, part, :]
            attended[part, span] = (sums[part, span] / mass).astype(BF16)
            high[h, part, :] = high[h, part, :] + jnp.log2(mass)
        partial[part, :] = contract(attended[part, :], out_w[...], ((1,), (1,))).astype(BF16)

    outs = [
        pltpu.make_async_copy(attended, attended_out, load_sem.at[6]),
        pltpu.make_async_copy(high, log_out, load_sem.at[7]),
    ]
    for out in outs:
        out.start()
    reduce = Reduce(
        at, partial, rows, width, (twin, corner_x, corner_y, from_x, from_y), reduce_send, reduce_recv
    )
    reduce.start()
    og_gather.end()
    reduce.twins()
    advance()
    reduce.corners()
    advance()
    own_branch = branch_gather.block(x, y, c)

    def store(part, value):
        own_branch[part, :] = value.astype(BF16)

    reduce.end(store)
    branch_gather.start()
    advance()
    branch_gather.middle()
    advance()
    branch_gather.corner()
    branch_gather.end()
    pltpu.sync_copy(branch, branch_out)

    def second_norm(x_ref, branch_ref, mlp_ref):
        normed, _ = normed_rows(x_ref[...].astype(F32) + branch_ref[...].astype(F32))
        mlp_ref[...] = (normed * gain2[...]).astype(BF16)

    spec = pl.BlockSpec((tile, features), lambda i: (i, 0))
    pltpu.emit_pipeline(second_norm, grid=(tiles,), in_specs=[spec, spec], out_specs=[spec])(
        x_all.at[0], branch_out, mlp_out
    )
    advance(len(events))

    for out in outs:
        out.wait()
    down.drain()
    up.drain()
    reduce.drain()
    branch_gather.drain()
    og_gather.drain()

    @pl.loop(0, count)
    def _(d):
        within(d, "drain")

        @pl.when((z >= d) & (d < count - 1) & (z < count - 1))
        def _():
            line_copy(d).wait_send()


def front(count, xs, og, w_query, w_key, w_value, w_out, w_up, w_down, gain1, gain2, start_of, key_place):
    rows, width = xs.shape
    group, features = 2 * rows, gain1.shape[1]
    local = w_query.shape[1] // 2
    heads = local // HD
    hidden = w_up.shape[1] // 2
    w_rows = w_up.shape[0]
    hbm, vmem = pl.BlockSpec(memory_space=pl.ANY), pl.BlockSpec(memory_space=pltpu.VMEM)

    def out(*shape, dtype=BF16):
        return jax.ShapeDtypeStruct(shape, dtype)

    dma = pltpu.SemaphoreType.DMA
    return pl.pallas_call(
        functools.partial(front_kernel, count),
        name="front",
        out_shape=(
            out(count, group, features),
            out(count, group, features),
            out(count, group, 2 * local),
            out(group, local),
            out(group, local),
            out(heads, group, HD, dtype=F32),
            out(group, features),
            out(group, features),
            out(group, features),
            out(count, 2, w_rows, hidden),
            out(count, 2, w_rows, hidden),
        ),
        in_specs=[hbm] * 8 + [vmem] * 4,
        out_specs=[hbm] * 11,
        scratch_shapes=[
            pltpu.VMEM((features, 3 * local), BF16),
            pltpu.VMEM((features, local), BF16),
            pltpu.VMEM((group, local), BF16),
            pltpu.VMEM((group, 2 * local), BF16),
            pltpu.VMEM((heads, group, HD), F32),
            pltpu.VMEM((heads, group, HD), F32),
            pltpu.VMEM((group, local), F32),
            pltpu.VMEM((group, local), BF16),
            pltpu.VMEM((group, features), BF16),
            pltpu.VMEM((group, features), BF16),
            *reduce_scratch(rows, width),
            dma((8,)),
            dma((count + 2, 9)),
            dma((count + 2, 9)),
            dma((count,)),
            dma((count,)),
            dma((2,)),
            dma((2,)),
            dma((2,)),
            dma((2, count, 2)),
            dma((2, count, 2)),
            dma((2, count, 2)),
            dma((10,)),
            dma((10,)),
        ],
        compiler_params=pltpu.CompilerParams(
            collective_id=0, has_side_effects=True, vmem_limit_bytes=56 * 1024 * 1024
        ),
    )(xs, og, w_query, w_key, w_value, w_out, w_up, w_down, gain1, gain2, start_of, key_place)


class LineSum:
    def __init__(self, at, which, terms, landing, sums, sends, recvs, eager=False):
        self.at, self.which, self.eager = at, which, eager
        self.terms, self.landing, self.sums = terms, landing, sums
        self.sends, self.recvs = sends, recvs
        self.rows = sums.shape[1]

    def chunk(self, c):
        return self.terms.at[pl.ds(pl.multiple_of(c * self.rows, self.rows), self.rows)]

    def move(self, source, c, slot, step):
        return pltpu.make_async_remote_copy(
            src_ref=source,
            dst_ref=self.landing.at[slot],
            send_sem=self.sends.at[self.which, c],
            recv_sem=self.recvs.at[self.which, slot],
            device_id={"z": self.at.z + step},
            device_id_type=MESH,
        )

    def landed(self, slot):
        self.move(self.landing.at[slot], 0, slot, 0).wait_recv()

    def total(self, refs, out):
        tile = min(256, self.rows)

        def step(*tiles):
            value = tiles[0][...].astype(F32)
            for other in tiles[1:-1]:
                value = value + other[...].astype(F32)
            tiles[-1][...] = value.astype(BF16)

        spec = pl.BlockSpec((tile, self.sums.shape[2]), lambda i: (i, 0))
        pltpu.emit_pipeline(
            step, grid=(self.rows // tile,), in_specs=[spec] * len(refs), out_specs=[spec]
        )(*refs, out)

    def begin(self, h):
        n, z = self.at.count, self.at.z
        for step, end, c, slot in ((1, 0, n - h, n - h), (-1, n - 1, h - 1, None)):
            if slot is None:
                slot = n if c == n - 2 else c

            @pl.when(z == end)
            def _():
                self.move(self.chunk(c), c, slot, step).start()

    def hop(self, h, steps=(1, -1)):
        at, n, z = self.at, self.at.count, self.at.z
        if h == 1:
            for each in range(1, n if self.eager else 2):
                self.begin(each)
        for step, c, there in (
            (1, n - h + z, (z <= h - 1) & (z < n - 1) & (z > 0)),
            (-1, z - n + h, (z >= n - h) & (z > 0) & (z < n - 1)),
        ):
            if step not in steps:
                continue
            slot = c if step > 0 else pick(c == z - 1, n, c)

            @pl.when(there)
            def _():
                self.landed(c)
                self.total([self.chunk(c), self.landing.at[c]], self.sums.at[c])
                self.move(self.sums.at[c], c, slot, step).start()

    def final(self, out):
        n, z = self.at.count, self.at.z
        below, above = self.landing.at[z], self.landing.at[n]

        @pl.when(z > 0)
        def _():
            self.landed(z)

        @pl.when(z < n - 1)
        def _():
            self.landed(n)

        @pl.when(z == 0)
        def _():
            self.total([self.chunk(z), above], out)

        @pl.when(z == n - 1)
        def _():
            self.total([self.chunk(z), below], out)

        @pl.when((z > 0) & (z < n - 1))
        def _():
            self.total([self.chunk(z), below, above], out)

    def drain(self):
        z = self.at.z

        @pl.loop(0, self.at.count)
        def _(c):
            @pl.when(c != z)
            def _():
                self.move(self.chunk(c), c, 0, 0).wait_send()


class Spread:
    def __init__(self, at, which, whole, ups, downs, lines, sides, sidesr):
        self.at, self.which, self.whole = at, which, whole
        self.ups, self.downs, self.lines, self.sides, self.sidesr = ups, downs, lines, sides, sidesr

    def move(self, layer, step):
        ref = self.whole.at[layer, self.at.x]
        sends = self.ups if step > 0 else self.downs
        return remote(ref, ref, sends, self.lines, (self.which, layer), z=self.at.z + step)

    def side(self, layer, part):
        ref = self.whole.at[layer, part]
        return remote(ref, ref, self.sides, self.sidesr, (self.which, layer), x=self.at.ox)

    def first(self):
        at = self.at

        @pl.when(at.z < at.count - 1)
        def _():
            self.move(at.z, 1).start()

        @pl.when(at.z > 0)
        def _():
            self.move(at.z, -1).start()

        self.side(at.z, at.x).start()

    def hop(self, distance, step):
        at = self.at
        layer = at.z - step * distance

        @pl.when((layer >= 0) & (layer < at.count))
        def _():
            self.move(layer, step).wait_recv()

            @pl.when((at.z + step >= 0) & (at.z + step < at.count))
            def _():
                self.move(layer, step).start()

            self.side(layer, at.x).start()

    def end(self):
        at = self.at

        @pl.loop(0, at.count)
        def _(layer):
            self.side(layer, at.ox).wait_recv()
            self.side(layer, at.x).wait_send()

            @pl.when((layer <= at.z) & (at.z < at.count - 1))
            def _():
                self.move(layer, 1).wait_send()

            @pl.when((layer >= at.z) & (at.z > 0))
            def _():
                self.move(layer, -1).wait_send()


ORDERS = {
    (4, 0): (
        "b2", "b3", "twins", "corners", "home0", "keep", "home1", "f0", "D01", "D02", "own",
        "f1", "middle", "D11", "D12", "f2", "D21", "D22", "f3", "D31", "D32", "D03", "D13",
        "D23", "D33", "rows",
    ),
    (4, 1): (
        "home0", "end", "twins", "u02", "home1", "u03", "corners", "u12", "u13", "d03", "f0",
        "u22", "keep", "D01", "u23", "s0", "u32", "u33", "own", "d13", "U01", "f1", "middle",
        "D11", "U11", "d23", "f2", "D21", "d33", "U21", "f3", "D31", "D02", "U31", "D12",
        "D22", "D32", "rows",
    ),
    (4, 2): (
        "home0", "d02", "home1", "d03", "u03", "f0", "end", "twins", "s0", "u13", "s1", "d12",
        "U01", "d13", "u23", "f1", "corners", "d22", "u33", "d23", "f2", "d32", "U02", "keep",
        "d33", "U11", "f3", "U12", "own", "U21", "D01", "D11", "D21", "middle", "U31", "D31",
        "U22", "U32", "rows",
    ),
    (4, 3): (
        "b2", "b3", "home0", "home1", "end", "twins", "f0", "U01", "f1", "U02", "corners",
        "f2", "U11", "f3", "U21", "keep", "own", "U03", "U12", "U31", "U13", "middle", "U22",
        "U32", "U23", "rows", "U33",
    ),
}


def back_kernel(
    count,
    x_all,
    in_all,
    kv_all,
    query_in,
    attended_in,
    log_in,
    branch_in,
    mlp_in,
    og_all,
    down_all,
    up_all,
    w_query,
    w_key,
    w_value,
    w_out,
    gain1,
    gain2,
    start_row,
    key_place,
    output,
    input_grad,
    gains_out,
    mlp_grads,
    out_grads,
    query_grads,
    key_grads,
    value_grads,
    down_terms,
    up_terms,
    out_terms,
    query_terms,
    key_terms,
    value_terms,
    down_landing,
    up_landing,
    out_landing,
    query_landing,
    key_landing,
    value_landing,
    down_sums,
    up_sums,
    out_sums,
    query_sums,
    key_sums,
    value_sums,
    mine,
    grad_branch,
    grad_resid,
    share_own,
    share_landing,
    share_sums,
    partials,
    full1,
    full3,
    twin,
    corner_x,
    corner_y,
    from_x,
    from_y,
    gains,
    gains_landing,
    load_sem,
    reduce_send,
    reduce_recv,
    gather_send,
    gather_recv,
    sum_send,
    sum_recv,
    home_send,
    home_recv,
    spread_up,
    spread_down,
    spread_line,
    spread_side,
    spread_side_recv,
    share_send,
    share_recv,
    gain_send,
    gain_recv,
):
    at = Place(count)
    z, x, y, c = at.z, at.x, at.y, at.c
    group, features = mlp_in.shape
    rows = group // 2
    width = output.shape[1]
    local = w_query.shape[1] // 2
    heads = local // HD
    hidden = down_all.shape[1]
    tile = min(256, group)
    tiles = group // tile
    thin = min(128, group)
    chunk = features // count
    block = min(512, features)
    blocks = features // block
    own_column = pl.ds(pl.multiple_of((2 * y + c) * width, width), width)

    def columns_of(weight):
        return weight.at[:, pl.ds(pl.multiple_of(x * local, local), local)]

    def rows_spec(size, many=None):
        return pl.BlockSpec((many or tile, size), lambda i: (i, 0))

    def column_spec(tall):
        return pl.BlockSpec((tall, block), lambda i: (0, i))

    def whole_spec(*shape):
        return pl.BlockSpec(shape, lambda i: (0,) * len(shape))

    def round_of(r):
        p = r % 2 if isinstance(r, int) else lax.rem(r, 2)
        third = r % 3 if isinstance(r, int) else lax.rem(r, 3)
        buffers = (twin.at[third],) + tuple(
            b.at[p] for b in (corner_x, corner_y, from_x, from_y)
        )
        return Reduce(
            at, partials.at[p], rows, width, buffers, reduce_send.at[r], reduce_recv.at[r]
        )

    def gather_of(array, k):
        return Gather(at, array, rows, width, gather_send, gather_recv, (k,))

    first_sum, out_sum = round_of(0), round_of(1)
    first_gather, last_gather = gather_of(full1, 0), gather_of(full3, 1)
    attn_grads = (out_grads, query_grads, key_grads, value_grads)

    def lines_at(at):
        arrays = (
            (down_terms, down_landing, down_sums),
            (up_terms, up_landing, up_sums),
            (out_terms, out_landing, out_sums),
            (query_terms, query_landing, query_sums),
            (key_terms, key_landing, key_sums),
            (value_terms, value_landing, value_sums),
        )
        return [
            LineSum(at, k, *three, sum_send, sum_recv, k > 1) for k, three in enumerate(arrays)
        ]

    def spreads_at(at):
        sems = (spread_up, spread_down, spread_line, spread_side, spread_side_recv)
        return [Spread(at, k, whole, *sems) for k, whole in enumerate(attn_grads)]

    down_line, up_line, *attn_lines = lines_at(at)
    spreads = spreads_at(at)

    def weight_terms(terms, left, right, first, many):
        size = terms.shape[1]

        def at_chunk(i):
            return lax.rem(first + i, count)

        def step(left_ref, right_ref, out_ref):
            out_ref[...] = contract(left_ref[...], right_ref[...], ((0,), (0,))).astype(BF16)

        pltpu.emit_pipeline(
            step,
            grid=(many,),
            in_specs=[
                pl.BlockSpec((group, chunk), lambda i: (0, at_chunk(i))),
                whole_spec(group, size),
            ],
            out_specs=[pl.BlockSpec((chunk, size), lambda i: (at_chunk(i), 0))],
        )(left, right, terms)

    def home(which, line):
        line.final(mine.at[which])
        half = mine.shape[1] // 2
        home_copy(which).start()

        def step(in_ref, out_ref):
            out_ref[...] = in_ref[...]

        spec = pl.BlockSpec((half, hidden), lambda i: (i, 0))
        pltpu.emit_pipeline(step, grid=(1,), in_specs=[spec], out_specs=[spec])(
            mine.at[which, pl.ds(pl.multiple_of(x * half, half), half)], mlp_grads.at[which, x]
        )

    def home_copy(which, landing_part=False):
        half = mine.shape[1] // 2
        return remote(
            mine.at[which, pl.ds(pl.multiple_of(at.ox * half, half), half)],
            mlp_grads.at[which, at.ox if landing_part else x],
            home_send,
            home_recv,
            (which,),
            x=at.ox,
        )

    def store_into(gather):
        def store(part, value):
            gather.block(x, y, c)[part, :] = value.astype(BF16)

        return store

    def feed_forward(active, grad_up, w_down, w_up):
        loads = [
            pltpu.make_async_copy(up_all, w_up, load_sem.at[0]),
            pltpu.make_async_copy(down_all, w_down, load_sem.at[1]),
        ]
        for load in loads:
            load.start()
        at.meet(whole_line=True)
        for load in loads:
            load.wait()

        def step(mlp_ref, og_ref, active_ref, grad_ref):
            up = jnp.dot(mlp_ref[...], w_up[...], preferred_element_type=F32)
            grad = jnp.dot(og_ref[...], w_down[...], preferred_element_type=F32)
            square = up * up
            root = 0.7978845608028654
            bend = jnp.tanh(up * (root + (root * 0.044715) * square))
            half = 0.5 * (1.0 + bend)
            slope = half + 0.5 * up * (1.0 - bend * bend) * (root + (3.0 * root * 0.044715) * square)
            active_ref[...] = (up * half).astype(BF16)
            grad_ref[...] = (grad * slope).astype(BF16)

        pltpu.emit_pipeline(
            step,
            grid=(tiles,),
            in_specs=[rows_spec(features)] * 2,
            out_specs=[rows_spec(hidden)] * 2,
        )(mlp_in, og_all, active, grad_up)
        first = jnp.where(z == 0, count - 1, 0)
        weight_terms(down_terms, og_all, active, first, 1)
        down_line.hop(1)
        weight_terms(up_terms, mlp_in, grad_up, first, 1)
        up_line.hop(1)

        def back_through(target, source, weight):
            @pl.loop(0, tiles)
            def _(i):
                part = pl.ds(pl.multiple_of(i * tile, tile), tile)
                target[part, :] = contract(source[part, :], weight[...], ((1,), (1,))).astype(BF16)

        back_through(partials.at[0], grad_up, w_up)
        first_sum.start()
        weight_terms(down_terms, og_all, active, first + 1, count - 1)
        first_sum.twins()
        weight_terms(up_terms, mlp_in, grad_up, first + 1, count - 1)
        for h in range(2, count):
            down_line.begin(h)
            up_line.begin(h)
        first_sum.corners()
        back_through(partials.at[1], active, w_down)
        first_sum.end(store_into(first_gather))
        first_gather.start()
        down_line.hop(2)
        out_sum.start()
        first_gather.middle()
        first_gather.corner()
        out_sum.twins()
        first_gather.end()

    pl.run_scoped(
        feed_forward,
        pltpu.VMEM((group, hidden), BF16),
        pltpu.VMEM((group, hidden), BF16),
        pltpu.VMEM((features, hidden), BF16),
        pltpu.VMEM((features, hidden), BF16),
    )

    def attention(
        qkv_w, out_w, query, attended, kv, grad_att, grad_query, grad_kv, grad_kv_low, kv_weight,
        logs, log_row, delta_row, wide, resid_x, resid_branch, share,
    ):
        loads = [
            pltpu.make_async_copy(
                columns_of(w), qkv_w.at[:, pl.ds(i * local, local)], load_sem.at[i]
            )
            for i, w in enumerate((w_key, w_value, w_query))
        ]
        loads += [
            pltpu.make_async_copy(columns_of(w_out), out_w, load_sem.at[3]),
            pltpu.make_async_copy(query_in, query, load_sem.at[4]),
            pltpu.make_async_copy(attended_in, attended, load_sem.at[5]),
            pltpu.make_async_copy(log_in, logs, load_sem.at[6]),
        ]
        for load in loads:
            load.start()
        for load in loads:
            load.wait()
        gains[...] = jnp.zeros_like(gains)

        def second_back(x_ref, branch_ref, og_ref, grad_ref, low_ref, resid_ref, att_ref):
            normed, inverse = normed_rows(x_ref[...].astype(F32) + branch_ref[...].astype(F32))
            grad = grad_ref[...].astype(F32)
            scaled = grad * gain2[...]
            centre = jnp.mean(scaled, axis=1, keepdims=True)
            slope = jnp.mean(scaled * normed, axis=1, keepdims=True)
            gains[1:2, :] += jnp.sum(grad * normed, axis=0, keepdims=True)
            total = og_ref[...].astype(F32) + inverse * (scaled - centre - normed * slope)
            wide[...] = total
            low = total.astype(BF16)
            low_ref[...] = low
            resid_ref[...] = wide[:, own_column]
            att_ref[...] = jnp.dot(low, out_w[...], preferred_element_type=F32).astype(BF16)

        up_line.hop(2)
        thin_spec = rows_spec(features, thin)
        pltpu.emit_pipeline(
            second_back,
            grid=(group // thin,),
            in_specs=[thin_spec] * 4,
            out_specs=[thin_spec, rows_spec(width, thin), rows_spec(local, thin)],
        )(x_all.at[0], branch_in, og_all, full1, grad_branch, grad_resid, grad_att)
        out_sum.corners()
        weight_terms(out_terms, grad_branch, attended, 0, count)
        for h in range(heads):
            span = slice(h * HD, (h + 1) * HD)
            log_row[h] = jnp.transpose(logs[h])[:1]
            product = grad_att[:, span].astype(F32) * attended[:, span].astype(F32)
            delta_row[h] = jnp.sum(jnp.transpose(product), axis=0, keepdims=True)
        grad_query[...] = jnp.zeros_like(grad_query)
        kv_weight[...] = jnp.zeros_like(kv_weight)

        def attend_back(layer, diagonal, early):
            if early:
                pltpu.sync_copy(kv_all.at[z - layer], kv)
                grad_kv[...] = jnp.zeros_like(grad_kv)
            keys = jnp.transpose(jnp.broadcast_to(key_place[layer], (HD, group)))[:, :1]
            middle = tiles // 2

            @pl.loop(0 if early else middle, middle if early else tiles)
            def _(i):
                part = pl.ds(pl.multiple_of(i * tile, tile), tile)
                allowed = keys >= start_row[:, part]
                if diagonal:
                    query_at = lax.broadcasted_iota(jnp.int32, (group, tile), 1) + i * tile
                    key_at = lax.broadcasted_iota(jnp.int32, (group, tile), 0)
                    allowed = (allowed & (key_at <= query_at)) | (key_at == query_at)
                for h in range(heads):
                    span = slice(h * HD, (h + 1) * HD)
                    value_span = slice(local + h * HD, local + (h + 1) * HD)
                    key, value = kv[:, span], kv[:, value_span]
                    asked, grad = query[part, span], grad_att[part, span]
                    scores = contract(key, asked, ((1,), (1,))) * (HD**-0.5 * LOG2E)
                    probs = jnp.exp2(jnp.where(allowed, scores, -1e30) - log_row[h, :, part])
                    grad_probs = contract(value, grad, ((1,), (1,)))
                    grad_scores = (
                        probs * (grad_probs - delta_row[h, :, part]) * HD**-0.5
                    ).astype(BF16)
                    grad_kv[:, value_span] += jnp.dot(
                        probs.astype(BF16), grad, preferred_element_type=F32
                    )
                    grad_kv[:, span] += jnp.dot(grad_scores, asked, preferred_element_type=F32)
                    grad_query[part, span] += contract(grad_scores, key, ((0,), (0,)))

            if not early:
                grad_kv_low[...] = grad_kv[...].astype(BF16)

        def kv_terms(layer):
            def add(in_ref, grad_ref, out_ref):
                out_ref[...] += contract(in_ref[...], grad_ref[...], ((0,), (0,)))

            pltpu.emit_pipeline(
                add,
                grid=(blocks,),
                in_specs=[column_spec(group), whole_spec(group, 2 * local)],
                out_specs=[pl.BlockSpec((block, 2 * local), lambda i: (i, 0))],
            )(in_all.at[z - layer], grad_kv_low, kv_weight)

        def back_to_rows(layer, diagonal):
            target = partials.at[lax.rem(layer, 2)]

            @pl.loop(0, tiles)
            def _(i):
                part = pl.ds(pl.multiple_of(i * tile, tile), tile)
                value = contract(grad_kv_low[part, :], qkv_w[:, : 2 * local], ((1,), (1,)))
                if diagonal:
                    value = value + contract(
                        grad_query[part, :].astype(BF16), qkv_w[:, 2 * local :], ((1,), (1,))
                    )
                target[part, :] = value.astype(BF16)

        def share_copy(layer, source):
            return remote(
                source.at[layer], share_landing.at[layer], share_send, share_recv, (layer,), z=z - 1
            )

        def keep_share(layer, z):
            def store(part, value):
                share[part, :] = value

            round_of(layer + 2).end(store)

            @pl.when(layer < z)
            def _():
                resid_x[...] = share[...].astype(BF16)
                pltpu.sync_copy(resid_x, share_own.at[layer])

                @pl.when(z == count - 1)
                def _():
                    share_copy(layer, share_own).start()

        def share_line(layer, z):
            @pl.when((layer < z) & (z < count - 1))
            def _():
                share_copy(layer, share_own).wait_recv()
                pltpu.sync_copy(share_own.at[layer], resid_x)
                pltpu.sync_copy(share_landing.at[layer], resid_branch)
                resid_x[...] = (resid_x[...].astype(F32) + resid_branch[...].astype(F32)).astype(
                    BF16
                )
                pltpu.sync_copy(resid_x, share_sums.at[layer])
                share_copy(layer, share_sums).start()

        def finish_output():
            own = pl.ds(pl.multiple_of(x * rows, rows), rows)
            pltpu.sync_copy(x_all.at[0, own, own_column], resid_x)
            pltpu.sync_copy(branch_in.at[own, own_column], resid_branch)

            def store(part, value):
                resid = resid_x[part, :].astype(F32) + resid_branch[part, :].astype(F32)
                resid_x[part, :] = (resid + value).astype(BF16)

            out_sum.end(store)
            pltpu.sync_copy(resid_x, output)

        def hop_of(line, h, steps=(1, -1)):
            return functools.partial(line.hop, h, steps)

        events = [[] for _ in range(count)]
        for h in range(3, count):
            events[min(h - 3, count - 2)].append(hop_of(down_line, h))
            events[min(h - 2, count - 2)].append(hop_of(up_line, h))
        attn_lines[0].hop(1)

        def split_terms(in_ref, grad_ref, kv_ref, query_ref, key_ref, value_ref):
            key_ref[...] = kv_ref[:, :local].astype(BF16)
            value_ref[...] = kv_ref[:, local:].astype(BF16)
            query_ref[...] = contract(in_ref[...], grad_ref[:, :local], ((0,), (0,))).astype(BF16)

        def both(layer, act):
            @pl.when(layer < z)
            def _():
                act(layer, False)

            @pl.when(layer == z)
            def _():
                act(layer, True)

        @pl.loop(0, z + 1)
        def _(layer):
            one, two = layer >= 1, layer >= 2
            both(layer, functools.partial(attend_back, early=True))

            @pl.when(layer == 0)
            def _():
                finish_output()

            @pl.when(two)
            def _():
                keep_share(layer - 2, z)

            @pl.when(one)
            def _():
                round_of(layer + 1).twins()

            both(layer, functools.partial(attend_back, early=False))
            for k in range(count):
                if events[k]:

                    @pl.when(layer == k)
                    def _():
                        for event in events[k]:
                            event()

            kv_terms(layer)

            @pl.when(layer == z)
            def _():
                kv[:, :local] = grad_query[...].astype(BF16)
                pltpu.emit_pipeline(
                    split_terms,
                    grid=(blocks,),
                    in_specs=[
                        column_spec(group),
                        whole_spec(group, 2 * local),
                        rows_spec(2 * local, block),
                    ],
                    out_specs=[rows_spec(local, block)] * 3,
                )(in_all.at[0], kv, kv_weight, query_terms, key_terms, value_terms)
                attn_lines[1].hop(1)

            @pl.when(one)
            def _():
                round_of(layer + 1).corners()

            round_of(layer).drain()
            both(layer, back_to_rows)
            round_of(layer + 2).start()

        def first_back(x_ref, grad_ref, resid_ref, out_ref):
            normed, inverse = normed_rows(x_ref[...].astype(F32))
            grad = grad_ref[...].astype(F32)
            scaled = grad * gain1[...]
            centre = jnp.mean(scaled, axis=1, keepdims=True)
            slope = jnp.mean(scaled * normed, axis=1, keepdims=True)
            gains[0:1, :] += jnp.sum(grad * normed, axis=0, keepdims=True)
            wide[...] = inverse * (scaled - centre - normed * slope)
            out_ref[...] = resid_ref[...] + wide[:, own_column]

        def gain_copy(step):
            to = lax.rem(z + step, count)
            return pltpu.make_async_remote_copy(
                src_ref=gains,
                dst_ref=gains_landing.at[z],
                send_sem=gain_send.at[step],
                recv_sem=gain_recv.at[z],
                device_id={"z": to},
                device_id_type=MESH,
            )

        def take_rows_back():
            pltpu.emit_pipeline(
                first_back,
                grid=(group // thin,),
                in_specs=[thin_spec, thin_spec, rows_spec(width, thin)],
                out_specs=[rows_spec(width, thin)],
            )(x_all.at[0], full3, grad_resid, input_grad)
            for step in range(1, count):
                gain_copy(step).start()

        def tail(z):
            here = at.fixed(z)
            down_here, up_here, *lines_here = lines_at(here)
            spreads_here = spreads_at(here)
            last = z + 2

            def end_before():
                @pl.when(z >= 1)
                def _():
                    keep_share(z - 1, z)

            def own_share():
                @pl.when(z < count - 1)
                def _():
                    share_copy(z, share_own).wait_recv()
                    pltpu.sync_copy(share_landing.at[z], resid_branch)
                    share[...] = share[...] + resid_branch[...].astype(F32)

                last_gather.block(x, y, c)[...] = share[...].astype(BF16)
                last_gather.start()

            def rows_back():
                last_gather.corner()
                last_gather.end()
                take_rows_back()

            def final(k):
                lines_here[k].final(attn_grads[k].at[z, x])
                spreads_here[k].first()

            todo = {
                "end": end_before,
                "twins": lambda: round_of(last).twins(),
                "corners": lambda: round_of(last).corners(),
                "keep": lambda: keep_share(z, z),
                "home0": lambda: home(0, down_here),
                "home1": lambda: home(1, up_here),
                "own": own_share,
                "middle": last_gather.middle,
                "rows": rows_back,
            }
            for k in range(4):
                if k > 1:
                    todo[f"b{k}"] = hop_of(lines_here[k], 1)
                for h in range(2, count):
                    todo[f"u{k}{h}"] = hop_of(lines_here[k], h, (1,))
                    todo[f"d{k}{h}"] = hop_of(lines_here[k], h, (-1,))
                todo[f"f{k}"] = functools.partial(final, k)
                for h in range(1, count):
                    todo[f"U{k}{h}"] = functools.partial(spreads_here[k].hop, h, 1)
                    todo[f"D{k}{h}"] = functools.partial(spreads_here[k].hop, h, -1)
            for layer in range(count - 1):
                todo[f"s{layer}"] = functools.partial(share_line, layer, z)
            order = ORDERS.get((count, z)) if isinstance(z, int) else None
            if order is None:
                order = ["end", "twins", "corners", "keep", "home0", "b2", "b3", "home1"]
                for k in range(4):
                    order += [f"{way}{k}{h}" for h in range(2, count) for way in "ud"] + [f"f{k}"]
                order += [f"s{layer}" for layer in range(count - 1)] + ["own", "middle", "rows"]
                for k in range(4):
                    order += [f"{way}{k}{h}" for h in range(1, count) for way in "UD"]
            for name in order:
                todo[name]()

        if count <= 4:
            for k in range(count):

                @pl.when(z == k)
                def _():
                    tail(k)
        else:
            tail(z)
        gains_landing[z] = gains[...]
        for step in range(1, count):
            source = lax.rem(z + step, count)
            pltpu.make_async_remote_copy(
                src_ref=gains,
                dst_ref=gains_landing.at[source],
                send_sem=gain_send.at[step],
                recv_sem=gain_recv.at[source],
                device_id={"z": source},
                device_id_type=MESH,
            ).wait_recv()
        for step in range(1, count):
            gain_copy(step).wait_send()
        gains[...] = jnp.sum(gains_landing[...], axis=0)
        pltpu.sync_copy(gains, gains_out)
        for spread in spreads:
            spread.end()

        @pl.loop(0, count)
        def _(layer):
            @pl.when(layer < z)
            def _():
                share_copy(layer, share_own).wait_send()

    pl.run_scoped(
        attention,
        pltpu.VMEM((features, 3 * local), BF16),
        pltpu.VMEM((features, local), BF16),
        pltpu.VMEM((group, local), BF16),
        pltpu.VMEM((group, local), BF16),
        pltpu.VMEM((group, 2 * local), BF16),
        pltpu.VMEM((group, local), BF16),
        pltpu.VMEM((group, local), F32),
        pltpu.VMEM((group, 2 * local), F32),
        pltpu.VMEM((group, 2 * local), BF16),
        pltpu.VMEM((features, 2 * local), F32),
        pltpu.VMEM((heads, group, HD), F32),
        pltpu.VMEM((heads, 1, group), F32),
        pltpu.VMEM((heads, 1, group), F32),
        pltpu.VMEM((thin, features), F32),
        pltpu.VMEM((rows, width), BF16),
        pltpu.VMEM((rows, width), BF16),
        pltpu.VMEM((rows, width), F32),
    )
    for which in (0, 1):
        home_copy(which, True).wait_recv()
        home_copy(which).wait_send()
    for line in (down_line, up_line, *attn_lines):
        line.drain()
    round_of(z + 1).drain()
    round_of(z + 2).drain()
    first_gather.drain()
    last_gather.drain()


def back(count, *args):
    (x_all, _, _, query, *_, gain1, gain2, start_row, key_place) = args
    down_all = args[9]
    _, group, features = x_all.shape
    rows = group // 2
    local = query.shape[1]
    hidden = down_all.shape[1]
    width = features // 4
    chunk = features // count
    hbm, vmem = pl.BlockSpec(memory_space=pl.ANY), pl.BlockSpec(memory_space=pltpu.VMEM)

    def out(*shape, dtype=BF16):
        return jax.ShapeDtypeStruct(shape, dtype)

    dma = pltpu.SemaphoreType.DMA
    sizes = (hidden, hidden) + (local,) * 4
    return pl.pallas_call(
        functools.partial(back_kernel, count),
        name="back",
        out_shape=(
            out(rows, width),
            out(group, width, dtype=F32),
            out(8, features, dtype=F32),
            out(2, 2, chunk // 2, hidden),
            *[out(count, 2, chunk, local)] * 4,
            *[out(features, size) for size in sizes],
            *[out(count + 1, chunk, size) for size in sizes],
            *[out(count, chunk, size) for size in sizes],
            out(2, chunk, hidden),
            out(group, features),
            out(group, width, dtype=F32),
            out(count, rows, width),
            out(count, rows, width),
            out(count, rows, width),
        ),
        in_specs=[hbm] * 15 + [vmem] * 4,
        out_specs=[hbm] * 32,
        scratch_shapes=[
            pltpu.VMEM((2, group, features), BF16),
            pltpu.VMEM((group, features), BF16),
            pltpu.VMEM((group, features), BF16),
            pltpu.VMEM((3, 4, rows, width), BF16),
            pltpu.VMEM((2, rows // 2, width), BF16),
            pltpu.VMEM((2, rows // 2, width), BF16),
            pltpu.VMEM((2, rows, width), BF16),
            pltpu.VMEM((2, rows, width), BF16),
            pltpu.VMEM((8, features), F32),
            pltpu.VMEM((count, 8, features), F32),
            dma((8,)),
            dma((count + 2, 10)),
            dma((count + 2, 10)),
            dma((2, 9)),
            dma((2, 9)),
            dma((6, count)),
            dma((6, count + 1)),
            dma((2,)),
            dma((2,)),
            *[dma((4, count))] * 5,
            *[dma((count,))] * 4,
        ],
        compiler_params=pltpu.CompilerParams(
            collective_id=1, has_side_effects=True, vmem_limit_bytes=60 * 1024 * 1024
        ),
    )(*args)


def finish(mlp_grads, *attn_grads):
    count, _, chunk, local = attn_grads[0].shape
    half, hidden = mlp_grads.shape[2:]
    steps = max(1, min(count, half // 16))
    part, layers = half // steps, count // steps

    def step(mlp_ref, *refs):
        up_ref, down_ref = refs[8:]
        for side in range(2):
            span = slice(side * local, (side + 1) * local)
            for source, target in zip(refs[:4], refs[4:8]):
                for i in range(layers):
                    target[i * chunk : (i + 1) * chunk, span] = source[i, side].astype(F32)
            span = slice(side * hidden, (side + 1) * hidden)
            down_ref[:, span] = mlp_ref[0, side].astype(F32)
            up_ref[:, span] = mlp_ref[1, side].astype(F32)

    def rows_of(tall, size):
        return pl.BlockSpec((tall, size), lambda i: (i, 0))

    return pl.pallas_call(
        step,
        name="finish",
        grid=(steps,),
        in_specs=[
            pl.BlockSpec((2, 2, part, hidden), lambda i: (0, 0, i, 0)),
            *[pl.BlockSpec((layers, 2, chunk, local), lambda i: (i, 0, 0, 0))] * 4,
        ],
        out_specs=[rows_of(layers * chunk, 2 * local)] * 4 + [rows_of(part, 2 * hidden)] * 2,
        out_shape=[jax.ShapeDtypeStruct((count * chunk, 2 * local), F32)] * 4
        + [jax.ShapeDtypeStruct((half, 2 * hidden), F32)] * 2,
        compiler_params=pltpu.CompilerParams(vmem_limit_bytes=48 * 1024 * 1024),
    )(mlp_grads, *attn_grads)


def body(
    layer_input,
    clip_lengths,
    key_padding,
    norm1_gain,
    w_query,
    w_key,
    w_value,
    w_out,
    norm2_gain,
    w_up,
    w_down,
    out_grad,
):
    count = lax.axis_size("z")
    z, x = lax.axis_index("z"), lax.axis_index("x")
    rows = layer_input.shape[0]
    width = w_query.shape[0]
    local = w_query.shape[1] // 2
    hidden = w_up.shape[1] // 2
    clip_ends = jnp.cumsum(clip_lengths)
    position = jnp.arange(key_padding.shape[0], dtype=jnp.int32)
    starts = jnp.max(jnp.where(position[:, None] >= clip_ends, clip_ends, 0), axis=1)
    key_place = jnp.where(key_padding > 0, position, -1).reshape(count, 1, 2 * rows)
    own_starts = lax.dynamic_slice_in_dim(starts, z * 2 * rows, 2 * rows)
    gain1, gain2 = norm1_gain[None], norm2_gain[None]
    *kept, down_full, up_full = front(
        count, layer_input, out_grad, w_query, w_key, w_value, w_out, w_up, w_down,
        gain1, gain2, own_starts[:, None], key_place,
    )
    output, input_grad, gains, mlp_grads, *rest = back(
        count, *kept, down_full.reshape(width, hidden), up_full.reshape(width, hidden),
        w_query, w_key, w_value, w_out, gain1, gain2, own_starts[None], key_place,
    )
    out_grad_w, query_grad, key_grad, value_grad, up_grad, down_grad = finish(
        mlp_grads, *rest[:4]
    )
    return (
        output,
        lax.dynamic_slice_in_dim(input_grad, x * rows, rows, 0),
        gains[0],
        query_grad,
        key_grad,
        value_grad,
        out_grad_w,
        gains[1],
        up_grad,
        down_grad,
    )


def solution(mesh):
    seq, head = mesh.shape["seq"], mesh.shape["head"]
    fine = Mesh(mesh.devices.reshape(seq // 2, 2, head // 2, 2), ("z", "x", "y", "core"))
    seq_axes, head_axes = ("z", "x"), ("y", "core")
    both, columns = P(seq_axes, head_axes), P(None, head_axes)
    return jax.shard_map(
        body,
        mesh=fine,
        in_specs=(both, P(), P(), P(), columns, columns, columns, columns, P(), both, both, both),
        out_specs=(both, both, P(), columns, columns, columns, columns, P(), both, both),
        check_vma=False,
    )
```

```python
import copy
import functools

import jax
import jax.numpy as jnp
from jax import lax
from jax.experimental import pallas as pl
from jax.experimental.pallas import tpu as pltpu
from jax.sharding import Mesh, PartitionSpec as P

HD = 128
NORM_EPS = 1e-05
BF16 = jnp.bfloat16
F32 = jnp.float32
LAYER = ("x", "y", "core")


MESH = pl.DeviceIdType.MESH
LOG2E = 1.4426950408889634


def clip_start(position, clip_lengths):
    end, start = jnp.int32(0), jnp.zeros_like(position)
    for clip in range(clip_lengths.shape[0]):
        end = end + clip_lengths[clip]
        start = jnp.where(position >= end, end, start)
    return start


def place_keys(key_place, key_padding, count, group):
    for layer in range(count):
        position = lax.broadcasted_iota(jnp.int32, (1, group), 1) + layer * group
        key_place[layer] = jnp.where(key_padding[layer] > 0, position, -1)


def remote(src, dst, sends, recvs, slot, **device):
    return pltpu.make_async_remote_copy(
        src_ref=src,
        dst_ref=dst,
        send_sem=sends.at[slot],
        recv_sem=recvs.at[slot],
        device_id=device,
        device_id_type=MESH,
    )


def pick(which, left, right):
    if isinstance(which, bool):
        return left if which else right
    return jnp.where(which, left, right)


def contract(left, right, dims):
    return lax.dot_general(left, right, (dims, ((), ())), preferred_element_type=F32)


class Place:
    def __init__(self, count):
        self.count = count
        self.z = lax.axis_index("z")
        self.x, self.y, self.c = lax.axis_index("x"), lax.axis_index("y"), lax.axis_index("core")
        self.ox, self.oy, self.oc = 1 - self.x, 1 - self.y, 1 - self.c

    def fixed(self, z):
        other = copy.copy(self)
        other.z = z
        return other

    def meet(self, whole_line=False):
        barrier = pltpu.get_barrier_semaphore()
        for device in ({"x": self.ox}, {"y": self.oy}, {"core": self.oc}):
            pl.semaphore_signal(barrier, inc=1, device_id=device, device_id_type=MESH)
        if whole_line:
            for step in range(1, self.count):
                pl.semaphore_signal(
                    barrier,
                    inc=1,
                    device_id={"z": lax.rem(self.z + step, self.count)},
                    device_id_type=MESH,
                )
            pl.semaphore_signal(
                barrier, inc=1, device_id={"y": self.oy, "core": self.oc}, device_id_type=MESH
            )
            pl.semaphore_wait(barrier, 4 + self.count - 1)
            return
        above, below = self.z < self.count - 1, self.z > 0
        for there, step in ((above, 1), (below, -1)):

            @pl.when(there)
            def _():
                pl.semaphore_signal(
                    barrier, inc=1, device_id={"z": self.z + step}, device_id_type=MESH
                )

        pl.semaphore_wait(barrier, 3 + above.astype(jnp.int32) + below.astype(jnp.int32))


class Gather:
    def __init__(self, at, array, rows, width, sends, recvs, lead=()):
        self.at, self.array, self.sends, self.recvs, self.lead = at, array, sends, recvs, lead
        self.rows, self.width = rows, width

    def block(self, xi, yi, ci, first=0, size=None):
        size = self.rows if size is None else size
        return self.array.at[
            pl.ds(pl.multiple_of(xi * self.rows + first, size), size),
            pl.ds(pl.multiple_of((2 * yi + ci) * self.width, self.width), self.width),
        ]

    def copy(self, k, landing=False):
        at, half = self.at, self.rows // 2
        x, y, c, ox, oy, oc = at.x, at.y, at.c, at.ox, at.oy, at.oc
        place = {
            0: ((x, y, c), (ox, y, c), {"x": ox}),
            1: ((x, y, c), (x, oy, c), {"y": oy}),
            2: ((x, y, c), (x, y, oc), {"core": oc}),
            3: ((ox, y, c, 0, half), (ox, oy, c, 0, half), {"y": oy}),
            4: ((x, oy, c, half, half), (ox, oy, c, half, half), {"x": ox}),
            5: ((ox, y, c), (ox, y, oc), {"core": oc}),
            6: ((x, oy, c), (x, oy, oc), {"core": oc}),
            7: ((ox, oy, c, 0, half), (ox, oy, oc, 0, half), {"core": oc}),
            8: ((ox, oy, c, half, half), (ox, oy, oc, half, half), {"core": oc}),
        }
        source, lands, device = place[k]
        ref = self.block(*(lands if landing else source))
        return remote(ref, ref, self.sends, self.recvs, self.lead + (k,), **device)

    def start(self):
        for k in (0, 1, 2):
            self.copy(k).start()

    def middle(self):
        self.copy(0, True).wait_recv()
        self.copy(3).start()
        self.copy(5).start()
        self.copy(1, True).wait_recv()
        self.copy(4).start()
        self.copy(6).start()

    def corner(self):
        self.copy(3, True).wait_recv()
        self.copy(7).start()
        self.copy(4, True).wait_recv()
        self.copy(8).start()

    def end(self):
        for k in (2, 5, 6, 7, 8):
            self.copy(k, True).wait_recv()

    def drain(self):
        for k in range(9):
            self.copy(k).wait_send()


class Reduce:
    def __init__(self, at, array, rows, width, buffers, sends, recvs, by_y=False):
        self.at, self.array, self.sends, self.recvs = at, array, sends, recvs
        self.rows, self.width, self.by_y = rows, width, by_y
        self.twin, self.corner_x, self.corner_y, self.from_x, self.from_y = buffers

    def block(self, xi, yi, ci, first=0, size=None):
        return Gather.block(self, xi, yi, ci, first, size)

    def copy(self, k):
        at, half = self.at, self.rows // 2
        x, y, c, ox, oy, oc = at.x, at.y, at.c, at.ox, at.oy, at.oc
        low, high = pl.ds(0, half), pl.ds(half, half)
        place = {
            0: ((ox, oy, oc), self.twin.at[0], {"core": oc}),
            1: ((ox, y, oc), self.twin.at[1], {"core": oc}),
            2: ((x, oy, oc), self.twin.at[2], {"core": oc}),
            3: ((x, y, oc), self.twin.at[3], {"core": oc}),
            4: ((ox, oy, c, 0, half), self.corner_y, {"y": oy}),
            5: ((ox, oy, c, half, half), self.corner_x, {"y": oy} if self.by_y else {"x": ox}),
            6: ((ox, y, c, half, half), self.from_x.at[high], {"x": ox}),
            7: ((x, oy, c, 0, half), self.from_y.at[low], {"y": oy}),
            8: ((ox, y, c, 0, half), self.from_x.at[low], {"x": ox}),
            9: ((x, oy, c, half, half), self.from_y.at[high], {"y": oy}),
        }
        source, lands, device = place[k]
        return remote(self.block(*source), lands, self.sends, self.recvs, (k,), **device)

    def add(self, target, other):
        rows = target.shape[0]
        tile = min(rows, 128)

        @pl.loop(0, rows // tile)
        def _(i):
            part = pl.ds(pl.multiple_of(i * tile, tile), tile)
            target[part, :] = (target[part, :].astype(F32) + other[part, :].astype(F32)).astype(
                target.dtype
            )

    def start(self):
        for k in (0, 1, 2, 3):
            self.copy(k).start()

    def twins(self):
        at, half = self.at, self.rows // 2
        x, y, c, ox, oy = at.x, at.y, at.c, at.ox, at.oy
        self.copy(0).wait_recv()
        self.add(self.block(ox, oy, c), self.twin.at[0])
        self.copy(4).start()
        self.copy(5).start()
        self.copy(1).wait_recv()
        self.add(self.block(ox, y, c), self.twin.at[1])
        if not self.by_y:
            self.copy(6).start()
        self.copy(2).wait_recv()
        self.add(self.block(x, oy, c), self.twin.at[2])
        self.copy(7).start()
        if self.by_y:
            self.copy(9).start()
        self.copy(3).wait_recv()

    def corners(self):
        at, half = self.at, self.rows // 2
        self.copy(4).wait_recv()
        self.add(self.block(at.ox, at.y, at.c, 0, half), self.corner_y)
        self.copy(8).start()
        self.copy(5).wait_recv()
        if self.by_y:
            self.add(self.block(at.ox, at.y, at.c, half, half), self.corner_x)
            self.copy(6).start()
        else:
            self.add(self.block(at.x, at.oy, at.c, half, half), self.corner_x)
            self.copy(9).start()

    def end(self, store):
        for k in (6, 7, 8, 9):
            self.copy(k).wait_recv()
        own = self.block(self.at.x, self.at.y, self.at.c)
        tile = min(self.rows, 128)

        @pl.loop(0, self.rows // tile)
        def _(i):
            part = pl.ds(pl.multiple_of(i * tile, tile), tile)
            store(
                part,
                own[part, :].astype(F32)
                + self.twin[3, part, :].astype(F32)
                + self.from_x[part, :].astype(F32)
                + self.from_y[part, :].astype(F32),
            )

    def drain(self):
        for k in range(10):
            self.copy(k).wait_send()


def reduce_scratch(rows, width):
    return [
        pltpu.VMEM((4, rows, width), BF16),
        pltpu.VMEM((rows // 2, width), BF16),
        pltpu.VMEM((rows // 2, width), BF16),
        pltpu.VMEM((rows, width), BF16),
        pltpu.VMEM((rows, width), BF16),
    ]


def normed_rows(rows):
    mean = jnp.mean(rows, axis=1, keepdims=True)
    centred = rows - mean
    inverse = lax.rsqrt(jnp.mean(centred * centred, axis=1, keepdims=True) + NORM_EPS)
    return centred * inverse, inverse


class Weights:
    def __init__(self, at, which, weight, whole, sems):
        self.at, self.which, self.weight, self.whole = at, which, weight, whole
        self.local, self.xs, self.xr, self.us, self.ds, self.rs = sems
        self.half = weight.shape[1] // 2

    def columns(self, which):
        return self.weight.at[:, pl.ds(pl.multiple_of(which * self.half, self.half), self.half)]

    def own(self, stage, out):
        at = self.at
        source, target = (stage, self.whole.at[at.z, at.x]) if out else (self.columns(at.x), stage)
        return pltpu.make_async_copy(source, target, self.local.at[self.which])

    def swap(self, landing=False):
        at = self.at
        dst = self.whole.at[at.z, at.ox] if landing else self.whole.at[at.z, at.x]
        return remote(self.columns(at.ox), dst, self.xs, self.xr, (self.which,), x=at.ox)

    def move(self, layer, part, step):
        ref = self.whole.at[layer, part]
        sends = self.us if step > 0 else self.ds
        return pltpu.make_async_remote_copy(
            src_ref=ref,
            dst_ref=ref,
            send_sem=sends.at[self.which, layer, part],
            recv_sem=self.rs.at[self.which, layer, part],
            device_id={"z": self.at.z + step},
            device_id_type=MESH,
        )

    def first(self, mine, steps=(1, -1)):
        at = self.at
        part = at.x if mine else at.ox
        for step, there in ((1, at.z < at.count - 1), (-1, at.z > 0)):
            if step in steps:

                @pl.when(there)
                def _():
                    self.move(at.z, part, step).start()

    def hop(self, distance, mine):
        at = self.at
        part = at.x if mine else at.ox

        @pl.when(at.z >= distance)
        def _():
            self.move(at.z - distance, part, 1).wait_recv()

            @pl.when(at.z < at.count - 1)
            def _():
                self.move(at.z - distance, part, 1).start()

        @pl.when(at.z + distance < at.count)
        def _():
            self.move(at.z + distance, part, -1).wait_recv()

            @pl.when(at.z > 0)
            def _():
                self.move(at.z + distance, part, -1).start()

    def drain(self):
        at = self.at
        self.swap().wait_send()
        for part in (0, 1):

            @pl.loop(0, at.count)
            def _(layer):
                @pl.when((layer <= at.z) & (at.z < at.count - 1))
                def _():
                    self.move(layer, part, 1).wait_send()

                @pl.when((layer >= at.z) & (at.z > 0))
                def _():
                    self.move(layer, part, -1).wait_send()


def front_kernel(
    count,
    xs,
    og,
    w_query,
    w_key,
    w_value,
    w_out,
    w_up,
    w_down,
    gain1,
    gain2,
    clip_lengths,
    key_padding,
    x_all,
    in_all,
    kv_all,
    query_out,
    attended_out,
    log_out,
    branch_out,
    mlp_out,
    og_all,
    down_all,
    up_all,
    start_of,
    key_place,
    qkv_w,
    out_w,
    query,
    kv,
    high,
    total,
    sums,
    attended,
    partial,
    branch,
    twin,
    corner_x,
    corner_y,
    from_x,
    from_y,
    load_sem,
    gather_send,
    gather_recv,
    line_send,
    line_recv,
    w_local,
    w_xs,
    w_xr,
    w_us,
    w_ds,
    w_rs,
    reduce_send,
    reduce_recv,
):
    at = Place(count)
    z, x, y, c = at.z, at.x, at.y, at.c
    rows, width = xs.shape
    group = 2 * rows
    local = w_query.shape[1] // 2
    heads = local // HD
    features = gain1.shape[1]
    tile = 256 if group % 256 == 0 else group
    tiles = group // tile

    def columns_of(weight):
        return weight.at[:, pl.ds(pl.multiple_of(x * local, local), local)]

    loads = [
        pltpu.make_async_copy(
            columns_of(w), qkv_w.at[:, pl.ds(i * local, local)], load_sem.at[i]
        )
        for i, w in enumerate((w_key, w_value, w_query))
    ]
    loads.append(pltpu.make_async_copy(columns_of(w_out), out_w, load_sem.at[3]))

    def gather_of(d):
        return Gather(at, x_all.at[d], rows, width, gather_send, gather_recv, (d,))

    og_gather = Gather(at, og_all, rows, width, gather_send, gather_recv, (count,))
    branch_gather = Gather(at, branch, rows, width, gather_send, gather_recv, (count + 1,))

    def own_block(d):
        return gather_of(d).block(x, y, c)

    def line_copy(d):
        return remote(own_block(d), own_block(d + 1), line_send, line_recv, (d,), z=z + 1)

    weight_sems = (w_local, w_xs, w_xr, w_us, w_ds, w_rs)
    down = Weights(at, 0, w_down, down_all, weight_sems)
    up = Weights(at, 1, w_up, up_all, weight_sems)

    w_rows, hidden = w_up.shape[0], w_up.shape[1] // 2
    places = [
        partial.at[pl.ds(0, rows), pl.ds(i * width, width)] for i in range(2)
    ] + [partial.at[pl.ds(rows, w_rows), pl.ds(i * hidden, hidden)] for i in range(2)]
    into = [
        pltpu.make_async_copy(xs, places[0], load_sem.at[4]),
        down.own(places[2], False),
        up.own(places[3], False),
        pltpu.make_async_copy(og, places[1], load_sem.at[5]),
    ]
    onto = [
        pltpu.make_async_copy(places[0], own_block(0), load_sem.at[4]),
        down.own(places[2], True),
        up.own(places[3], True),
        pltpu.make_async_copy(places[1], og_gather.block(x, y, c), load_sem.at[5]),
    ]
    for copy in into + loads:
        copy.start()
    position = lax.broadcasted_iota(jnp.int32, (group, 1), 0) + z * group
    start_of[...] = clip_start(position, clip_lengths)
    place_keys(key_place, key_padding, count, group)
    for first, second in zip(into, onto):
        first.wait()
        second.start()
    at.meet()
    onto[0].wait()

    @pl.when(z < count - 1)
    def _():
        line_copy(0).start()

    gather_of(0).start()
    onto[1].wait()
    down.first(True)
    onto[2].wait()
    up.first(True, (-1,))
    onto[3].wait()
    gather_of(0).middle()
    for load in loads:
        load.wait()

    def project(d, with_query):
        size = qkv_w.shape[1] if with_query else 2 * local

        def step(x_ref, in_ref, kv_ref, *maybe_query):
            normed, _ = normed_rows(x_ref[...].astype(F32))
            rounded = (normed * gain1[...]).astype(BF16)
            in_ref[...] = rounded
            product = jnp.dot(rounded, qkv_w[:, :size], preferred_element_type=F32)
            kv_ref[...] = product[:, : 2 * local].astype(BF16)
            if with_query:
                maybe_query[0][...] = product[:, 2 * local :].astype(BF16)

        def rows_of(size):
            return pl.BlockSpec((tile, size), lambda i: (i, 0))

        outs = [rows_of(features), rows_of(2 * local)] + ([rows_of(local)] if with_query else [])
        refs = [in_all.at[d], kv_all.at[d]] + ([query_out] if with_query else [])
        pltpu.emit_pipeline(step, grid=(tiles,), in_specs=[rows_of(features)], out_specs=outs)(
            x_all.at[d], *refs
        )

    def attend(d, diagonal):
        keys = key_place[z - d]

        @pl.loop(0, tiles)
        def _(i):
            part = pl.ds(pl.multiple_of(i * tile, tile), tile)
            allowed = keys >= start_of[part, :]
            if diagonal:
                query_at = lax.broadcasted_iota(jnp.int32, (tile, group), 0) + i * tile
                key_at = lax.broadcasted_iota(jnp.int32, (tile, group), 1)
                allowed = (allowed & (key_at <= query_at)) | (key_at == query_at)
            for h in range(heads):
                span = slice(h * HD, (h + 1) * HD)
                scores = contract(query[part, span], kv[:, span], ((1,), (1,)))
                scores = jnp.where(allowed, scores * (HD**-0.5 * LOG2E), -1e30)
                top = jnp.max(scores, axis=1, keepdims=True)
                if not diagonal:
                    old = high[h, part, :1]
                    top = jnp.maximum(old, top)
                    fade = jnp.exp2(old - top)
                weights = jnp.exp2(scores - top)
                mass = jnp.sum(weights, axis=1, keepdims=True)
                value = jnp.dot(
                    weights.astype(BF16),
                    kv[:, local + h * HD : local + (h + 1) * HD],
                    preferred_element_type=F32,
                )
                if not diagonal:
                    mass = mass + total[h, part, :1] * fade
                    value = value + sums[part, span] * fade
                high[h, part, :] = jnp.broadcast_to(top, (tile, HD))
                total[h, part, :] = jnp.broadcast_to(mass, (tile, HD))
                sums[part, span] = value

    def fetch(d, diagonal):
        pltpu.sync_copy(kv_all.at[d], kv)
        if diagonal:
            pltpu.sync_copy(query_out, query)

    def bring(d):
        @pl.when(z >= d)
        def _():
            remote(own_block(d - 1), own_block(d), line_send, line_recv, (d - 1,), z=z).wait_recv()

            @pl.when((d < count - 1) & (z < count - 1))
            def _():
                line_copy(d).start()

            gather_of(d).start()

    def within(d, *names):
        @pl.when(z >= d)
        def _():
            for name in names:
                getattr(gather_of(d), name)()

    def other_rows(weight):
        weight.swap(True).wait_recv()
        weight.first(False)

    def hop_of(weight, distance, mine):
        return functools.partial(weight.hop, distance, mine)

    events = [
        hop_of(down, 1, True),
        hop_of(up, 1, True),
        functools.partial(other_rows, down),
        hop_of(down, 1, False),
        functools.partial(other_rows, up),
        hop_of(up, 1, False),
    ]
    for distance in range(2, count):
        for mine in (True, False):
            events += [hop_of(down, distance, mine), hop_of(up, distance, mine)]

    def advance(many=1):
        for _ in range(min(many, len(events))):
            events.pop(0)()

    bring(1)
    up.first(True, (1,))
    gather_of(0).corner()
    gather_of(0).end()
    project(0, True)
    within(1, "middle")
    down.swap().start()
    fetch(0, True)
    attend(0, True)

    @pl.loop(2, count)
    def _(d):
        bring(d)

        for k in (2, 3):

            @pl.when(d == k)
            def _():
                events[2 * k - 4]()

        within(d - 1, "corner", "end")

        @pl.when(z >= d - 1)
        def _():
            project(d - 1, False)

        within(d, "middle")

        for k in (2, 3):

            @pl.when(d == k)
            def _():
                if k == 2:
                    up.swap().start()
                events[2 * k - 3]()

        @pl.when(z >= d - 1)
        def _():
            fetch(d - 1, False)
            attend(d - 1, False)

    if count < 3:
        up.swap().start()
    del events[: 2 * min(count - 2, 2)]
    advance()
    og_gather.start()
    within(count - 1, "corner", "end")

    @pl.when(z >= count - 1)
    def _():
        project(count - 1, False)

    advance()
    og_gather.middle()

    @pl.when(z >= count - 1)
    def _():
        fetch(count - 1, False)
        attend(count - 1, False)

    advance(2)
    og_gather.corner()

    @pl.loop(0, tiles)
    def _(i):
        part = pl.ds(pl.multiple_of(i * tile, tile), tile)
        for h in range(heads):
            span = slice(h * HD, (h + 1) * HD)
            mass = total[h, part, :]
            attended[part, span] = (sums[part, span] / mass).astype(BF16)
            high[h, part, :] = high[h, part, :] + jnp.log2(mass)
        partial[part, :] = contract(attended[part, :], out_w[...], ((1,), (1,))).astype(BF16)

    outs = [
        pltpu.make_async_copy(attended, attended_out, load_sem.at[6]),
        pltpu.make_async_copy(high, log_out, load_sem.at[7]),
    ]
    for out in outs:
        out.start()
    reduce = Reduce(
        at, partial, rows, width, (twin, corner_x, corner_y, from_x, from_y), reduce_send, reduce_recv
    )
    reduce.start()
    og_gather.end()
    reduce.twins()
    advance()
    reduce.corners()
    advance()
    own_branch = branch_gather.block(x, y, c)

    def store(part, value):
        own_branch[part, :] = value.astype(BF16)

    reduce.end(store)
    branch_gather.start()
    advance()
    branch_gather.middle()
    advance()
    branch_gather.corner()
    branch_gather.end()
    pltpu.sync_copy(branch, branch_out)

    def second_norm(x_ref, branch_ref, mlp_ref):
        normed, _ = normed_rows(x_ref[...].astype(F32) + branch_ref[...].astype(F32))
        mlp_ref[...] = (normed * gain2[...]).astype(BF16)

    spec = pl.BlockSpec((tile, features), lambda i: (i, 0))
    pltpu.emit_pipeline(second_norm, grid=(tiles,), in_specs=[spec, spec], out_specs=[spec])(
        x_all.at[0], branch_out, mlp_out
    )
    advance(len(events))

    for out in outs:
        out.wait()
    down.drain()
    up.drain()
    reduce.drain()
    branch_gather.drain()
    og_gather.drain()

    @pl.loop(0, count)
    def _(d):
        within(d, "drain")

        @pl.when((z >= d) & (d < count - 1) & (z < count - 1))
        def _():
            line_copy(d).wait_send()


def front(count, xs, og, *args):
    w_query, w_up, gain1 = args[0], args[4], args[6]
    rows, width = xs.shape
    group, features = 2 * rows, gain1.shape[1]
    local = w_query.shape[1] // 2
    heads = local // HD
    hidden = w_up.shape[1] // 2
    w_rows = w_up.shape[0]
    hbm, vmem, smem = (
        pl.BlockSpec(memory_space=space) for space in (pl.ANY, pltpu.VMEM, pltpu.SMEM)
    )

    def out(*shape, dtype=BF16):
        return jax.ShapeDtypeStruct(shape, dtype)

    dma = pltpu.SemaphoreType.DMA
    return pl.pallas_call(
        functools.partial(front_kernel, count),
        name="front",
        out_shape=(
            out(count, group, features),
            out(count, group, features),
            out(count, group, 2 * local),
            out(group, local),
            out(group, local),
            out(heads, group, HD, dtype=F32),
            out(group, features),
            out(group, features),
            out(group, features),
            out(count, 2, w_rows, hidden),
            out(count, 2, w_rows, hidden),
        ),
        in_specs=[hbm] * 8 + [vmem] * 2 + [smem, vmem],
        out_specs=[hbm] * 11,
        scratch_shapes=[
            pltpu.VMEM((group, 1), jnp.int32),
            pltpu.VMEM((count, 1, group), jnp.int32),
            pltpu.VMEM((features, 3 * local), BF16),
            pltpu.VMEM((features, local), BF16),
            pltpu.VMEM((group, local), BF16),
            pltpu.VMEM((group, 2 * local), BF16),
            pltpu.VMEM((heads, group, HD), F32),
            pltpu.VMEM((heads, group, HD), F32),
            pltpu.VMEM((group, local), F32),
            pltpu.VMEM((group, local), BF16),
            pltpu.VMEM((group, features), BF16),
            pltpu.VMEM((group, features), BF16),
            *reduce_scratch(rows, width),
            dma((8,)),
            dma((count + 2, 9)),
            dma((count + 2, 9)),
            dma((count,)),
            dma((count,)),
            dma((2,)),
            dma((2,)),
            dma((2,)),
            dma((2, count, 2)),
            dma((2, count, 2)),
            dma((2, count, 2)),
            dma((10,)),
            dma((10,)),
        ],
        compiler_params=pltpu.CompilerParams(
            collective_id=0, has_side_effects=True, vmem_limit_bytes=56 * 1024 * 1024
        ),
    )(xs, og, *args)


class LineSum:
    def __init__(self, at, which, terms, landing, sums, sends, recvs, eager=False):
        self.at, self.which, self.eager = at, which, eager
        self.terms, self.landing, self.sums = terms, landing, sums
        self.sends, self.recvs = sends, recvs
        self.rows = sums.shape[1]

    def chunk(self, c):
        return self.terms.at[pl.ds(pl.multiple_of(c * self.rows, self.rows), self.rows)]

    def move(self, source, c, slot, step):
        return pltpu.make_async_remote_copy(
            src_ref=source,
            dst_ref=self.landing.at[slot],
            send_sem=self.sends.at[self.which, c],
            recv_sem=self.recvs.at[self.which, slot],
            device_id={"z": self.at.z + step},
            device_id_type=MESH,
        )

    def landed(self, slot):
        self.move(self.landing.at[slot], 0, slot, 0).wait_recv()

    def total(self, refs, out):
        tile = min(256, self.rows)

        def step(*tiles):
            value = tiles[0][...].astype(F32)
            for other in tiles[1:-1]:
                value = value + other[...].astype(F32)
            tiles[-1][...] = value.astype(BF16)

        spec = pl.BlockSpec((tile, self.sums.shape[2]), lambda i: (i, 0))
        pltpu.emit_pipeline(
            step, grid=(self.rows // tile,), in_specs=[spec] * len(refs), out_specs=[spec]
        )(*refs, out)

    def begin(self, h):
        n, z = self.at.count, self.at.z
        for step, end, c, slot in ((1, 0, n - h, n - h), (-1, n - 1, h - 1, None)):
            if slot is None:
                slot = n if c == n - 2 else c

            @pl.when(z == end)
            def _():
                self.move(self.chunk(c), c, slot, step).start()

    def hop(self, h, steps=(1, -1)):
        at, n, z = self.at, self.at.count, self.at.z
        if h == 1:
            for each in range(1, n if self.eager else 2):
                self.begin(each)
        for step, c, there in (
            (1, n - h + z, (z <= h - 1) & (z < n - 1) & (z > 0)),
            (-1, z - n + h, (z >= n - h) & (z > 0) & (z < n - 1)),
        ):
            if step not in steps:
                continue
            slot = c if step > 0 else pick(c == z - 1, n, c)

            @pl.when(there)
            def _():
                self.landed(c)
                self.total([self.chunk(c), self.landing.at[c]], self.sums.at[c])
                self.move(self.sums.at[c], c, slot, step).start()

    def final(self, out):
        n, z = self.at.count, self.at.z
        below, above = self.landing.at[z], self.landing.at[n]

        @pl.when(z > 0)
        def _():
            self.landed(z)

        @pl.when(z < n - 1)
        def _():
            self.landed(n)

        @pl.when(z == 0)
        def _():
            self.total([self.chunk(z), above], out)

        @pl.when(z == n - 1)
        def _():
            self.total([self.chunk(z), below], out)

        @pl.when((z > 0) & (z < n - 1))
        def _():
            self.total([self.chunk(z), below, above], out)

    def drain(self):
        z = self.at.z

        @pl.loop(0, self.at.count)
        def _(c):
            @pl.when(c != z)
            def _():
                self.move(self.chunk(c), c, 0, 0).wait_send()


class Spread:
    def __init__(self, at, which, whole, ups, downs, lines, sides, sidesr):
        self.at, self.which, self.whole = at, which, whole
        self.ups, self.downs, self.lines, self.sides, self.sidesr = ups, downs, lines, sides, sidesr

    def move(self, layer, step):
        ref = self.whole.at[layer, self.at.x]
        sends = self.ups if step > 0 else self.downs
        return remote(ref, ref, sends, self.lines, (self.which, layer), z=self.at.z + step)

    def side(self, layer, part):
        ref = self.whole.at[layer, part]
        return remote(ref, ref, self.sides, self.sidesr, (self.which, layer), x=self.at.ox)

    def first(self):
        at = self.at

        @pl.when(at.z < at.count - 1)
        def _():
            self.move(at.z, 1).start()

        @pl.when(at.z > 0)
        def _():
            self.move(at.z, -1).start()

        self.side(at.z, at.x).start()

    def hop(self, distance, step):
        at = self.at
        layer = at.z - step * distance

        @pl.when((layer >= 0) & (layer < at.count))
        def _():
            self.move(layer, step).wait_recv()

            @pl.when((at.z + step >= 0) & (at.z + step < at.count))
            def _():
                self.move(layer, step).start()

            self.side(layer, at.x).start()

    def end(self):
        at = self.at

        @pl.loop(0, at.count)
        def _(layer):
            self.side(layer, at.ox).wait_recv()
            self.side(layer, at.x).wait_send()

            @pl.when((layer <= at.z) & (at.z < at.count - 1))
            def _():
                self.move(layer, 1).wait_send()

            @pl.when((layer >= at.z) & (at.z > 0))
            def _():
                self.move(layer, -1).wait_send()


ORDERS = {
    (4, 0): (
        "b2", "b3", "twins", "corners", "home0", "keep", "home1", "f0", "D01", "D02", "norm",
        "own", "rows", "columns", "f1", "D11", "D12", "f2", "D21", "D22", "f3", "D31", "D32",
        "D03", "D13", "D23", "D33", "gains",
    ),
    (4, 1): (
        "home0", "end", "twins", "u02", "home1", "u03", "corners", "u12", "u13", "d03", "f0",
        "u22", "keep", "D01", "u23", "norm", "s0", "u32", "u33", "own", "rows", "columns",
        "d13", "U01", "gains", "f1", "D11", "d23", "U11", "f2", "D21", "d33", "U21", "f3",
        "D31", "D02", "U31", "D12", "D22", "D32",
    ),
    (4, 2): (
        "d02", "home1", "d03", "u03", "f0", "s0", "end", "twins", "u13", "s1", "d12", "U01",
        "d13", "u23", "corners", "f1", "d22", "u33", "d23", "keep", "f2", "d32", "U02", "d33",
        "U11", "f3", "norm", "D01", "U12", "U21", "own", "rows", "columns", "D11", "gains",
        "D21", "U31", "D31", "U22", "U32",
    ),
    (4, 3): (
        "b2", "b3", "norm", "f0", "U01", "end", "s2", "twins", "f1", "U02", "f2", "U11",
        "corners", "f3", "U21", "keep", "own", "rows", "U12", "columns", "gains", "U31", "U03",
        "U22", "U13", "U32", "U23", "U33",
    ),
}


def back_kernel(
    count,
    x_all,
    in_all,
    kv_all,
    query_in,
    attended_in,
    log_in,
    branch_in,
    mlp_in,
    og_all,
    down_all,
    up_all,
    w_query,
    w_key,
    w_value,
    w_out,
    gain1,
    gain2,
    clip_lengths,
    key_padding,
    output,
    input_grad,
    gains_out,
    mlp_grads,
    out_grads,
    query_grads,
    key_grads,
    value_grads,
    down_terms,
    up_terms,
    out_terms,
    query_terms,
    key_terms,
    value_terms,
    down_landing,
    up_landing,
    out_landing,
    query_landing,
    key_landing,
    value_landing,
    down_sums,
    up_sums,
    out_sums,
    query_sums,
    key_sums,
    value_sums,
    mine,
    grad_branch,
    grad_resid,
    share_own,
    share_landing,
    share_sums,
    start_row,
    key_place,
    partials,
    full1,
    stat_own,
    stat_in,
    part_own,
    part_x,
    part_in,
    twin,
    corner_x,
    corner_y,
    from_x,
    from_y,
    gains,
    gains_landing,
    load_sem,
    reduce_send,
    reduce_recv,
    gather_send,
    gather_recv,
    sum_send,
    sum_recv,
    home_send,
    home_recv,
    spread_up,
    spread_down,
    spread_line,
    spread_side,
    spread_side_recv,
    share_send,
    share_recv,
    gain_send,
    gain_recv,
    stat_send,
    stat_recv,
    part_send,
    part_recv,
):
    at = Place(count)
    z, x, y, c = at.z, at.x, at.y, at.c
    group, features = mlp_in.shape
    rows = group // 2
    width = output.shape[1]
    local = w_query.shape[1] // 2
    heads = local // HD
    hidden = down_all.shape[1]
    tile = min(256, group)
    tiles = group // tile
    thin = min(128, group)
    chunk = features // count
    block = min(512, features)
    blocks = features // block
    own_column = pl.ds(pl.multiple_of((2 * y + c) * width, width), width)

    def columns_of(weight):
        return weight.at[:, pl.ds(pl.multiple_of(x * local, local), local)]

    def rows_spec(size, many=None):
        return pl.BlockSpec((many or tile, size), lambda i: (i, 0))

    def column_spec(tall):
        return pl.BlockSpec((tall, block), lambda i: (0, i))

    def whole_spec(*shape):
        return pl.BlockSpec(shape, lambda i: (0,) * len(shape))

    def round_of(r, by_y=False):
        p = r % 2 if isinstance(r, int) else lax.rem(r, 2)
        third = r % 3 if isinstance(r, int) else lax.rem(r, 3)
        buffers = (twin.at[third],) + tuple(
            b.at[p] for b in (corner_x, corner_y, from_x, from_y)
        )
        return Reduce(
            at,
            partials.at[p],
            rows,
            width,
            buffers,
            reduce_send.at[r],
            reduce_recv.at[r],
            by_y,
        )

    def gather_of(array, k):
        return Gather(at, array, rows, width, gather_send, gather_recv, (k,))

    first_sum, out_sum = round_of(0, False), round_of(1, False)
    first_gather = gather_of(full1, 0)
    attn_grads = (out_grads, query_grads, key_grads, value_grads)

    def lines_at(at):
        arrays = (
            (down_terms, down_landing, down_sums),
            (up_terms, up_landing, up_sums),
            (out_terms, out_landing, out_sums),
            (query_terms, query_landing, query_sums),
            (key_terms, key_landing, key_sums),
            (value_terms, value_landing, value_sums),
        )
        return [
            LineSum(at, k, *three, sum_send, sum_recv, k > 1) for k, three in enumerate(arrays)
        ]

    def spreads_at(at):
        sems = (spread_up, spread_down, spread_line, spread_side, spread_side_recv)
        return [Spread(at, k, whole, *sems) for k, whole in enumerate(attn_grads)]

    down_line, up_line, *attn_lines = lines_at(at)
    spreads = spreads_at(at)

    def weight_terms(terms, left, right, first, many):
        size = terms.shape[1]

        def at_chunk(i):
            return lax.rem(first + i, count)

        def step(left_ref, right_ref, out_ref):
            out_ref[...] = contract(left_ref[...], right_ref[...], ((0,), (0,))).astype(BF16)

        pltpu.emit_pipeline(
            step,
            grid=(many,),
            in_specs=[
                pl.BlockSpec((group, chunk), lambda i: (0, at_chunk(i))),
                whole_spec(group, size),
            ],
            out_specs=[pl.BlockSpec((chunk, size), lambda i: (at_chunk(i), 0))],
        )(left, right, terms)

    def home(which, line):
        line.final(mine.at[which])
        half = mine.shape[1] // 2
        home_copy(which).start()

        def step(in_ref, out_ref):
            out_ref[...] = in_ref[...]

        spec = pl.BlockSpec((half, hidden), lambda i: (i, 0))
        pltpu.emit_pipeline(step, grid=(1,), in_specs=[spec], out_specs=[spec])(
            mine.at[which, pl.ds(pl.multiple_of(x * half, half), half)], mlp_grads.at[which, x]
        )

    def home_copy(which, landing_part=False):
        half = mine.shape[1] // 2
        return remote(
            mine.at[which, pl.ds(pl.multiple_of(at.ox * half, half), half)],
            mlp_grads.at[which, at.ox if landing_part else x],
            home_send,
            home_recv,
            (which,),
            x=at.ox,
        )

    def store_into(gather):
        def store(part, value):
            gather.block(x, y, c)[part, :] = value.astype(BF16)

        return store

    def feed_forward(active, grad_up, w_down, w_up):
        loads = [
            pltpu.make_async_copy(up_all, w_up, load_sem.at[0]),
            pltpu.make_async_copy(down_all, w_down, load_sem.at[1]),
        ]
        for load in loads:
            load.start()
        position = lax.broadcasted_iota(jnp.int32, (1, group), 1) + z * group
        start_row[...] = clip_start(position, clip_lengths)
        place_keys(key_place, key_padding, count, group)
        at.meet(whole_line=True)
        for load in loads:
            load.wait()

        def step(mlp_ref, og_ref, active_ref, grad_ref):
            up = jnp.dot(mlp_ref[...], w_up[...], preferred_element_type=F32)
            grad = jnp.dot(og_ref[...], w_down[...], preferred_element_type=F32)
            square = up * up
            root = 0.7978845608028654
            bend = jnp.tanh(up * (root + (root * 0.044715) * square))
            half = 0.5 * (1.0 + bend)
            slope = half + 0.5 * up * (1.0 - bend * bend) * (root + (3.0 * root * 0.044715) * square)
            active_ref[...] = (up * half).astype(BF16)
            grad_ref[...] = (grad * slope).astype(BF16)

        pltpu.emit_pipeline(
            step,
            grid=(tiles,),
            in_specs=[rows_spec(features)] * 2,
            out_specs=[rows_spec(hidden)] * 2,
        )(mlp_in, og_all, active, grad_up)
        first = pick(z == 0, count - 1, 0)
        weight_terms(down_terms, og_all, active, first, 1)
        down_line.hop(1)
        weight_terms(up_terms, mlp_in, grad_up, first, 1)
        up_line.hop(1)

        def back_through(target, source, weight):
            @pl.loop(0, tiles)
            def _(i):
                part = pl.ds(pl.multiple_of(i * tile, tile), tile)
                target[part, :] = contract(source[part, :], weight[...], ((1,), (1,))).astype(BF16)

        back_through(partials.at[0], grad_up, w_up)
        first_sum.start()
        weight_terms(down_terms, og_all, active, first + 1, count - 1)
        first_sum.twins()
        weight_terms(up_terms, mlp_in, grad_up, first + 1, count - 1)
        for h in range(2, count):
            down_line.begin(h)
            up_line.begin(h)
        first_sum.corners()
        back_through(partials.at[1], active, w_down)
        first_sum.end(store_into(first_gather))
        first_gather.start()
        down_line.hop(2)
        out_sum.start()
        first_gather.middle()
        first_gather.corner()
        out_sum.twins()
        first_gather.end()

    pl.run_scoped(
        feed_forward,
        pltpu.VMEM((group, hidden), BF16),
        pltpu.VMEM((group, hidden), BF16),
        pltpu.VMEM((features, hidden), BF16),
        pltpu.VMEM((features, hidden), BF16),
    )

    def attention(
        qkv_w, out_w, query, attended, kv, grad_att, grad_query, grad_kv, grad_kv_low, kv_weight,
        logs, log_row, delta_row, wide, resid_x, resid_branch, share, resid, normed1, inverse1,
    ):
        loads = [
            pltpu.make_async_copy(
                columns_of(w), qkv_w.at[:, pl.ds(i * local, local)], load_sem.at[i]
            )
            for i, w in enumerate((w_key, w_value, w_query))
        ]
        loads += [
            pltpu.make_async_copy(columns_of(w_out), out_w, load_sem.at[3]),
            pltpu.make_async_copy(query_in, query, load_sem.at[4]),
            pltpu.make_async_copy(attended_in, attended, load_sem.at[5]),
            pltpu.make_async_copy(log_in, logs, load_sem.at[6]),
        ]
        for load in loads:
            load.start()
        for load in loads:
            load.wait()
        gains[...] = jnp.zeros_like(gains)

        def second_back(x_ref, branch_ref, og_ref, grad_ref, low_ref, resid_ref, att_ref):
            normed, inverse = normed_rows(x_ref[...].astype(F32) + branch_ref[...].astype(F32))
            grad = grad_ref[...].astype(F32)
            scaled = grad * gain2[...]
            centre = jnp.mean(scaled, axis=1, keepdims=True)
            slope = jnp.mean(scaled * normed, axis=1, keepdims=True)
            gains[1:2, :] += jnp.sum(grad * normed, axis=0, keepdims=True)
            total = og_ref[...].astype(F32) + inverse * (scaled - centre - normed * slope)
            wide[...] = total
            low = total.astype(BF16)
            low_ref[...] = low
            resid_ref[...] = wide[:, own_column]
            att_ref[...] = jnp.dot(low, out_w[...], preferred_element_type=F32).astype(BF16)

        up_line.hop(2)
        thin_spec = rows_spec(features, thin)
        pltpu.emit_pipeline(
            second_back,
            grid=(group // thin,),
            in_specs=[thin_spec] * 4,
            out_specs=[thin_spec, rows_spec(width, thin), rows_spec(local, thin)],
        )(x_all.at[0], branch_in, og_all, full1, grad_branch, grad_resid, grad_att)
        out_sum.corners()
        weight_terms(out_terms, grad_branch, attended, 0, count)
        for h in range(heads):
            span = slice(h * HD, (h + 1) * HD)
            log_row[h] = jnp.transpose(logs[h])[:1]
            product = grad_att[:, span].astype(F32) * attended[:, span].astype(F32)
            delta_row[h] = jnp.sum(jnp.transpose(product), axis=0, keepdims=True)
        grad_query[...] = jnp.zeros_like(grad_query)
        kv_weight[...] = jnp.zeros_like(kv_weight)

        def attend_back(layer, diagonal, early):
            if early:
                pltpu.sync_copy(kv_all.at[z - layer], kv)
                grad_kv[...] = jnp.zeros_like(grad_kv)
            keys = jnp.transpose(jnp.broadcast_to(key_place[layer], (HD, group)))[:, :1]
            middle = tiles // 2

            @pl.loop(0 if early else middle, middle if early else tiles)
            def _(i):
                part = pl.ds(pl.multiple_of(i * tile, tile), tile)
                allowed = keys >= start_row[:, part]
                if diagonal:
                    query_at = lax.broadcasted_iota(jnp.int32, (group, tile), 1) + i * tile
                    key_at = lax.broadcasted_iota(jnp.int32, (group, tile), 0)
                    allowed = (allowed & (key_at <= query_at)) | (key_at == query_at)
                for h in range(heads):
                    span = slice(h * HD, (h + 1) * HD)
                    value_span = slice(local + h * HD, local + (h + 1) * HD)
                    key, value = kv[:, span], kv[:, value_span]
                    asked, grad = query[part, span], grad_att[part, span]
                    scores = contract(key, asked, ((1,), (1,))) * (HD**-0.5 * LOG2E)
                    probs = jnp.exp2(jnp.where(allowed, scores, -1e30) - log_row[h, :, part])
                    grad_probs = contract(value, grad, ((1,), (1,)))
                    grad_scores = (
                        probs * (grad_probs - delta_row[h, :, part]) * HD**-0.5
                    ).astype(BF16)
                    grad_kv[:, value_span] += jnp.dot(
                        probs.astype(BF16), grad, preferred_element_type=F32
                    )
                    grad_kv[:, span] += jnp.dot(grad_scores, asked, preferred_element_type=F32)
                    grad_query[part, span] += contract(grad_scores, key, ((0,), (0,)))

            if not early:
                grad_kv_low[...] = grad_kv[...].astype(BF16)

        def kv_terms(layer):
            def add(in_ref, grad_ref, out_ref):
                out_ref[...] += contract(in_ref[...], grad_ref[...], ((0,), (0,)))

            pltpu.emit_pipeline(
                add,
                grid=(blocks,),
                in_specs=[column_spec(group), whole_spec(group, 2 * local)],
                out_specs=[pl.BlockSpec((block, 2 * local), lambda i: (i, 0))],
            )(in_all.at[z - layer], grad_kv_low, kv_weight)

        def back_to_rows(layer, diagonal):
            target = partials.at[lax.rem(layer, 2)]

            @pl.loop(0, tiles)
            def _(i):
                part = pl.ds(pl.multiple_of(i * tile, tile), tile)
                value = contract(grad_kv_low[part, :], qkv_w[:, : 2 * local], ((1,), (1,)))
                if diagonal:
                    value = value + contract(
                        grad_query[part, :].astype(BF16), qkv_w[:, 2 * local :], ((1,), (1,))
                    )
                target[part, :] = value.astype(BF16)

        def share_copy(layer, source):
            return remote(
                source.at[layer], share_landing.at[layer], share_send, share_recv, (layer,), z=z - 1
            )

        def keep_share(layer, z):
            def store(part, value):
                share[part, :] = value

            round_of(layer + 2).end(store)

            @pl.when(layer < z)
            def _():
                resid_x[...] = share[...].astype(BF16)
                pltpu.sync_copy(resid_x, share_own.at[layer])

                @pl.when((z == count - 1) & (layer < z - 1))
                def _():
                    share_copy(layer, share_own).start()

        def share_line(layer, z):
            if layer == count - 2:

                @pl.when(z == count - 1)
                def _():
                    share_copy(layer, share_own).start()

            @pl.when((layer < z) & (z < count - 1))
            def _():
                share_copy(layer, share_own).wait_recv()
                pltpu.sync_copy(share_own.at[layer], resid_x)
                pltpu.sync_copy(share_landing.at[layer], resid_branch)
                resid_x[...] = (resid_x[...].astype(F32) + resid_branch[...].astype(F32)).astype(
                    BF16
                )
                pltpu.sync_copy(resid_x, share_sums.at[layer])
                share_copy(layer, share_sums).start()

        def finish_output():
            own = pl.ds(pl.multiple_of(x * rows, rows), rows)
            pltpu.sync_copy(x_all.at[0, own, own_column], resid_x)
            pltpu.sync_copy(branch_in.at[own, own_column], resid_branch)

            def store(part, value):
                resid = resid_x[part, :].astype(F32) + resid_branch[part, :].astype(F32)
                resid_x[part, :] = (resid + value).astype(BF16)

            out_sum.end(store)
            pltpu.sync_copy(resid_x, output)

        def hop_of(line, h, steps=(1, -1)):
            return functools.partial(line.hop, h, steps)

        events = [[] for _ in range(count)]
        for h in range(3, count):
            events[min(h - 3, count - 2)].append(hop_of(down_line, h))
            events[min(h - 2, count - 2)].append(hop_of(up_line, h))
        if count > 3:
            events[count - 2].append(functools.partial(home, 0, down_line))
        if count == 4:
            events[count - 1].append(functools.partial(home, 1, up_line))
        attn_lines[0].hop(1)

        def split_terms(in_ref, grad_ref, kv_ref, query_ref, key_ref, value_ref):
            key_ref[...] = kv_ref[:, :local].astype(BF16)
            value_ref[...] = kv_ref[:, local:].astype(BF16)
            query_ref[...] = contract(in_ref[...], grad_ref[:, :local], ((0,), (0,))).astype(BF16)

        def both(layer, act):
            @pl.when(layer < z)
            def _():
                act(layer, False)

            @pl.when(layer == z)
            def _():
                act(layer, True)

        @pl.loop(0, z + 1)
        def _(layer):
            one, two = layer >= 1, layer >= 2
            both(layer, functools.partial(attend_back, early=True))

            @pl.when(layer == 0)
            def _():
                finish_output()

            @pl.when(two)
            def _():
                keep_share(layer - 2, z)

            @pl.when(one)
            def _():
                round_of(layer + 1).twins()

            both(layer, functools.partial(attend_back, early=False))
            for k in range(count):
                if events[k]:

                    @pl.when(layer == k)
                    def _():
                        for event in events[k]:
                            event()

            kv_terms(layer)

            @pl.when(layer == z)
            def _():
                kv[:, :local] = grad_query[...].astype(BF16)
                pltpu.emit_pipeline(
                    split_terms,
                    grid=(blocks,),
                    in_specs=[
                        column_spec(group),
                        whole_spec(group, 2 * local),
                        rows_spec(2 * local, block),
                    ],
                    out_specs=[rows_spec(local, block)] * 3,
                )(in_all.at[0], kv, kv_weight, query_terms, key_terms, value_terms)
                attn_lines[1].hop(1)

            @pl.when(one)
            def _():
                round_of(layer + 1).corners()

            round_of(layer).drain()
            both(layer, back_to_rows)
            round_of(layer + 2).start()

        own_rows = pl.ds(pl.multiple_of(x * rows, rows), rows)

        def first_norm():
            def step(x_ref, normed_ref, inverse_ref):
                normed, inverse = normed_rows(x_ref[...].astype(F32))
                wide[...] = normed
                normed_ref[...] = wide[:, own_column]
                inverse_ref[...] = jnp.broadcast_to(inverse, inverse_ref.shape)

            pltpu.emit_pipeline(
                step,
                grid=(rows // thin,),
                in_specs=[rows_spec(features, thin)],
                out_specs=[rows_spec(width, thin), rows_spec(HD, thin)],
            )(x_all.at[0, own_rows], normed1, inverse1)
            pltpu.sync_copy(grad_resid.at[own_rows], resid)

        def beside(k):
            return ({"core": at.oc}, {"y": at.oy}, {"y": at.oy, "core": at.oc})[k]

        def stat_copy(k):
            return remote(stat_own, stat_in.at[k], stat_send, stat_recv, (k,), **beside(k))

        def part_copy(k):
            return remote(part_own, part_in.at[k], part_send, part_recv, (k,), **beside(k))

        def part_across():
            return remote(part_own, part_x, part_send, part_recv, (3,), x=at.ox)

        def row_stats():
            grad = share[...]
            scaled = grad * gain1[:, own_column]
            lane = lax.broadcasted_iota(jnp.int32, (rows, HD), 1)
            first = jnp.sum(scaled, axis=1, keepdims=True)
            second = jnp.sum(scaled * normed1[...], axis=1, keepdims=True)
            both_sums = jnp.where(lane == 0, first, jnp.where(lane == 1, second, 0.0))
            stat_own[...] = jnp.transpose(both_sums)[:8]
            for k in range(3):
                stat_copy(k).start()
            part_own[...] = jnp.broadcast_to(
                jnp.sum(grad * normed1[...], axis=0, keepdims=True), part_own.shape
            )
            part_across().start()

        def rows_back():
            for k in range(3):
                stat_copy(k).wait_recv()
            sums = (stat_own[...] + stat_in[0] + stat_in[1] + stat_in[2]) * (1.0 / features)
            sums = jnp.transpose(jnp.concatenate([sums] * (HD // 8), axis=0))
            centre, slope = sums[:, :1], sums[:, 1:2]
            scaled = share[...] * gain1[:, own_column]
            share[...] = resid[...] + inverse1[:, :1] * (
                scaled - centre - normed1[...] * slope
            )
            pltpu.sync_copy(share, input_grad)

        def gain_columns():
            part_across().wait_recv()
            part_across().wait_send()
            part_own[...] = part_own[...] + part_x[...]
            for k in range(3):
                part_copy(k).start()

        def gain_line():
            def column_of(yi, ci):
                return pl.ds(pl.multiple_of((2 * yi + ci) * width, width), width)

            gains[0:1, own_column] = part_own[:1]
            for k, (yi, ci) in enumerate(((y, at.oc), (at.oy, c), (at.oy, at.oc))):
                part_copy(k).wait_recv()
                gains[0:1, column_of(yi, ci)] = part_in[k, :1]
            for step in range(1, count):
                gain_copy(step).start()

        def gain_copy(step):
            to = lax.rem(z + step, count)
            return pltpu.make_async_remote_copy(
                src_ref=gains,
                dst_ref=gains_landing.at[z],
                send_sem=gain_send.at[step],
                recv_sem=gain_recv.at[z],
                device_id={"z": to},
                device_id_type=MESH,
            )

        def tail(z):
            here = at.fixed(z)
            down_here, up_here, *lines_here = lines_at(here)
            spreads_here = spreads_at(here)
            last = at.z + 2

            def end_before():
                @pl.when(z >= 1)
                def _():
                    keep_share(z - 1, z)

            def own_share():
                @pl.when(z < count - 1)
                def _():
                    share_copy(z, share_own).wait_recv()
                    pltpu.sync_copy(share_landing.at[z], resid_branch)
                    share[...] = share[...] + resid_branch[...].astype(F32)

                row_stats()

            def final(k):
                lines_here[k].final(attn_grads[k].at[z, x])
                spreads_here[k].first()

            todo = {
                "end": end_before,
                "twins": lambda: round_of(last).twins(),
                "corners": lambda: round_of(last).corners(),
                "keep": lambda: keep_share(z, z),
                "home0": lambda: pl.when(count < 4 or z < count - 2)(lambda: home(0, down_here)),
                "home1": lambda: pl.when(count != 4 or z < count - 1)(lambda: home(1, up_here)),
                "norm": first_norm,
                "own": own_share,
                "rows": rows_back,
                "columns": gain_columns,
                "gains": gain_line,
            }
            for k in range(4):
                if k > 1:
                    todo[f"b{k}"] = hop_of(lines_here[k], 1)
                for h in range(2, count):
                    todo[f"u{k}{h}"] = hop_of(lines_here[k], h, (1,))
                    todo[f"d{k}{h}"] = hop_of(lines_here[k], h, (-1,))
                todo[f"f{k}"] = functools.partial(final, k)
                for h in range(1, count):
                    todo[f"U{k}{h}"] = functools.partial(spreads_here[k].hop, h, 1)
                    todo[f"D{k}{h}"] = functools.partial(spreads_here[k].hop, h, -1)
            for layer in range(count - 1):
                todo[f"s{layer}"] = functools.partial(share_line, layer, z)
            order = ORDERS.get((count, z)) if isinstance(z, int) else None
            if order is None:
                order = ["end", "twins", "corners", "keep", "home0", "b2", "b3", "home1"]
                for k in range(4):
                    order += [f"{way}{k}{h}" for h in range(2, count) for way in "ud"] + [f"f{k}"]
                order += [f"s{layer}" for layer in range(count - 1)] + ["norm", "own", "rows"]
                order += ["columns", "gains"]
                for k in range(4):
                    order += [f"{way}{k}{h}" for h in range(1, count) for way in "UD"]
            for name in order:
                todo[name]()

        if count <= 4:
            for k in range(count):

                @pl.when(z == k)
                def _():
                    tail(k)
        else:
            tail(z)
        gains_landing[z] = gains[...]
        for step in range(1, count):
            source = lax.rem(z + step, count)
            pltpu.make_async_remote_copy(
                src_ref=gains,
                dst_ref=gains_landing.at[source],
                send_sem=gain_send.at[step],
                recv_sem=gain_recv.at[source],
                device_id={"z": source},
                device_id_type=MESH,
            ).wait_recv()
        for step in range(1, count):
            gain_copy(step).wait_send()
        for k in range(3):
            stat_copy(k).wait_send()
            part_copy(k).wait_send()
        gains[...] = jnp.sum(gains_landing[...], axis=0)
        pltpu.sync_copy(gains, gains_out)
        for spread in spreads:
            spread.end()

        @pl.loop(0, count)
        def _(layer):
            @pl.when(layer < z)
            def _():
                share_copy(layer, share_own).wait_send()

    pl.run_scoped(
        attention,
        pltpu.VMEM((features, 3 * local), BF16),
        pltpu.VMEM((features, local), BF16),
        pltpu.VMEM((group, local), BF16),
        pltpu.VMEM((group, local), BF16),
        pltpu.VMEM((group, 2 * local), BF16),
        pltpu.VMEM((group, local), BF16),
        pltpu.VMEM((group, local), F32),
        pltpu.VMEM((group, 2 * local), F32),
        pltpu.VMEM((group, 2 * local), BF16),
        pltpu.VMEM((features, 2 * local), F32),
        pltpu.VMEM((heads, group, HD), F32),
        pltpu.VMEM((heads, 1, group), F32),
        pltpu.VMEM((heads, 1, group), F32),
        pltpu.VMEM((thin, features), F32),
        pltpu.VMEM((rows, width), BF16),
        pltpu.VMEM((rows, width), BF16),
        pltpu.VMEM((rows, width), F32),
        pltpu.VMEM((rows, width), F32),
        pltpu.VMEM((rows, width), F32),
        pltpu.VMEM((rows, HD), F32),
    )
    for which in (0, 1):
        home_copy(which, True).wait_recv()
        home_copy(which).wait_send()
    for line in (down_line, up_line, *attn_lines):
        line.drain()
    round_of(z + 1).drain()
    round_of(z + 2).drain()
    first_gather.drain()


def back(count, *args):
    x_all, query, down_all = args[0], args[3], args[9]
    _, group, features = x_all.shape
    rows = group // 2
    local = query.shape[1]
    hidden = down_all.shape[1]
    width = features // 4
    chunk = features // count
    hbm, vmem, smem = (
        pl.BlockSpec(memory_space=space) for space in (pl.ANY, pltpu.VMEM, pltpu.SMEM)
    )

    def out(*shape, dtype=BF16):
        return jax.ShapeDtypeStruct(shape, dtype)

    dma = pltpu.SemaphoreType.DMA
    sizes = (hidden, hidden) + (local,) * 4
    return pl.pallas_call(
        functools.partial(back_kernel, count),
        name="back",
        out_shape=(
            out(rows, width),
            out(rows, width, dtype=F32),
            out(8, features, dtype=F32),
            out(2, 2, chunk // 2, hidden),
            *[out(count, 2, chunk, local)] * 4,
            *[out(features, size) for size in sizes],
            *[out(count + 1, chunk, size) for size in sizes],
            *[out(count, chunk, size) for size in sizes],
            out(2, chunk, hidden),
            out(group, features),
            out(group, width, dtype=F32),
            out(count, rows, width),
            out(count, rows, width),
            out(count, rows, width),
        ),
        in_specs=[hbm] * 15 + [vmem] * 2 + [smem, vmem],
        out_specs=[hbm] * 32,
        scratch_shapes=[
            pltpu.VMEM((1, group), jnp.int32),
            pltpu.VMEM((count, 1, group), jnp.int32),
            pltpu.VMEM((2, group, features), BF16),
            pltpu.VMEM((group, features), BF16),
            pltpu.VMEM((8, rows), F32),
            pltpu.VMEM((3, 8, rows), F32),
            pltpu.VMEM((8, width), F32),
            pltpu.VMEM((8, width), F32),
            pltpu.VMEM((3, 8, width), F32),
            pltpu.VMEM((3, 4, rows, width), BF16),
            pltpu.VMEM((2, rows // 2, width), BF16),
            pltpu.VMEM((2, rows // 2, width), BF16),
            pltpu.VMEM((2, rows, width), BF16),
            pltpu.VMEM((2, rows, width), BF16),
            pltpu.VMEM((8, features), F32),
            pltpu.VMEM((count, 8, features), F32),
            dma((8,)),
            dma((count + 2, 10)),
            dma((count + 2, 10)),
            dma((1, 9)),
            dma((1, 9)),
            dma((6, count)),
            dma((6, count + 1)),
            dma((2,)),
            dma((2,)),
            *[dma((4, count))] * 5,
            *[dma((count,))] * 4,
            *[dma((3,))] * 2,
            *[dma((4,))] * 2,
        ],
        compiler_params=pltpu.CompilerParams(
            collective_id=1, has_side_effects=True, vmem_limit_bytes=60 * 1024 * 1024
        ),
    )(*args)


def finish(output, input_grad, gains, mlp_grads, *attn_grads):
    count, _, chunk, local = attn_grads[0].shape
    half, hidden = mlp_grads.shape[2:]
    steps = max(1, min(2 * count, half // 16))
    part, layers = half // steps, max(count // steps, 1)
    pieces = max(steps // count, 1)
    tall = chunk // pieces
    rows, width = output.shape

    def step(output_ref, input_ref, gains_ref, mlp_ref, *refs):
        sources, targets = refs[:4], refs[4:8]
        up_ref, down_ref, output_out, input_out, gain1_out, gain2_out = refs[8:]
        output_out[...] = output_ref[...]
        input_out[...] = input_ref[...]
        gain1_out[...] = gains_ref[0:1]
        gain2_out[...] = gains_ref[1:2]
        for side in range(2):
            span = slice(side * local, (side + 1) * local)
            for source, target in zip(sources, targets):
                for i in range(layers):
                    target[i * tall : (i + 1) * tall, span] = source[i, side].astype(F32)
            span = slice(side * hidden, (side + 1) * hidden)
            down_ref[:, span] = mlp_ref[0, side].astype(F32)
            up_ref[:, span] = mlp_ref[1, side].astype(F32)

    def rows_of(tall, size):
        return pl.BlockSpec((tall, size), lambda i: (i, 0))

    def whole(*shape):
        return pl.BlockSpec(shape, lambda i: (0, 0))

    share = rows_of(rows // steps, width)
    gain = jax.ShapeDtypeStruct((1, gains.shape[1]), F32)
    return pl.pallas_call(
        step,
        name="finish",
        grid=(steps,),
        in_specs=[
            share,
            share,
            whole(*gains.shape),
            pl.BlockSpec((2, 2, part, hidden), lambda i: (0, 0, i, 0)),
            *[
                pl.BlockSpec(
                    (layers, 2, tall, local), lambda i: (i // pieces, 0, i % pieces, 0)
                )
            ]
            * 4,
        ],
        out_specs=[rows_of(layers * tall, 2 * local)] * 4
        + [rows_of(part, 2 * hidden)] * 2
        + [share, share, whole(*gain.shape), whole(*gain.shape)],
        out_shape=[jax.ShapeDtypeStruct((count * chunk, 2 * local), F32)] * 4
        + [jax.ShapeDtypeStruct((half, 2 * hidden), F32)] * 2
        + [
            jax.ShapeDtypeStruct(output.shape, output.dtype),
            jax.ShapeDtypeStruct(input_grad.shape, input_grad.dtype),
            gain,
            gain,
        ],
        compiler_params=pltpu.CompilerParams(vmem_limit_bytes=62 * 1024 * 1024),
    )(output, input_grad, gains, mlp_grads, *attn_grads)


def body(
    layer_input,
    clip_lengths,
    key_padding,
    norm1_gain,
    w_query,
    w_key,
    w_value,
    w_out,
    norm2_gain,
    w_up,
    w_down,
    out_grad,
):
    count = lax.axis_size("z")
    rows = layer_input.shape[0]
    width = w_query.shape[0]
    hidden = w_up.shape[1] // 2
    gain1, gain2 = norm1_gain[None], norm2_gain[None]
    key_padding = key_padding.reshape(count, 1, 2 * rows)
    *kept, down_full, up_full = front(
        count, layer_input, out_grad, w_query, w_key, w_value, w_out, w_up, w_down,
        gain1, gain2, clip_lengths, key_padding,
    )
    results = back(
        count, *kept, down_full.reshape(width, hidden), up_full.reshape(width, hidden),
        w_query, w_key, w_value, w_out, gain1, gain2, clip_lengths, key_padding,
    )
    grads = finish(*results[:8])
    out_grad_w, query_grad, key_grad, value_grad, up_grad, down_grad = grads[:6]
    output, input_grad, gain1_grad, gain2_grad = grads[6:]
    return (
        output,
        input_grad,
        gain1_grad[0],
        query_grad,
        key_grad,
        value_grad,
        out_grad_w,
        gain2_grad[0],
        up_grad,
        down_grad,
    )


def solution(mesh):
    seq, head = mesh.shape["seq"], mesh.shape["head"]
    fine = Mesh(mesh.devices.reshape(seq // 2, 2, head // 2, 2), ("z", "x", "y", "core"))
    seq_axes, head_axes = ("z", "x"), ("y", "core")
    both, columns = P(seq_axes, head_axes), P(None, head_axes)
    return jax.shard_map(
        body,
        mesh=fine,
        in_specs=(both, P(), P(), P(), columns, columns, columns, columns, P(), both, both, both),
        out_specs=(both, both, P(), columns, columns, columns, columns, P(), both, both),
        check_vma=False,
    )
```

```python
import copy
import functools

import jax
import jax.numpy as jnp
from jax import lax
from jax.experimental import pallas as pl
from jax.experimental.pallas import tpu as pltpu
from jax.sharding import Mesh, PartitionSpec as P

HD = 128
NORM_EPS = 1e-05
BF16 = jnp.bfloat16
F32 = jnp.float32
LAYER = ("x", "y", "core")


MESH = pl.DeviceIdType.MESH
LOG2E = 1.4426950408889634


def clip_start(position, clip_lengths):
    end, start = jnp.int32(0), jnp.zeros_like(position)
    for clip in range(clip_lengths.shape[0]):
        end = end + clip_lengths[clip]
        start = jnp.where(position >= end, end, start)
    return start


def place_keys(key_place, key_padding, count, group):
    for layer in range(count):
        position = lax.broadcasted_iota(jnp.int32, (1, group), 1) + layer * group
        key_place[layer] = jnp.where(key_padding[layer] > 0, position, -1)


def remote(src, dst, sends, recvs, slot, **device):
    return pltpu.make_async_remote_copy(
        src_ref=src,
        dst_ref=dst,
        send_sem=sends.at[slot],
        recv_sem=recvs.at[slot],
        device_id=device,
        device_id_type=MESH,
    )


def pick(which, left, right):
    if isinstance(which, bool):
        return left if which else right
    return jnp.where(which, left, right)


def contract(left, right, dims):
    return lax.dot_general(left, right, (dims, ((), ())), preferred_element_type=F32)


class Place:
    def __init__(self, count):
        self.count = count
        self.z = lax.axis_index("z")
        self.x, self.y, self.c = lax.axis_index("x"), lax.axis_index("y"), lax.axis_index("core")
        self.ox, self.oy, self.oc = 1 - self.x, 1 - self.y, 1 - self.c

    def fixed(self, z):
        other = copy.copy(self)
        other.z = z
        return other

    def meet(self, whole_line=False):
        barrier = pltpu.get_barrier_semaphore()
        for device in ({"x": self.ox}, {"y": self.oy}, {"core": self.oc}):
            pl.semaphore_signal(barrier, inc=1, device_id=device, device_id_type=MESH)
        if whole_line:
            for step in range(1, self.count):
                pl.semaphore_signal(
                    barrier,
                    inc=1,
                    device_id={"z": lax.rem(self.z + step, self.count)},
                    device_id_type=MESH,
                )
            pl.semaphore_signal(
                barrier, inc=1, device_id={"y": self.oy, "core": self.oc}, device_id_type=MESH
            )
            pl.semaphore_wait(barrier, 4 + self.count - 1)
            return
        above, below = self.z < self.count - 1, self.z > 0
        for there, step in ((above, 1), (below, -1)):

            @pl.when(there)
            def _():
                pl.semaphore_signal(
                    barrier, inc=1, device_id={"z": self.z + step}, device_id_type=MESH
                )

        pl.semaphore_wait(barrier, 3 + above.astype(jnp.int32) + below.astype(jnp.int32))


class Gather:
    def __init__(self, at, array, rows, width, sends, recvs, lead=()):
        self.at, self.array, self.sends, self.recvs, self.lead = at, array, sends, recvs, lead
        self.rows, self.width = rows, width

    def block(self, xi, yi, ci, first=0, size=None):
        size = self.rows if size is None else size
        return self.array.at[
            pl.ds(pl.multiple_of(xi * self.rows + first, size), size),
            pl.ds(pl.multiple_of((2 * yi + ci) * self.width, self.width), self.width),
        ]

    def copy(self, k, landing=False):
        at, half = self.at, self.rows // 2
        x, y, c, ox, oy, oc = at.x, at.y, at.c, at.ox, at.oy, at.oc
        place = {
            0: ((x, y, c), (ox, y, c), {"x": ox}),
            1: ((x, y, c), (x, oy, c), {"y": oy}),
            2: ((x, y, c), (x, y, oc), {"core": oc}),
            3: ((ox, y, c, 0, half), (ox, oy, c, 0, half), {"y": oy}),
            4: ((x, oy, c, half, half), (ox, oy, c, half, half), {"x": ox}),
            5: ((ox, y, c), (ox, y, oc), {"core": oc}),
            6: ((x, oy, c), (x, oy, oc), {"core": oc}),
            7: ((ox, oy, c, 0, half), (ox, oy, oc, 0, half), {"core": oc}),
            8: ((ox, oy, c, half, half), (ox, oy, oc, half, half), {"core": oc}),
        }
        source, lands, device = place[k]
        ref = self.block(*(lands if landing else source))
        return remote(ref, ref, self.sends, self.recvs, self.lead + (k,), **device)

    def start(self):
        for k in (0, 1, 2):
            self.copy(k).start()

    def middle(self):
        self.copy(0, True).wait_recv()
        self.copy(3).start()
        self.copy(5).start()
        self.copy(1, True).wait_recv()
        self.copy(4).start()
        self.copy(6).start()

    def corner(self):
        self.copy(3, True).wait_recv()
        self.copy(7).start()
        self.copy(4, True).wait_recv()
        self.copy(8).start()

    def end(self):
        for k in (2, 5, 6, 7, 8):
            self.copy(k, True).wait_recv()

    def drain(self):
        for k in range(9):
            self.copy(k).wait_send()


class Reduce:
    def __init__(self, at, array, rows, width, buffers, sends, recvs, by_y=False):
        self.at, self.array, self.sends, self.recvs = at, array, sends, recvs
        self.rows, self.width, self.by_y = rows, width, by_y
        self.twin, self.corner_x, self.corner_y, self.from_x, self.from_y = buffers

    def block(self, xi, yi, ci, first=0, size=None):
        return Gather.block(self, xi, yi, ci, first, size)

    def copy(self, k):
        at, half = self.at, self.rows // 2
        x, y, c, ox, oy, oc = at.x, at.y, at.c, at.ox, at.oy, at.oc
        low, high = pl.ds(0, half), pl.ds(half, half)
        place = {
            0: ((ox, oy, oc), self.twin.at[0], {"core": oc}),
            1: ((ox, y, oc), self.twin.at[1], {"core": oc}),
            2: ((x, oy, oc), self.twin.at[2], {"core": oc}),
            3: ((x, y, oc), self.twin.at[3], {"core": oc}),
            4: ((ox, oy, c, 0, half), self.corner_y, {"y": oy}),
            5: ((ox, oy, c, half, half), self.corner_x, {"y": oy} if self.by_y else {"x": ox}),
            6: ((ox, y, c, half, half), self.from_x.at[high], {"x": ox}),
            7: ((x, oy, c, 0, half), self.from_y.at[low], {"y": oy}),
            8: ((ox, y, c, 0, half), self.from_x.at[low], {"x": ox}),
            9: ((x, oy, c, half, half), self.from_y.at[high], {"y": oy}),
        }
        source, lands, device = place[k]
        return remote(self.block(*source), lands, self.sends, self.recvs, (k,), **device)

    def add(self, target, other):
        rows = target.shape[0]
        tile = min(rows, 128)

        @pl.loop(0, rows // tile)
        def _(i):
            part = pl.ds(pl.multiple_of(i * tile, tile), tile)
            target[part, :] = (target[part, :].astype(F32) + other[part, :].astype(F32)).astype(
                target.dtype
            )

    def start(self):
        for k in (0, 1, 2, 3):
            self.copy(k).start()

    def twins(self):
        at, half = self.at, self.rows // 2
        x, y, c, ox, oy = at.x, at.y, at.c, at.ox, at.oy
        self.copy(0).wait_recv()
        self.add(self.block(ox, oy, c), self.twin.at[0])
        self.copy(4).start()
        self.copy(5).start()
        self.copy(1).wait_recv()
        self.add(self.block(ox, y, c), self.twin.at[1])
        if not self.by_y:
            self.copy(6).start()
        self.copy(2).wait_recv()
        self.add(self.block(x, oy, c), self.twin.at[2])
        self.copy(7).start()
        if self.by_y:
            self.copy(9).start()
        self.copy(3).wait_recv()

    def corners(self):
        at, half = self.at, self.rows // 2
        self.copy(4).wait_recv()
        self.add(self.block(at.ox, at.y, at.c, 0, half), self.corner_y)
        self.copy(8).start()
        self.copy(5).wait_recv()
        if self.by_y:
            self.add(self.block(at.ox, at.y, at.c, half, half), self.corner_x)
            self.copy(6).start()
        else:
            self.add(self.block(at.x, at.oy, at.c, half, half), self.corner_x)
            self.copy(9).start()

    def end(self, store):
        for k in (6, 7, 8, 9):
            self.copy(k).wait_recv()
        own = self.block(self.at.x, self.at.y, self.at.c)
        tile = min(self.rows, 128)

        @pl.loop(0, self.rows // tile)
        def _(i):
            part = pl.ds(pl.multiple_of(i * tile, tile), tile)
            store(
                part,
                own[part, :].astype(F32)
                + self.twin[3, part, :].astype(F32)
                + self.from_x[part, :].astype(F32)
                + self.from_y[part, :].astype(F32),
            )

    def drain(self):
        for k in range(10):
            self.copy(k).wait_send()


def reduce_scratch(rows, width):
    return [
        pltpu.VMEM((4, rows, width), BF16),
        pltpu.VMEM((rows // 2, width), BF16),
        pltpu.VMEM((rows // 2, width), BF16),
        pltpu.VMEM((rows, width), BF16),
        pltpu.VMEM((rows, width), BF16),
    ]


def normed_rows(rows):
    mean = jnp.mean(rows, axis=1, keepdims=True)
    centred = rows - mean
    inverse = lax.rsqrt(jnp.mean(centred * centred, axis=1, keepdims=True) + NORM_EPS)
    return centred * inverse, inverse


class Weights:
    def __init__(self, at, which, weight, whole, sems):
        self.at, self.which, self.weight, self.whole = at, which, weight, whole
        self.local, self.xs, self.xr, self.us, self.ds, self.rs = sems
        self.half = weight.shape[1] // 2

    def columns(self, which):
        return self.weight.at[:, pl.ds(pl.multiple_of(which * self.half, self.half), self.half)]

    def own(self, stage, out):
        at = self.at
        source, target = (stage, self.whole.at[at.z, at.x]) if out else (self.columns(at.x), stage)
        return pltpu.make_async_copy(source, target, self.local.at[self.which])

    def swap(self, landing=False):
        at = self.at
        dst = self.whole.at[at.z, at.ox] if landing else self.whole.at[at.z, at.x]
        return remote(self.columns(at.ox), dst, self.xs, self.xr, (self.which,), x=at.ox)

    def move(self, layer, part, step):
        ref = self.whole.at[layer, part]
        sends = self.us if step > 0 else self.ds
        return pltpu.make_async_remote_copy(
            src_ref=ref,
            dst_ref=ref,
            send_sem=sends.at[self.which, layer, part],
            recv_sem=self.rs.at[self.which, layer, part],
            device_id={"z": self.at.z + step},
            device_id_type=MESH,
        )

    def first(self, mine, steps=(1, -1)):
        at = self.at
        part = at.x if mine else at.ox
        for step, there in ((1, at.z < at.count - 1), (-1, at.z > 0)):
            if step in steps:

                @pl.when(there)
                def _():
                    self.move(at.z, part, step).start()

    def hop(self, distance, mine):
        at = self.at
        part = at.x if mine else at.ox

        @pl.when(at.z >= distance)
        def _():
            self.move(at.z - distance, part, 1).wait_recv()

            @pl.when(at.z < at.count - 1)
            def _():
                self.move(at.z - distance, part, 1).start()

        @pl.when(at.z + distance < at.count)
        def _():
            self.move(at.z + distance, part, -1).wait_recv()

            @pl.when(at.z > 0)
            def _():
                self.move(at.z + distance, part, -1).start()

    def drain(self):
        at = self.at
        self.swap().wait_send()
        for part in (0, 1):

            @pl.loop(0, at.count)
            def _(layer):
                @pl.when((layer <= at.z) & (at.z < at.count - 1))
                def _():
                    self.move(layer, part, 1).wait_send()

                @pl.when((layer >= at.z) & (at.z > 0))
                def _():
                    self.move(layer, part, -1).wait_send()


def front_kernel(
    count,
    xs,
    og,
    w_query,
    w_key,
    w_value,
    w_out,
    w_up,
    w_down,
    gain1,
    gain2,
    clip_lengths,
    key_padding,
    x_all,
    in_all,
    kv_all,
    query_out,
    attended_out,
    log_out,
    branch_out,
    mlp_out,
    og_all,
    down_all,
    up_all,
    start_of,
    key_place,
    qkv_w,
    out_w,
    query,
    kv,
    high,
    total,
    sums,
    attended,
    partial,
    branch,
    twin,
    corner_x,
    corner_y,
    from_x,
    from_y,
    load_sem,
    gather_send,
    gather_recv,
    line_send,
    line_recv,
    w_local,
    w_xs,
    w_xr,
    w_us,
    w_ds,
    w_rs,
    reduce_send,
    reduce_recv,
):
    at = Place(count)
    z, x, y, c = at.z, at.x, at.y, at.c
    rows, width = xs.shape
    group = 2 * rows
    local = w_query.shape[1] // 2
    heads = local // HD
    features = gain1.shape[1]
    tile = 256 if group % 256 == 0 else group
    tiles = group // tile

    def columns_of(weight):
        return weight.at[:, pl.ds(pl.multiple_of(x * local, local), local)]

    loads = [
        pltpu.make_async_copy(
            columns_of(w), qkv_w.at[:, pl.ds(i * local, local)], load_sem.at[i]
        )
        for i, w in enumerate((w_key, w_value, w_query))
    ]
    loads.append(pltpu.make_async_copy(columns_of(w_out), out_w, load_sem.at[3]))

    def gather_of(d):
        return Gather(at, x_all.at[d], rows, width, gather_send, gather_recv, (d,))

    og_gather = Gather(at, og_all, rows, width, gather_send, gather_recv, (count,))
    branch_gather = Gather(at, branch, rows, width, gather_send, gather_recv, (count + 1,))

    def own_block(d):
        return gather_of(d).block(x, y, c)

    def line_copy(d):
        return remote(own_block(d), own_block(d + 1), line_send, line_recv, (d,), z=z + 1)

    weight_sems = (w_local, w_xs, w_xr, w_us, w_ds, w_rs)
    down = Weights(at, 0, w_down, down_all, weight_sems)
    up = Weights(at, 1, w_up, up_all, weight_sems)

    w_rows, hidden = w_up.shape[0], w_up.shape[1] // 2
    places = [
        partial.at[pl.ds(0, rows), pl.ds(i * width, width)] for i in range(2)
    ] + [partial.at[pl.ds(rows, w_rows), pl.ds(i * hidden, hidden)] for i in range(2)]
    into = [
        pltpu.make_async_copy(xs, places[0], load_sem.at[4]),
        down.own(places[2], False),
        up.own(places[3], False),
        pltpu.make_async_copy(og, places[1], load_sem.at[5]),
    ]
    onto = [
        pltpu.make_async_copy(places[0], own_block(0), load_sem.at[4]),
        down.own(places[2], True),
        up.own(places[3], True),
        pltpu.make_async_copy(places[1], og_gather.block(x, y, c), load_sem.at[5]),
    ]
    for copy in into + loads:
        copy.start()
    position = lax.broadcasted_iota(jnp.int32, (group, 1), 0) + z * group
    start_of[...] = clip_start(position, clip_lengths)
    place_keys(key_place, key_padding, count, group)
    for first, second in zip(into, onto):
        first.wait()
        second.start()
    at.meet()
    onto[0].wait()

    @pl.when(z < count - 1)
    def _():
        line_copy(0).start()

    gather_of(0).start()
    onto[1].wait()
    down.first(True)
    onto[2].wait()
    up.first(True, (-1,))
    onto[3].wait()
    gather_of(0).middle()
    for load in loads:
        load.wait()

    def project(d, with_query):
        size = qkv_w.shape[1] if with_query else 2 * local

        def step(x_ref, in_ref, kv_ref, *maybe_query):
            normed, _ = normed_rows(x_ref[...].astype(F32))
            rounded = (normed * gain1[...]).astype(BF16)
            in_ref[...] = rounded
            product = jnp.dot(rounded, qkv_w[:, :size], preferred_element_type=F32)
            kv_ref[...] = product[:, : 2 * local].astype(BF16)
            if with_query:
                maybe_query[0][...] = product[:, 2 * local :].astype(BF16)

        def rows_of(size):
            return pl.BlockSpec((tile, size), lambda i: (i, 0))

        outs = [rows_of(features), rows_of(2 * local)] + ([rows_of(local)] if with_query else [])
        refs = [in_all.at[d], kv_all.at[d]] + ([query_out] if with_query else [])
        pltpu.emit_pipeline(step, grid=(tiles,), in_specs=[rows_of(features)], out_specs=outs)(
            x_all.at[d], *refs
        )

    def attend(d, diagonal):
        keys = key_place[z - d]

        @pl.loop(0, tiles)
        def _(i):
            part = pl.ds(pl.multiple_of(i * tile, tile), tile)
            allowed = keys >= start_of[part, :]
            if diagonal:
                query_at = lax.broadcasted_iota(jnp.int32, (tile, group), 0) + i * tile
                key_at = lax.broadcasted_iota(jnp.int32, (tile, group), 1)
                allowed = (allowed & (key_at <= query_at)) | (key_at == query_at)
            for h in range(heads):
                span = slice(h * HD, (h + 1) * HD)
                scores = contract(query[part, span], kv[:, span], ((1,), (1,)))
                scores = jnp.where(allowed, scores * (HD**-0.5 * LOG2E), -1e30)
                top = jnp.max(scores, axis=1, keepdims=True)
                if not diagonal:
                    old = high[h, part, :1]
                    top = jnp.maximum(old, top)
                    fade = jnp.exp2(old - top)
                weights = jnp.exp2(scores - top)
                mass = jnp.sum(weights, axis=1, keepdims=True)
                value = jnp.dot(
                    weights.astype(BF16),
                    kv[:, local + h * HD : local + (h + 1) * HD],
                    preferred_element_type=F32,
                )
                if not diagonal:
                    mass = mass + total[h, part, :1] * fade
                    value = value + sums[part, span] * fade
                high[h, part, :] = jnp.broadcast_to(top, (tile, HD))
                total[h, part, :] = jnp.broadcast_to(mass, (tile, HD))
                sums[part, span] = value

    def fetch(d, diagonal):
        pltpu.sync_copy(kv_all.at[d], kv)
        if diagonal:
            pltpu.sync_copy(query_out, query)

    def bring(d):
        @pl.when(z >= d)
        def _():
            remote(own_block(d - 1), own_block(d), line_send, line_recv, (d - 1,), z=z).wait_recv()

            @pl.when((d < count - 1) & (z < count - 1))
            def _():
                line_copy(d).start()

            gather_of(d).start()

    def within(d, *names):
        @pl.when(z >= d)
        def _():
            for name in names:
                getattr(gather_of(d), name)()

    def other_rows(weight):
        weight.swap(True).wait_recv()
        weight.first(False)

    def hop_of(weight, distance, mine):
        return functools.partial(weight.hop, distance, mine)

    events = [
        hop_of(down, 1, True),
        hop_of(up, 1, True),
        functools.partial(other_rows, down),
        hop_of(down, 1, False),
        functools.partial(other_rows, up),
        hop_of(up, 1, False),
    ]
    for distance in range(2, count):
        for mine in (True, False):
            events += [hop_of(down, distance, mine), hop_of(up, distance, mine)]

    def advance(many=1):
        for _ in range(min(many, len(events))):
            events.pop(0)()

    bring(1)
    up.first(True, (1,))
    gather_of(0).corner()
    gather_of(0).end()
    project(0, True)
    within(1, "middle")
    down.swap().start()
    fetch(0, True)
    attend(0, True)

    @pl.loop(2, count)
    def _(d):
        bring(d)

        for k in (2, 3):

            @pl.when(d == k)
            def _():
                events[2 * k - 4]()

        within(d - 1, "corner", "end")

        @pl.when(z >= d - 1)
        def _():
            project(d - 1, False)

        within(d, "middle")

        for k in (2, 3):

            @pl.when(d == k)
            def _():
                if k == 2:
                    up.swap().start()
                events[2 * k - 3]()

        @pl.when(z >= d - 1)
        def _():
            fetch(d - 1, False)
            attend(d - 1, False)

    if count < 3:
        up.swap().start()
    del events[: 2 * min(count - 2, 2)]
    advance()
    og_gather.start()
    within(count - 1, "corner", "end")

    @pl.when(z >= count - 1)
    def _():
        project(count - 1, False)

    advance()
    og_gather.middle()

    @pl.when(z >= count - 1)
    def _():
        fetch(count - 1, False)
        attend(count - 1, False)

    advance(2)
    og_gather.corner()

    @pl.loop(0, tiles)
    def _(i):
        part = pl.ds(pl.multiple_of(i * tile, tile), tile)
        for h in range(heads):
            span = slice(h * HD, (h + 1) * HD)
            mass = total[h, part, :]
            attended[part, span] = (sums[part, span] / mass).astype(BF16)
            high[h, part, :] = high[h, part, :] + jnp.log2(mass)
        partial[part, :] = contract(attended[part, :], out_w[...], ((1,), (1,))).astype(BF16)

    outs = [
        pltpu.make_async_copy(attended, attended_out, load_sem.at[6]),
        pltpu.make_async_copy(high, log_out, load_sem.at[7]),
    ]
    for out in outs:
        out.start()
    reduce = Reduce(
        at, partial, rows, width, (twin, corner_x, corner_y, from_x, from_y), reduce_send, reduce_recv
    )
    reduce.start()
    og_gather.end()
    reduce.twins()
    advance()
    reduce.corners()
    advance()
    own_branch = branch_gather.block(x, y, c)

    def store(part, value):
        own_branch[part, :] = value.astype(BF16)

    reduce.end(store)
    branch_gather.start()
    advance()
    branch_gather.middle()
    advance()
    branch_gather.corner()
    branch_gather.end()
    pltpu.sync_copy(branch, branch_out)

    def second_norm(x_ref, branch_ref, mlp_ref):
        normed, _ = normed_rows(x_ref[...].astype(F32) + branch_ref[...].astype(F32))
        mlp_ref[...] = (normed * gain2[...]).astype(BF16)

    spec = pl.BlockSpec((tile, features), lambda i: (i, 0))
    pltpu.emit_pipeline(second_norm, grid=(tiles,), in_specs=[spec, spec], out_specs=[spec])(
        x_all.at[0], branch_out, mlp_out
    )
    advance(len(events))

    for out in outs:
        out.wait()
    down.drain()
    up.drain()
    reduce.drain()
    branch_gather.drain()
    og_gather.drain()

    @pl.loop(0, count)
    def _(d):
        within(d, "drain")

        @pl.when((z >= d) & (d < count - 1) & (z < count - 1))
        def _():
            line_copy(d).wait_send()


def front(count, xs, og, *args):
    w_query, w_up, gain1 = args[0], args[4], args[6]
    rows, width = xs.shape
    group, features = 2 * rows, gain1.shape[1]
    local = w_query.shape[1] // 2
    heads = local // HD
    hidden = w_up.shape[1] // 2
    w_rows = w_up.shape[0]
    hbm, vmem, smem = (
        pl.BlockSpec(memory_space=space) for space in (pl.ANY, pltpu.VMEM, pltpu.SMEM)
    )

    def out(*shape, dtype=BF16):
        return jax.ShapeDtypeStruct(shape, dtype)

    dma = pltpu.SemaphoreType.DMA
    return pl.pallas_call(
        functools.partial(front_kernel, count),
        name="front",
        out_shape=(
            out(count, group, features),
            out(count, group, features),
            out(count, group, 2 * local),
            out(group, local),
            out(group, local),
            out(heads, group, HD, dtype=F32),
            out(group, features),
            out(group, features),
            out(group, features),
            out(count, 2, w_rows, hidden),
            out(count, 2, w_rows, hidden),
        ),
        in_specs=[hbm] * 8 + [vmem] * 2 + [smem, vmem],
        out_specs=[hbm] * 11,
        scratch_shapes=[
            pltpu.VMEM((group, 1), jnp.int32),
            pltpu.VMEM((count, 1, group), jnp.int32),
            pltpu.VMEM((features, 3 * local), BF16),
            pltpu.VMEM((features, local), BF16),
            pltpu.VMEM((group, local), BF16),
            pltpu.VMEM((group, 2 * local), BF16),
            pltpu.VMEM((heads, group, HD), F32),
            pltpu.VMEM((heads, group, HD), F32),
            pltpu.VMEM((group, local), F32),
            pltpu.VMEM((group, local), BF16),
            pltpu.VMEM((group, features), BF16),
            pltpu.VMEM((group, features), BF16),
            *reduce_scratch(rows, width),
            dma((8,)),
            dma((count + 2, 9)),
            dma((count + 2, 9)),
            dma((count,)),
            dma((count,)),
            dma((2,)),
            dma((2,)),
            dma((2,)),
            dma((2, count, 2)),
            dma((2, count, 2)),
            dma((2, count, 2)),
            dma((10,)),
            dma((10,)),
        ],
        compiler_params=pltpu.CompilerParams(
            collective_id=0, has_side_effects=True, vmem_limit_bytes=56 * 1024 * 1024
        ),
    )(xs, og, *args)


class LineSum:
    def __init__(self, at, which, terms, landing, sums, sends, recvs, eager=False):
        self.at, self.which, self.eager = at, which, eager
        self.terms, self.landing, self.sums = terms, landing, sums
        self.sends, self.recvs = sends, recvs
        self.rows = sums.shape[1]

    def chunk(self, c):
        return self.terms.at[pl.ds(pl.multiple_of(c * self.rows, self.rows), self.rows)]

    def move(self, source, c, slot, step):
        return pltpu.make_async_remote_copy(
            src_ref=source,
            dst_ref=self.landing.at[slot],
            send_sem=self.sends.at[self.which, c],
            recv_sem=self.recvs.at[self.which, slot],
            device_id={"z": self.at.z + step},
            device_id_type=MESH,
        )

    def landed(self, slot):
        self.move(self.landing.at[slot], 0, slot, 0).wait_recv()

    def total(self, refs, out):
        tile = min(256, self.rows)

        def step(*tiles):
            value = tiles[0][...].astype(F32)
            for other in tiles[1:-1]:
                value = value + other[...].astype(F32)
            tiles[-1][...] = value.astype(BF16)

        spec = pl.BlockSpec((tile, self.sums.shape[2]), lambda i: (i, 0))
        pltpu.emit_pipeline(
            step, grid=(self.rows // tile,), in_specs=[spec] * len(refs), out_specs=[spec]
        )(*refs, out)

    def begin(self, h):
        n, z = self.at.count, self.at.z
        for step, end, c, slot in ((1, 0, n - h, n - h), (-1, n - 1, h - 1, None)):
            if slot is None:
                slot = n if c == n - 2 else c

            @pl.when(z == end)
            def _():
                self.move(self.chunk(c), c, slot, step).start()

    def hop(self, h, steps=(1, -1)):
        at, n, z = self.at, self.at.count, self.at.z
        if h == 1:
            for each in range(1, n if self.eager else 2):
                self.begin(each)
        for step, c, there in (
            (1, n - h + z, (z <= h - 1) & (z < n - 1) & (z > 0)),
            (-1, z - n + h, (z >= n - h) & (z > 0) & (z < n - 1)),
        ):
            if step not in steps:
                continue
            slot = c if step > 0 else pick(c == z - 1, n, c)

            @pl.when(there)
            def _():
                self.landed(c)
                self.total([self.chunk(c), self.landing.at[c]], self.sums.at[c])
                self.move(self.sums.at[c], c, slot, step).start()

    def final(self, out):
        n, z = self.at.count, self.at.z
        below, above = self.landing.at[z], self.landing.at[n]

        @pl.when(z > 0)
        def _():
            self.landed(z)

        @pl.when(z < n - 1)
        def _():
            self.landed(n)

        @pl.when(z == 0)
        def _():
            self.total([self.chunk(z), above], out)

        @pl.when(z == n - 1)
        def _():
            self.total([self.chunk(z), below], out)

        @pl.when((z > 0) & (z < n - 1))
        def _():
            self.total([self.chunk(z), below, above], out)

    def drain(self):
        z = self.at.z

        @pl.loop(0, self.at.count)
        def _(c):
            @pl.when(c != z)
            def _():
                self.move(self.chunk(c), c, 0, 0).wait_send()


class Spread:
    def __init__(self, at, which, whole, ups, downs, lines, sides, sidesr):
        self.at, self.which, self.whole = at, which, whole
        self.ups, self.downs, self.lines, self.sides, self.sidesr = ups, downs, lines, sides, sidesr

    def move(self, layer, step):
        ref = self.whole.at[layer, self.at.x]
        sends = self.ups if step > 0 else self.downs
        return remote(ref, ref, sends, self.lines, (self.which, layer), z=self.at.z + step)

    def side(self, layer, part):
        ref = self.whole.at[layer, part]
        return remote(ref, ref, self.sides, self.sidesr, (self.which, layer), x=self.at.ox)

    def first(self):
        at = self.at

        @pl.when(at.z < at.count - 1)
        def _():
            self.move(at.z, 1).start()

        @pl.when(at.z > 0)
        def _():
            self.move(at.z, -1).start()

        self.side(at.z, at.x).start()

    def hop(self, distance, step):
        at = self.at
        layer = at.z - step * distance

        @pl.when((layer >= 0) & (layer < at.count))
        def _():
            self.move(layer, step).wait_recv()

            @pl.when((at.z + step >= 0) & (at.z + step < at.count))
            def _():
                self.move(layer, step).start()

            self.side(layer, at.x).start()

    def end(self):
        at = self.at

        @pl.loop(0, at.count)
        def _(layer):
            self.side(layer, at.ox).wait_recv()
            self.side(layer, at.x).wait_send()

            @pl.when((layer <= at.z) & (at.z < at.count - 1))
            def _():
                self.move(layer, 1).wait_send()

            @pl.when((layer >= at.z) & (at.z > 0))
            def _():
                self.move(layer, -1).wait_send()


ORDERS = {
    (4, 0): (
        "b2", "b3", "twins", "corners", "home0", "keep", "home1", "f0", "D01", "D02", "norm",
        "own", "rows", "columns", "f1", "D11", "D12", "f2", "D21", "D22", "f3", "D31", "D32",
        "D03", "D13", "D23", "D33", "gains",
    ),
    (4, 1): (
        "home0", "end", "twins", "u02", "home1", "u03", "corners", "u12", "u13", "d03", "f0",
        "u22", "keep", "D01", "u23", "norm", "s0", "u32", "u33", "own", "rows", "columns",
        "d13", "U01", "gains", "f1", "D11", "d23", "U11", "f2", "D21", "d33", "U21", "f3",
        "D31", "D02", "U31", "D12", "D22", "D32",
    ),
    (4, 2): (
        "d02", "home1", "d03", "u03", "f0", "s0", "end", "twins", "u13", "s1", "d12", "U01",
        "d13", "u23", "corners", "f1", "d22", "u33", "d23", "keep", "f2", "d32", "U02", "d33",
        "U11", "f3", "norm", "D01", "U12", "U21", "own", "rows", "columns", "D11", "gains",
        "D21", "U31", "D31", "U22", "U32",
    ),
    (4, 3): (
        "b2", "b3", "norm", "f0", "U01", "end", "s2", "twins", "f1", "U02", "f2", "U11",
        "corners", "f3", "U21", "keep", "own", "rows", "U12", "columns", "gains", "U31", "U03",
        "U22", "U13", "U32", "U23", "U33",
    ),
}


def back_kernel(
    count,
    x_all,
    in_all,
    kv_all,
    query_in,
    attended_in,
    log_in,
    branch_in,
    mlp_in,
    og_all,
    down_all,
    up_all,
    w_query,
    w_key,
    w_value,
    w_out,
    gain1,
    gain2,
    clip_lengths,
    key_padding,
    output,
    input_grad,
    gains_out,
    mlp_grads,
    out_grads,
    query_grads,
    key_grads,
    value_grads,
    down_terms,
    up_terms,
    out_terms,
    query_terms,
    key_terms,
    value_terms,
    down_landing,
    up_landing,
    out_landing,
    query_landing,
    key_landing,
    value_landing,
    down_sums,
    up_sums,
    out_sums,
    query_sums,
    key_sums,
    value_sums,
    mine,
    grad_branch,
    grad_resid,
    share_own,
    share_landing,
    share_sums,
    start_row,
    key_place,
    partials,
    full1,
    stat_own,
    stat_in,
    part_own,
    part_x,
    part_in,
    twin,
    corner_x,
    corner_y,
    from_x,
    from_y,
    gains,
    gains_landing,
    load_sem,
    reduce_send,
    reduce_recv,
    gather_send,
    gather_recv,
    sum_send,
    sum_recv,
    home_send,
    home_recv,
    spread_up,
    spread_down,
    spread_line,
    spread_side,
    spread_side_recv,
    share_send,
    share_recv,
    gain_send,
    gain_recv,
    stat_send,
    stat_recv,
    part_send,
    part_recv,
):
    at = Place(count)
    z, x, y, c = at.z, at.x, at.y, at.c
    group, features = mlp_in.shape
    rows = group // 2
    width = output.shape[1]
    local = w_query.shape[1] // 2
    heads = local // HD
    hidden = down_all.shape[1]
    tile = min(256, group)
    tiles = group // tile
    thin = min(128, group)
    chunk = features // count
    block = min(512, features)
    blocks = features // block
    own_column = pl.ds(pl.multiple_of((2 * y + c) * width, width), width)

    def columns_of(weight):
        return weight.at[:, pl.ds(pl.multiple_of(x * local, local), local)]

    def rows_spec(size, many=None):
        return pl.BlockSpec((many or tile, size), lambda i: (i, 0))

    def column_spec(tall):
        return pl.BlockSpec((tall, block), lambda i: (0, i))

    def whole_spec(*shape):
        return pl.BlockSpec(shape, lambda i: (0,) * len(shape))

    def round_of(r, by_y=False):
        p = r % 2 if isinstance(r, int) else lax.rem(r, 2)
        third = r % 3 if isinstance(r, int) else lax.rem(r, 3)
        buffers = (twin.at[third],) + tuple(
            b.at[p] for b in (corner_x, corner_y, from_x, from_y)
        )
        return Reduce(
            at,
            partials.at[p],
            rows,
            width,
            buffers,
            reduce_send.at[r],
            reduce_recv.at[r],
            by_y,
        )

    def gather_of(array, k):
        return Gather(at, array, rows, width, gather_send, gather_recv, (k,))

    first_sum, out_sum = round_of(0, False), round_of(1, False)
    first_gather = gather_of(full1, 0)
    attn_grads = (out_grads, query_grads, key_grads, value_grads)

    def lines_at(at):
        arrays = (
            (down_terms, down_landing, down_sums),
            (up_terms, up_landing, up_sums),
            (out_terms, out_landing, out_sums),
            (query_terms, query_landing, query_sums),
            (key_terms, key_landing, key_sums),
            (value_terms, value_landing, value_sums),
        )
        return [
            LineSum(at, k, *three, sum_send, sum_recv, k > 1) for k, three in enumerate(arrays)
        ]

    def spreads_at(at):
        sems = (spread_up, spread_down, spread_line, spread_side, spread_side_recv)
        return [Spread(at, k, whole, *sems) for k, whole in enumerate(attn_grads)]

    down_line, up_line, *attn_lines = lines_at(at)
    spreads = spreads_at(at)

    def weight_terms(terms, left, right, first, many):
        size = terms.shape[1]

        def at_chunk(i):
            return lax.rem(first + i, count)

        def step(left_ref, right_ref, out_ref):
            out_ref[...] = contract(left_ref[...], right_ref[...], ((0,), (0,))).astype(BF16)

        pltpu.emit_pipeline(
            step,
            grid=(many,),
            in_specs=[
                pl.BlockSpec((group, chunk), lambda i: (0, at_chunk(i))),
                whole_spec(group, size),
            ],
            out_specs=[pl.BlockSpec((chunk, size), lambda i: (at_chunk(i), 0))],
        )(left, right, terms)

    def home(which, line):
        line.final(mine.at[which])
        half = mine.shape[1] // 2
        home_copy(which).start()

        def step(in_ref, out_ref):
            out_ref[...] = in_ref[...]

        spec = pl.BlockSpec((half, hidden), lambda i: (i, 0))
        pltpu.emit_pipeline(step, grid=(1,), in_specs=[spec], out_specs=[spec])(
            mine.at[which, pl.ds(pl.multiple_of(x * half, half), half)], mlp_grads.at[which, x]
        )

    def home_copy(which, landing_part=False):
        half = mine.shape[1] // 2
        return remote(
            mine.at[which, pl.ds(pl.multiple_of(at.ox * half, half), half)],
            mlp_grads.at[which, at.ox if landing_part else x],
            home_send,
            home_recv,
            (which,),
            x=at.ox,
        )

    def store_into(gather):
        def store(part, value):
            gather.block(x, y, c)[part, :] = value.astype(BF16)

        return store

    def feed_forward(active, grad_up, w_down, w_up):
        loads = [
            pltpu.make_async_copy(up_all, w_up, load_sem.at[0]),
            pltpu.make_async_copy(down_all, w_down, load_sem.at[1]),
        ]
        for load in loads:
            load.start()
        position = lax.broadcasted_iota(jnp.int32, (1, group), 1) + z * group
        start_row[...] = clip_start(position, clip_lengths)
        place_keys(key_place, key_padding, count, group)
        at.meet(whole_line=True)
        for load in loads:
            load.wait()

        def step(mlp_ref, og_ref, active_ref, grad_ref):
            up = jnp.dot(mlp_ref[...], w_up[...], preferred_element_type=F32)
            grad = jnp.dot(og_ref[...], w_down[...], preferred_element_type=F32)
            square = up * up
            root = 0.7978845608028654
            bend = jnp.tanh(up * (root + (root * 0.044715) * square))
            half = 0.5 * (1.0 + bend)
            slope = half + 0.5 * up * (1.0 - bend * bend) * (root + (3.0 * root * 0.044715) * square)
            active_ref[...] = (up * half).astype(BF16)
            grad_ref[...] = (grad * slope).astype(BF16)

        pltpu.emit_pipeline(
            step,
            grid=(tiles,),
            in_specs=[rows_spec(features)] * 2,
            out_specs=[rows_spec(hidden)] * 2,
        )(mlp_in, og_all, active, grad_up)
        first = pick(z == 0, count - 1, 0)
        weight_terms(down_terms, og_all, active, first, 1)
        down_line.hop(1)
        weight_terms(up_terms, mlp_in, grad_up, first, 1)
        up_line.hop(1)

        def back_through(target, source, weight):
            @pl.loop(0, tiles)
            def _(i):
                part = pl.ds(pl.multiple_of(i * tile, tile), tile)
                target[part, :] = contract(source[part, :], weight[...], ((1,), (1,))).astype(BF16)

        back_through(partials.at[0], grad_up, w_up)
        first_sum.start()
        weight_terms(down_terms, og_all, active, first + 1, count - 1)
        first_sum.twins()
        weight_terms(up_terms, mlp_in, grad_up, first + 1, count - 1)
        for h in range(2, count):
            down_line.begin(h)
            up_line.begin(h)
        first_sum.corners()
        back_through(partials.at[1], active, w_down)
        first_sum.end(store_into(first_gather))
        first_gather.start()
        down_line.hop(2)
        out_sum.start()
        first_gather.middle()
        first_gather.corner()
        out_sum.twins()
        first_gather.end()

    pl.run_scoped(
        feed_forward,
        pltpu.VMEM((group, hidden), BF16),
        pltpu.VMEM((group, hidden), BF16),
        pltpu.VMEM((features, hidden), BF16),
        pltpu.VMEM((features, hidden), BF16),
    )

    def attention(
        qkv_w, out_w, query, attended, kv, grad_att, grad_query, grad_kv, grad_kv_low, kv_weight,
        logs, log_row, delta_row, wide, resid_x, resid_branch, share, resid, normed1, inverse1,
    ):
        loads = [
            pltpu.make_async_copy(
                columns_of(w), qkv_w.at[:, pl.ds(i * local, local)], load_sem.at[i]
            )
            for i, w in enumerate((w_key, w_value, w_query))
        ]
        loads += [
            pltpu.make_async_copy(columns_of(w_out), out_w, load_sem.at[3]),
            pltpu.make_async_copy(query_in, query, load_sem.at[4]),
            pltpu.make_async_copy(attended_in, attended, load_sem.at[5]),
            pltpu.make_async_copy(log_in, logs, load_sem.at[6]),
        ]
        for load in loads:
            load.start()
        for load in loads:
            load.wait()
        gains[...] = jnp.zeros_like(gains)

        def second_back(x_ref, branch_ref, og_ref, grad_ref, low_ref, resid_ref, att_ref):
            normed, inverse = normed_rows(x_ref[...].astype(F32) + branch_ref[...].astype(F32))
            grad = grad_ref[...].astype(F32)
            scaled = grad * gain2[...]
            centre = jnp.mean(scaled, axis=1, keepdims=True)
            slope = jnp.mean(scaled * normed, axis=1, keepdims=True)
            gains[1:2, :] += jnp.sum(grad * normed, axis=0, keepdims=True)
            total = og_ref[...].astype(F32) + inverse * (scaled - centre - normed * slope)
            wide[...] = total
            low = total.astype(BF16)
            low_ref[...] = low
            resid_ref[...] = wide[:, own_column]
            att_ref[...] = jnp.dot(low, out_w[...], preferred_element_type=F32).astype(BF16)

        up_line.hop(2)
        thin_spec = rows_spec(features, thin)
        pltpu.emit_pipeline(
            second_back,
            grid=(group // thin,),
            in_specs=[thin_spec] * 4,
            out_specs=[thin_spec, rows_spec(width, thin), rows_spec(local, thin)],
        )(x_all.at[0], branch_in, og_all, full1, grad_branch, grad_resid, grad_att)
        out_sum.corners()
        weight_terms(out_terms, grad_branch, attended, 0, count)
        for h in range(heads):
            span = slice(h * HD, (h + 1) * HD)
            log_row[h] = jnp.transpose(logs[h])[:1]
            product = grad_att[:, span].astype(F32) * attended[:, span].astype(F32)
            delta_row[h] = jnp.sum(jnp.transpose(product), axis=0, keepdims=True)
        grad_query[...] = jnp.zeros_like(grad_query)
        kv_weight[...] = jnp.zeros_like(kv_weight)

        def attend_back(layer, diagonal, early):
            if early:
                pltpu.sync_copy(kv_all.at[z - layer], kv)
                grad_kv[...] = jnp.zeros_like(grad_kv)
            keys = jnp.transpose(jnp.broadcast_to(key_place[layer], (HD, group)))[:, :1]
            middle = tiles // 2

            @pl.loop(0 if early else middle, middle if early else tiles)
            def _(i):
                part = pl.ds(pl.multiple_of(i * tile, tile), tile)
                allowed = keys >= start_row[:, part]
                if diagonal:
                    query_at = lax.broadcasted_iota(jnp.int32, (group, tile), 1) + i * tile
                    key_at = lax.broadcasted_iota(jnp.int32, (group, tile), 0)
                    allowed = (allowed & (key_at <= query_at)) | (key_at == query_at)
                for h in range(heads):
                    span = slice(h * HD, (h + 1) * HD)
                    value_span = slice(local + h * HD, local + (h + 1) * HD)
                    key, value = kv[:, span], kv[:, value_span]
                    asked, grad = query[part, span], grad_att[part, span]
                    scores = contract(key, asked, ((1,), (1,))) * (HD**-0.5 * LOG2E)
                    probs = jnp.exp2(jnp.where(allowed, scores, -1e30) - log_row[h, :, part])
                    grad_probs = contract(value, grad, ((1,), (1,)))
                    grad_scores = (
                        probs * (grad_probs - delta_row[h, :, part]) * HD**-0.5
                    ).astype(BF16)
                    grad_kv[:, value_span] += jnp.dot(
                        probs.astype(BF16), grad, preferred_element_type=F32
                    )
                    grad_kv[:, span] += jnp.dot(grad_scores, asked, preferred_element_type=F32)
                    grad_query[part, span] += contract(grad_scores, key, ((0,), (0,)))

            if not early:
                grad_kv_low[...] = grad_kv[...].astype(BF16)

        def kv_terms(layer):
            def add(in_ref, grad_ref, out_ref):
                out_ref[...] += contract(in_ref[...], grad_ref[...], ((0,), (0,)))

            pltpu.emit_pipeline(
                add,
                grid=(blocks,),
                in_specs=[column_spec(group), whole_spec(group, 2 * local)],
                out_specs=[pl.BlockSpec((block, 2 * local), lambda i: (i, 0))],
            )(in_all.at[z - layer], grad_kv_low, kv_weight)

        def back_to_rows(layer, diagonal):
            target = partials.at[lax.rem(layer, 2)]

            @pl.loop(0, tiles)
            def _(i):
                part = pl.ds(pl.multiple_of(i * tile, tile), tile)
                value = contract(grad_kv_low[part, :], qkv_w[:, : 2 * local], ((1,), (1,)))
                if diagonal:
                    value = value + contract(
                        grad_query[part, :].astype(BF16), qkv_w[:, 2 * local :], ((1,), (1,))
                    )
                target[part, :] = value.astype(BF16)

        def share_copy(layer, source):
            return remote(
                source.at[layer], share_landing.at[layer], share_send, share_recv, (layer,), z=z - 1
            )

        def keep_share(layer, z):
            def store(part, value):
                share[part, :] = value

            round_of(layer + 2).end(store)

            @pl.when(layer < z)
            def _():
                resid_x[...] = share[...].astype(BF16)
                pltpu.sync_copy(resid_x, share_own.at[layer])

                @pl.when((z == count - 1) & (layer < z - 1))
                def _():
                    share_copy(layer, share_own).start()

        def share_line(layer, z):
            if layer == count - 2:

                @pl.when(z == count - 1)
                def _():
                    share_copy(layer, share_own).start()

            @pl.when((layer < z) & (z < count - 1))
            def _():
                share_copy(layer, share_own).wait_recv()
                pltpu.sync_copy(share_own.at[layer], resid_x)
                pltpu.sync_copy(share_landing.at[layer], resid_branch)
                resid_x[...] = (resid_x[...].astype(F32) + resid_branch[...].astype(F32)).astype(
                    BF16
                )
                pltpu.sync_copy(resid_x, share_sums.at[layer])
                share_copy(layer, share_sums).start()

        def finish_output():
            own = pl.ds(pl.multiple_of(x * rows, rows), rows)
            pltpu.sync_copy(x_all.at[0, own, own_column], resid_x)
            pltpu.sync_copy(branch_in.at[own, own_column], resid_branch)

            def store(part, value):
                resid = resid_x[part, :].astype(F32) + resid_branch[part, :].astype(F32)
                resid_x[part, :] = (resid + value).astype(BF16)

            out_sum.end(store)
            pltpu.sync_copy(resid_x, output)

        def hop_of(line, h, steps=(1, -1)):
            return functools.partial(line.hop, h, steps)

        events = [[] for _ in range(count)]
        for h in range(3, count):
            events[min(h - 3, count - 2)].append(hop_of(down_line, h))
            events[min(h - 2, count - 2)].append(hop_of(up_line, h))
        if count > 3:
            events[count - 2].append(functools.partial(home, 0, down_line))
        if count == 4:
            events[count - 1].append(functools.partial(home, 1, up_line))
        attn_lines[0].hop(1)

        def split_terms(in_ref, grad_ref, kv_ref, query_ref, key_ref, value_ref):
            key_ref[...] = kv_ref[:, :local].astype(BF16)
            value_ref[...] = kv_ref[:, local:].astype(BF16)
            query_ref[...] = contract(in_ref[...], grad_ref[:, :local], ((0,), (0,))).astype(BF16)

        def both(layer, act):
            @pl.when(layer < z)
            def _():
                act(layer, False)

            @pl.when(layer == z)
            def _():
                act(layer, True)

        @pl.loop(0, z + 1)
        def _(layer):
            one, two = layer >= 1, layer >= 2
            both(layer, functools.partial(attend_back, early=True))

            @pl.when(layer == 0)
            def _():
                finish_output()

            @pl.when(two)
            def _():
                keep_share(layer - 2, z)

            @pl.when(one)
            def _():
                round_of(layer + 1).twins()

            both(layer, functools.partial(attend_back, early=False))
            for k in range(count):
                if events[k]:

                    @pl.when(layer == k)
                    def _():
                        for event in events[k]:
                            event()

            kv_terms(layer)

            @pl.when(layer == z)
            def _():
                kv[:, :local] = grad_query[...].astype(BF16)
                pltpu.emit_pipeline(
                    split_terms,
                    grid=(blocks,),
                    in_specs=[
                        column_spec(group),
                        whole_spec(group, 2 * local),
                        rows_spec(2 * local, block),
                    ],
                    out_specs=[rows_spec(local, block)] * 3,
                )(in_all.at[0], kv, kv_weight, query_terms, key_terms, value_terms)
                attn_lines[1].hop(1)

            @pl.when(one)
            def _():
                round_of(layer + 1).corners()

            round_of(layer).drain()
            both(layer, back_to_rows)
            round_of(layer + 2).start()

        own_rows = pl.ds(pl.multiple_of(x * rows, rows), rows)

        def first_norm():
            def step(x_ref, normed_ref, inverse_ref):
                normed, inverse = normed_rows(x_ref[...].astype(F32))
                wide[...] = normed
                normed_ref[...] = wide[:, own_column]
                inverse_ref[...] = jnp.broadcast_to(inverse, inverse_ref.shape)

            pltpu.emit_pipeline(
                step,
                grid=(rows // thin,),
                in_specs=[rows_spec(features, thin)],
                out_specs=[rows_spec(width, thin), rows_spec(HD, thin)],
            )(x_all.at[0, own_rows], normed1, inverse1)
            pltpu.sync_copy(grad_resid.at[own_rows], resid)

        def beside(k):
            return ({"core": at.oc}, {"y": at.oy}, {"y": at.oy, "core": at.oc})[k]

        def stat_copy(k):
            return remote(stat_own, stat_in.at[k], stat_send, stat_recv, (k,), **beside(k))

        def part_copy(k):
            return remote(part_own, part_in.at[k], part_send, part_recv, (k,), **beside(k))

        def part_across():
            return remote(part_own, part_x, part_send, part_recv, (3,), x=at.ox)

        def row_stats():
            grad = share[...]
            scaled = grad * gain1[:, own_column]
            lane = lax.broadcasted_iota(jnp.int32, (rows, HD), 1)
            first = jnp.sum(scaled, axis=1, keepdims=True)
            second = jnp.sum(scaled * normed1[...], axis=1, keepdims=True)
            both_sums = jnp.where(lane == 0, first, jnp.where(lane == 1, second, 0.0))
            stat_own[...] = jnp.transpose(both_sums)[:8]
            for k in range(3):
                stat_copy(k).start()
            part_own[...] = jnp.broadcast_to(
                jnp.sum(grad * normed1[...], axis=0, keepdims=True), part_own.shape
            )
            part_across().start()

        def rows_back():
            for k in range(3):
                stat_copy(k).wait_recv()
            sums = (stat_own[...] + stat_in[0] + stat_in[1] + stat_in[2]) * (1.0 / features)
            sums = jnp.transpose(jnp.concatenate([sums] * (HD // 8), axis=0))
            centre, slope = sums[:, :1], sums[:, 1:2]
            scaled = share[...] * gain1[:, own_column]
            share[...] = resid[...] + inverse1[:, :1] * (
                scaled - centre - normed1[...] * slope
            )
            pltpu.sync_copy(share, input_grad)

        def gain_columns():
            part_across().wait_recv()
            part_across().wait_send()
            part_own[...] = part_own[...] + part_x[...]
            for k in range(3):
                part_copy(k).start()

        def gain_line():
            def column_of(yi, ci):
                return pl.ds(pl.multiple_of((2 * yi + ci) * width, width), width)

            gains[0:1, own_column] = part_own[:1]
            for k, (yi, ci) in enumerate(((y, at.oc), (at.oy, c), (at.oy, at.oc))):
                part_copy(k).wait_recv()
                gains[0:1, column_of(yi, ci)] = part_in[k, :1]
            for step in range(1, count):
                gain_copy(step).start()

        def gain_copy(step):
            to = lax.rem(z + step, count)
            return pltpu.make_async_remote_copy(
                src_ref=gains,
                dst_ref=gains_landing.at[z],
                send_sem=gain_send.at[step],
                recv_sem=gain_recv.at[z],
                device_id={"z": to},
                device_id_type=MESH,
            )

        def tail(z):
            here = at.fixed(z)
            down_here, up_here, *lines_here = lines_at(here)
            spreads_here = spreads_at(here)
            last = at.z + 2

            def end_before():
                @pl.when(z >= 1)
                def _():
                    keep_share(z - 1, z)

            def own_share():
                @pl.when(z < count - 1)
                def _():
                    share_copy(z, share_own).wait_recv()
                    pltpu.sync_copy(share_landing.at[z], resid_branch)
                    share[...] = share[...] + resid_branch[...].astype(F32)

                row_stats()

            def final(k):
                lines_here[k].final(attn_grads[k].at[z, x])
                spreads_here[k].first()

            todo = {
                "end": end_before,
                "twins": lambda: round_of(last).twins(),
                "corners": lambda: round_of(last).corners(),
                "keep": lambda: keep_share(z, z),
                "home0": lambda: pl.when(count < 4 or z < count - 2)(lambda: home(0, down_here)),
                "home1": lambda: pl.when(count != 4 or z < count - 1)(lambda: home(1, up_here)),
                "norm": first_norm,
                "own": own_share,
                "rows": rows_back,
                "columns": gain_columns,
                "gains": gain_line,
            }
            for k in range(4):
                if k > 1:
                    todo[f"b{k}"] = hop_of(lines_here[k], 1)
                for h in range(2, count):
                    todo[f"u{k}{h}"] = hop_of(lines_here[k], h, (1,))
                    todo[f"d{k}{h}"] = hop_of(lines_here[k], h, (-1,))
                todo[f"f{k}"] = functools.partial(final, k)
                for h in range(1, count):
                    todo[f"U{k}{h}"] = functools.partial(spreads_here[k].hop, h, 1)
                    todo[f"D{k}{h}"] = functools.partial(spreads_here[k].hop, h, -1)
            for layer in range(count - 1):
                todo[f"s{layer}"] = functools.partial(share_line, layer, z)
            order = ORDERS.get((count, z)) if isinstance(z, int) else None
            if order is None:
                order = ["end", "twins", "corners", "keep", "home0", "b2", "b3", "home1"]
                for k in range(4):
                    order += [f"{way}{k}{h}" for h in range(2, count) for way in "ud"] + [f"f{k}"]
                order += [f"s{layer}" for layer in range(count - 1)] + ["norm", "own", "rows"]
                order += ["columns", "gains"]
                for k in range(4):
                    order += [f"{way}{k}{h}" for h in range(1, count) for way in "UD"]
            for name in order:
                todo[name]()

        if count <= 4:
            for k in range(count):

                @pl.when(z == k)
                def _():
                    tail(k)
        else:
            tail(z)
        gains_landing[z] = gains[...]
        for step in range(1, count):
            source = lax.rem(z + step, count)
            pltpu.make_async_remote_copy(
                src_ref=gains,
                dst_ref=gains_landing.at[source],
                send_sem=gain_send.at[step],
                recv_sem=gain_recv.at[source],
                device_id={"z": source},
                device_id_type=MESH,
            ).wait_recv()
        for step in range(1, count):
            gain_copy(step).wait_send()
        for k in range(3):
            stat_copy(k).wait_send()
            part_copy(k).wait_send()
        gains[...] = jnp.sum(gains_landing[...], axis=0)
        pltpu.sync_copy(gains, gains_out)
        for spread in spreads:
            spread.end()

        @pl.loop(0, count)
        def _(layer):
            @pl.when(layer < z)
            def _():
                share_copy(layer, share_own).wait_send()

    pl.run_scoped(
        attention,
        pltpu.VMEM((features, 3 * local), BF16),
        pltpu.VMEM((features, local), BF16),
        pltpu.VMEM((group, local), BF16),
        pltpu.VMEM((group, local), BF16),
        pltpu.VMEM((group, 2 * local), BF16),
        pltpu.VMEM((group, local), BF16),
        pltpu.VMEM((group, local), F32),
        pltpu.VMEM((group, 2 * local), F32),
        pltpu.VMEM((group, 2 * local), BF16),
        pltpu.VMEM((features, 2 * local), F32),
        pltpu.VMEM((heads, group, HD), F32),
        pltpu.VMEM((heads, 1, group), F32),
        pltpu.VMEM((heads, 1, group), F32),
        pltpu.VMEM((thin, features), F32),
        pltpu.VMEM((rows, width), BF16),
        pltpu.VMEM((rows, width), BF16),
        pltpu.VMEM((rows, width), F32),
        pltpu.VMEM((rows, width), F32),
        pltpu.VMEM((rows, width), F32),
        pltpu.VMEM((rows, HD), F32),
    )
    for which in (0, 1):
        home_copy(which, True).wait_recv()
        home_copy(which).wait_send()
    for line in (down_line, up_line, *attn_lines):
        line.drain()
    round_of(z + 1).drain()
    round_of(z + 2).drain()
    first_gather.drain()


def back(count, *args):
    x_all, query, down_all = args[0], args[3], args[9]
    _, group, features = x_all.shape
    rows = group // 2
    local = query.shape[1]
    hidden = down_all.shape[1]
    width = features // 4
    chunk = features // count
    hbm, vmem, smem = (
        pl.BlockSpec(memory_space=space) for space in (pl.ANY, pltpu.VMEM, pltpu.SMEM)
    )

    def out(*shape, dtype=BF16):
        return jax.ShapeDtypeStruct(shape, dtype)

    dma = pltpu.SemaphoreType.DMA
    sizes = (hidden, hidden) + (local,) * 4
    return pl.pallas_call(
        functools.partial(back_kernel, count),
        name="back",
        out_shape=(
            out(rows, width),
            out(rows, width, dtype=F32),
            out(8, features, dtype=F32),
            out(2, 2, chunk // 2, hidden),
            *[out(count, 2, chunk, local)] * 4,
            *[out(features, size) for size in sizes],
            *[out(count + 1, chunk, size) for size in sizes],
            *[out(count, chunk, size) for size in sizes],
            out(2, chunk, hidden),
            out(group, features),
            out(group, width, dtype=F32),
            out(count, rows, width),
            out(count, rows, width),
            out(count, rows, width),
        ),
        in_specs=[hbm] * 15 + [vmem] * 2 + [smem, vmem],
        out_specs=[hbm] * 32,
        scratch_shapes=[
            pltpu.VMEM((1, group), jnp.int32),
            pltpu.VMEM((count, 1, group), jnp.int32),
            pltpu.VMEM((2, group, features), BF16),
            pltpu.VMEM((group, features), BF16),
            pltpu.VMEM((8, rows), F32),
            pltpu.VMEM((3, 8, rows), F32),
            pltpu.VMEM((8, width), F32),
            pltpu.VMEM((8, width), F32),
            pltpu.VMEM((3, 8, width), F32),
            pltpu.VMEM((3, 4, rows, width), BF16),
            pltpu.VMEM((2, rows // 2, width), BF16),
            pltpu.VMEM((2, rows // 2, width), BF16),
            pltpu.VMEM((2, rows, width), BF16),
            pltpu.VMEM((2, rows, width), BF16),
            pltpu.VMEM((8, features), F32),
            pltpu.VMEM((count, 8, features), F32),
            dma((8,)),
            dma((count + 2, 10)),
            dma((count + 2, 10)),
            dma((1, 9)),
            dma((1, 9)),
            dma((6, count)),
            dma((6, count + 1)),
            dma((2,)),
            dma((2,)),
            *[dma((4, count))] * 5,
            *[dma((count,))] * 4,
            *[dma((3,))] * 2,
            *[dma((4,))] * 2,
        ],
        compiler_params=pltpu.CompilerParams(
            collective_id=1, has_side_effects=True, vmem_limit_bytes=60 * 1024 * 1024
        ),
    )(*args)


def finish(output, input_grad, gains, mlp_grads, *attn_grads):
    count, _, chunk, local = attn_grads[0].shape
    half, hidden = mlp_grads.shape[2:]
    steps = max(1, min(count, half // 16))
    part, layers = half // steps, max(count // steps, 1)
    pieces = max(steps // count, 1)
    tall = chunk // pieces
    rows, width = output.shape

    def step(output_ref, input_ref, gains_ref, mlp_ref, *refs):
        sources, targets = refs[:4], refs[4:8]
        up_ref, down_ref, output_out, input_out, gain1_out, gain2_out = refs[8:]
        output_out[...] = output_ref[...]
        input_out[...] = input_ref[...]
        gain1_out[...] = gains_ref[0:1]
        gain2_out[...] = gains_ref[1:2]
        for side in range(2):
            span = slice(side * local, (side + 1) * local)
            for source, target in zip(sources, targets):
                for i in range(layers):
                    target[i * tall : (i + 1) * tall, span] = source[i, side].astype(F32)
            span = slice(side * hidden, (side + 1) * hidden)
            down_ref[:, span] = mlp_ref[0, side].astype(F32)
            up_ref[:, span] = mlp_ref[1, side].astype(F32)

    def rows_of(tall, size):
        return pl.BlockSpec((tall, size), lambda i: (i, 0))

    def whole(*shape):
        return pl.BlockSpec(shape, lambda i: (0, 0))

    share = rows_of(rows // steps, width)
    gain = jax.ShapeDtypeStruct((1, gains.shape[1]), F32)
    return pl.pallas_call(
        step,
        name="finish",
        grid=(steps,),
        in_specs=[
            share,
            share,
            whole(*gains.shape),
            pl.BlockSpec((2, 2, part, hidden), lambda i: (0, 0, i, 0)),
            *[
                pl.BlockSpec(
                    (layers, 2, tall, local), lambda i: (i // pieces, 0, i % pieces, 0)
                )
            ]
            * 4,
        ],
        out_specs=[rows_of(layers * tall, 2 * local)] * 4
        + [rows_of(part, 2 * hidden)] * 2
        + [share, share, whole(*gain.shape), whole(*gain.shape)],
        out_shape=[jax.ShapeDtypeStruct((count * chunk, 2 * local), F32)] * 4
        + [jax.ShapeDtypeStruct((half, 2 * hidden), F32)] * 2
        + [
            jax.ShapeDtypeStruct(output.shape, output.dtype),
            jax.ShapeDtypeStruct(input_grad.shape, input_grad.dtype),
            gain,
            gain,
        ],
        compiler_params=pltpu.CompilerParams(vmem_limit_bytes=62 * 1024 * 1024),
    )(output, input_grad, gains, mlp_grads, *attn_grads)


def body(
    layer_input,
    clip_lengths,
    key_padding,
    norm1_gain,
    w_query,
    w_key,
    w_value,
    w_out,
    norm2_gain,
    w_up,
    w_down,
    out_grad,
):
    count = lax.axis_size("z")
    rows = layer_input.shape[0]
    width = w_query.shape[0]
    hidden = w_up.shape[1] // 2
    gain1, gain2 = norm1_gain[None], norm2_gain[None]
    key_padding = key_padding.reshape(count, 1, 2 * rows)
    *kept, down_full, up_full = front(
        count, layer_input, out_grad, w_query, w_key, w_value, w_out, w_up, w_down,
        gain1, gain2, clip_lengths, key_padding,
    )
    results = back(
        count, *kept, down_full.reshape(width, hidden), up_full.reshape(width, hidden),
        w_query, w_key, w_value, w_out, gain1, gain2, clip_lengths, key_padding,
    )
    grads = finish(*results[:8])
    out_grad_w, query_grad, key_grad, value_grad, up_grad, down_grad = grads[:6]
    output, input_grad, gain1_grad, gain2_grad = grads[6:]
    return (
        output,
        input_grad,
        gain1_grad[0],
        query_grad,
        key_grad,
        value_grad,
        out_grad_w,
        gain2_grad[0],
        up_grad,
        down_grad,
    )


def solution(mesh):
    seq, head = mesh.shape["seq"], mesh.shape["head"]
    fine = Mesh(mesh.devices.reshape(seq // 2, 2, head // 2, 2), ("z", "x", "y", "core"))
    seq_axes, head_axes = ("z", "x"), ("y", "core")
    both, columns = P(seq_axes, head_axes), P(None, head_axes)
    return jax.shard_map(
        body,
        mesh=fine,
        in_specs=(both, P(), P(), P(), columns, columns, columns, columns, P(), both, both, both),
        out_specs=(both, both, P(), columns, columns, columns, columns, P(), both, both),
        check_vma=False,
    )
```
